256 devices in a mesh: grp: 8 (over y, core), dev: 32 (over x, z).
Axes of the slice: x: 4, y: 4, z: 8, core: 2. Of those that a mesh axis runs over, the one named last changes fastest.
Arguments:
- old_fine: float32 [2048, 9, 128, 128], P('dev', None, 'grp'), may hold values from -6 to 6
- old_ids: int32 [8, 2048], P('grp', 'dev'), may hold values from -1 to 2047, as said below
- old_coarse: float32 [1024, 9, 64, 64], P('dev', None, 'grp'), may hold values from -6 to 6
- coarse_ids: int32 [8, 1024], P('grp', 'dev'), may hold values from 0 to 1023, as said below
- velocity: float32 [2048, 3, 128, 128], P('dev', None, 'grp'), may hold values from -0.12 to 0.12
- diffusion: float32 [9], replicated, may hold values from 0.01 to 0.1
Outputs:
- species_out: float32 [2048, 9, 128, 128], P('dev', None, 'grp')
The draws below stay inside these ranges and needn't reach their ends.
Inputs may be any that keep to these rules, and one draw needn't show every extreme that they name: `old_ids`: row g names, for each old fine slot k of group g (on dev index k // 64), the x-plane that the slot holds, or -1 for an empty slot whose rows of old_fine are ignored. No plane is named twice; planes named nowhere are newly refined. The slots of one device hold at most 4 planes of any one new box, box e holding planes e * 64 to e * 64 + 63. `coarse_ids`: each row is a permutation. The slots of one device hold at most 2 of the coarse planes e * 32 to e * 32 + 31 of any one new box e.
All inputs are finite; a program needn't handle non-finite values.
Results may differ from the reference program's by a relative error of at most 0.000092.
Values sent between devices are 32-bit elements; how exact they have to be, the bound alone decides.
No kernel may reach another device: no remote copies, remote signals or barrier semaphores. Data moves between devices by JAX's collectives and lax.ppermute only.
A program may use at most 192 MiB of HBM per device.

```python
import math
import jax
import jax.numpy as jnp

S = 9
BX = 64
BY = 16
BZ = 128
ITERS = 2
CAP = 4
CBX = 32
CCAP = 2
NX = 2048
NY = 128
CX = 1024
CY = 64
CZ = 64
N_GRP = 8
N_DEV = 32


def regrid_map(key, block_len, capacity, with_empty):
    rows_out = []
    for group_index in range(N_GRP):
        group_key = jax.random.fold_in(key, group_index)
        key_order = jax.random.fold_in(group_key, 1)
        key_offset = jax.random.fold_in(group_key, 2)
        key_slots = jax.random.fold_in(group_key, 3)
        key_level = jax.random.fold_in(group_key, 4)
        key_rolls = jax.random.fold_in(group_key, 5)
        placing = jax.random.permutation(key_order, N_DEV)
        shuffled = jax.random.permutation(key_offset, capacity * N_DEV) // capacity
        first_value = shuffled[0]
        scores = jnp.where(shuffled == first_value, 1, 0).astype(jnp.int32)
        reorder = jnp.argsort(scores, stable=True)
        rest_values = shuffled[reorder][:block_len - capacity]
        offsets = jnp.concatenate([jnp.full((capacity,), first_value, jnp.int32), rest_values.astype(jnp.int32)])
        slot_order = jax.random.permutation(key_slots, block_len)
        boxes = jnp.arange(N_DEV, dtype=jnp.int32)[:, None]
        planes = jnp.arange(block_len, dtype=jnp.int32)[None, :]
        holder = (placing[:, None] + offsets[None, :]) % N_DEV
        positions = holder * block_len + slot_order[None, :]
        values = boxes * block_len + planes
        if with_empty:
            levels = jax.random.randint(key_level, (N_DEV,), 0, 5)
            rolls = jax.random.randint(key_rolls, (N_DEV, block_len), 0, 8)
            fresh_mask = (rolls < levels[:, None]) & jnp.logical_not((boxes == 0) & (planes < capacity))
            values = jnp.where(fresh_mask, -1, values)
        row_values = jnp.zeros((N_DEV * block_len,), jnp.int32).at[positions.reshape(-1)].set(values.reshape(-1).astype(jnp.int32))
        rows_out.append(row_values)
    return jnp.stack(rows_out, axis=0)


def draw_old_ids(key, part):
    return regrid_map(jax.random.fold_in(key, 11), BX, CAP, True)


def draw_coarse_ids(key, part):
    return regrid_map(jax.random.fold_in(key, 23), CBX, CCAP, False)


def level_of(stream_key, shape, split, smallest, high):
    loudness, own = 1.0, jax.random.fold_in(stream_key, 6)
    for axis_at, parts in split:
        heights = jnp.exp(jax.random.uniform(jax.random.fold_in(own, axis_at), (parts,), jnp.float32, smallest / len(split), high / len(split)))
        loudness = loudness * jnp.repeat(heights, shape[axis_at] // parts).reshape([-1 if axis == axis_at else 1 for axis in range(len(shape))])
    return loudness


def gaussian(own_key, dims, spread, reach, cuts=(), kind=jnp.bfloat16):
    loudness = level_of(own_key, dims, cuts, -0.22, 0.18) if cuts else 1.0
    array = jax.random.normal(own_key, dims, jnp.float32) * spread * loudness
    return jnp.minimum(jnp.maximum(array, -reach), reach).astype(kind)


def setup_inputs(seed: int = 0) -> dict:
    arg_keys = jax.random.split(jax.random.key(seed), 7)
    old_fine = gaussian(arg_keys[0], (NX, S, NY, BZ), 1.0, 6.0, ((0, 32), (2, 8)), jnp.float32)
    old_ids = draw_old_ids(jax.random.fold_in(arg_keys[6], 71), 0)
    old_coarse = gaussian(arg_keys[2], (CX, S, CY, CZ), 1.0, 6.0, ((0, 32), (2, 8)), jnp.float32)
    coarse_ids = draw_coarse_ids(jax.random.fold_in(arg_keys[6], 71), 0)
    velocity = gaussian(arg_keys[4], (NX, 3, NY, BZ), 0.045, 0.12, ((0, 32), (2, 8)), jnp.float32)
    diffusion = jnp.clip(jnp.exp(jax.random.uniform(arg_keys[5], (S,), jnp.float32, math.log(0.01), math.log(0.1))), 0.01, 0.1)
    return dict(old_fine=old_fine, old_ids=old_ids, old_coarse=old_coarse, coarse_ids=coarse_ids, velocity=velocity, diffusion=diffusion)


def refine(coarse):
    extent = coarse.shape
    ypadded = jnp.concatenate([coarse[:, :, :1], coarse, coarse[:, :, -1:]], axis=2)
    zpadded = jnp.concatenate([coarse[..., :1], coarse, coarse[..., -1:]], axis=3)
    slope_y = 0.5 * (ypadded[:, :, 2:] - ypadded[:, :, :-2])
    slope_z = 0.5 * (zpadded[..., 2:] - zpadded[..., :-2])
    row_parts = []
    for row_half in range(2):
        col_parts = [coarse + (0.5 * row_half - 0.25) * slope_y + (0.5 * col_half - 0.25) * slope_z for col_half in range(2)]
        row_parts.append(jnp.stack(col_parts, axis=-1))
    children = jnp.stack(row_parts, axis=3)
    refined = children.reshape(extent[0], extent[1], 2 * extent[2], 2 * extent[3])
    return jnp.repeat(refined, 2, axis=0)


def advance(padded, flow_field, diffusion):
    center = padded[1:-1, :, 1:-1]
    zpadded = jnp.concatenate([center[..., :1], center, center[..., -1:]], axis=3)
    minus_side = [padded[:-2, :, 1:-1], padded[1:-1, :, :-2], zpadded[..., :-2]]
    plus_side = [padded[2:, :, 1:-1], padded[1:-1, :, 2:], zpadded[..., 2:]]
    laplace = minus_side[0] + plus_side[0] + minus_side[1] + plus_side[1] + minus_side[2] + plus_side[2] - 6.0 * center
    transport = jnp.zeros_like(center)
    for direction in range(3):
        speed_part = flow_field[:, direction:direction + 1]
        transport = transport + jnp.maximum(speed_part, 0.0) * (center - minus_side[direction]) + jnp.minimum(speed_part, 0.0) * (plus_side[direction] - center)
    return center + diffusion[None, :, None, None] * laplace - transport


def reference(old_fine, old_ids, old_coarse, coarse_ids, velocity, diffusion):
    pieces = []
    half_rows = BY // 2
    for group_index in range(N_GRP):
        labels = old_ids[group_index]
        target = jnp.where(labels >= 0, labels, NX).astype(jnp.int32)
        source = jnp.full((NX,), -1, jnp.int32).at[target].set(jnp.arange(NX, dtype=jnp.int32), mode="drop")
        moved_rows = old_fine[jnp.maximum(source, 0).astype(jnp.int32), :, group_index * BY:(group_index + 1) * BY]
        coarse_source = jnp.zeros((CX,), jnp.int32).at[coarse_ids[group_index].astype(jnp.int32)].set(jnp.arange(CX, dtype=jnp.int32))
        parents = old_coarse[coarse_source, :, group_index * half_rows:(group_index + 1) * half_rows]
        interp = refine(parents)
        pieces.append(jnp.where((source < 0)[:, None, None, None], interp, moved_rows))
    species_state = jnp.concatenate(pieces, axis=2)
    for repeat in range(ITERS):
        padded = jnp.pad(species_state, ((1, 1), (0, 0), (1, 1), (0, 0)))
        species_state = advance(padded, velocity, diffusion)
    return species_state
```

```python
import functools

import jax
import jax.numpy as jnp
from jax import lax
from jax.experimental import pallas as pl
from jax.experimental.pallas import tpu as pltpu
from jax.sharding import PartitionSpec as P

ITERS = 2
FINE_CAP = 4
COARSE_CAP = 2
VMEM = pl.BlockSpec(memory_space=pltpu.VMEM)
SMEM = pl.BlockSpec(memory_space=pltpu.SMEM)
PARAMS = pltpu.CompilerParams(vmem_limit_bytes=56 * 1024 * 1024)


def ranks(boxes):
    count = boxes.shape[-1]
    earlier = jnp.arange(count)[None, :] < jnp.arange(count)[:, None]
    same = boxes[..., None, :] == boxes[..., :, None]
    return jnp.sum((same & earlier).astype(jnp.int32), axis=-1)


def pack_fine_kernel(slot_ref, fine_ref, out_ref):
    planes = fine_ref.shape[0]

    def body(k, carry):
        slot = slot_ref[k]

        @pl.when(slot >= 0)
        def _():
            out_ref[slot] = fine_ref[k]

        return carry

    lax.fori_loop(0, planes, body, 0)


def pack_coarse_kernel(slot_ref, coarse_ref, out_ref):
    planes, _, _, depth = coarse_ref.shape

    def body(k, carry):
        slot = slot_ref[k]
        pair = slot // 2

        @pl.when(slot % 2 == 0)
        def _():
            out_ref[pair, :, :, 0:depth] = coarse_ref[k]

        @pl.when(slot % 2 == 1)
        def _():
            out_ref[pair, :, :, depth : 2 * depth] = coarse_ref[k]

        return carry

    lax.fori_loop(0, planes, body, 0)


def build_kernel(fine_at_ref, coarse_at_ref, fine_ref, coarse_ref, out_ref, ylow_ref, yhigh_ref, xlow_ref, xhigh_ref):
    planes, species, rows, lanes = out_ref.shape
    half = rows // 2
    lane = lax.broadcasted_iota(jnp.int32, (half, lanes), 1)
    row = lax.broadcasted_iota(jnp.int32, (half, lanes), 0)
    sign = jnp.where(lane % 2 == 0, -0.25, 0.25)
    lane_first = lane % (lanes // 2) == 0
    lane_last = lane % (lanes // 2) == lanes // 2 - 1

    def body(c, carry):
        at = [fine_at_ref[2 * c], fine_at_ref[2 * c + 1]]

        @pl.when((at[0] < 0) | (at[1] < 0))
        def _():
            slot = coarse_at_ref[c]
            pair = slot // 2
            index = (slot % 2) * (lanes // 2) + lane // 2
            for s in range(species):
                p = coarse_ref[pair, s]
                below = jnp.where(row == 0, p, pltpu.roll(p, 1, 0))
                above = jnp.where(row == half - 1, p, pltpu.roll(p, half - 1, 0))
                left = jnp.where(lane_first, p, pltpu.roll(p, 1, 1))
                right = jnp.where(lane_last, p, pltpu.roll(p, lanes - 1, 1))
                slope_y = 0.125 * (above - below)
                slope_z = 0.5 * (right - left)
                gz = jnp.take_along_axis(slope_z, index, axis=1) * sign
                even = jnp.take_along_axis(p - slope_y, index, axis=1) + gz
                odd = jnp.take_along_axis(p + slope_y, index, axis=1) + gz
                for child in range(2):

                    @pl.when(at[child] < 0)
                    def _():
                        x = 2 * c + child
                        out_ref[x, s, pl.ds(0, half, 2), :] = even
                        out_ref[x, s, pl.ds(1, half, 2), :] = odd
                        ylow_ref[pl.ds(x * species + s, 1), :] = even[0:1]
                        yhigh_ref[pl.ds(x * species + s, 1), :] = odd[half - 1 : half]

        for child in range(2):

            @pl.when(at[child] >= 0)
            def _():
                x = 2 * c + child
                for s in range(species):
                    value = fine_ref[at[child], s]
                    out_ref[x, s] = value
                    ylow_ref[pl.ds(x * species + s, 1), :] = value[0:1]
                    yhigh_ref[pl.ds(x * species + s, 1), :] = value[rows - 1 : rows]

        return carry

    lax.fori_loop(0, planes // 2, body, 0)
    xlow_ref[...] = out_ref[0]
    xhigh_ref[...] = out_ref[planes - 1]


def step_kernel(edges, diff_ref, u_ref, vel_ref, ylow_ref, yhigh_ref, xlow_ref, xhigh_ref, out_ref, *edge_refs):
    planes, species, rows, lanes = u_ref.shape
    lane = lax.broadcasted_iota(jnp.int32, (rows, lanes), 1)
    row = lax.broadcasted_iota(jnp.int32, (rows, lanes), 0)

    def plane(x, below, above):
        positive = [jnp.maximum(vel_ref[x, k], 0.0) for k in range(3)]
        negative = [jnp.minimum(vel_ref[x, k], 0.0) for k in range(3)]
        keep = 1.0
        for k in range(3):
            keep = keep - (positive[k] - negative[k])
        for s in range(species):
            d = diff_ref[s]
            u = u_ref[x, s]
            y_low = jnp.where(row == 0, ylow_ref[pl.ds(x * species + s, 1), :], pltpu.roll(u, 1, 0))
            y_high = jnp.where(row == rows - 1, yhigh_ref[pl.ds(x * species + s, 1), :], pltpu.roll(u, rows - 1, 0))
            z_low = jnp.where(lane == 0, u, pltpu.roll(u, 1, 1))
            z_high = jnp.where(lane == lanes - 1, u, pltpu.roll(u, lanes - 1, 1))
            new = u * (keep - 6.0 * d)
            for k, (low, high) in enumerate(((below(s), above(s)), (y_low, y_high), (z_low, z_high))):
                new = new + low * (d + positive[k]) + high * (d - negative[k])
            out_ref[x, s] = new
            if edges:
                edge_refs[0][pl.ds(x * species + s, 1), :] = new[0:1]
                edge_refs[1][pl.ds(x * species + s, 1), :] = new[rows - 1 : rows]

    plane(0, lambda s: xlow_ref[s], lambda s: u_ref[1, s])

    def body(x, carry):
        plane(x, lambda s: u_ref[x - 1, s], lambda s: u_ref[x + 1, s])
        return carry

    lax.fori_loop(1, planes - 1, body, 0)
    plane(planes - 1, lambda s: u_ref[planes - 2, s], lambda s: xhigh_ref[s])
    if edges:
        edge_refs[2][...] = out_ref[0]
        edge_refs[3][...] = out_ref[planes - 1]


def halo(ylow, yhigh, xlow, xhigh):
    got = []
    for axis, low, high in (("grp", ylow, yhigh), ("dev", xlow, xhigh)):
        size = lax.axis_size(axis)
        up = [(i, (i + 1) % size) for i in range(size - 1)]
        got.append(lax.ppermute(high, axis, up))
        got.append(lax.ppermute(low, axis, [(b, a) for a, b in up]))
    return got


def on_device(old_fine, old_ids, old_coarse, coarse_ids, velocity, diffusion):
    devices = lax.axis_size("dev")
    me = lax.axis_index("dev")
    planes, species, rows, lanes = old_fine.shape
    coarse_planes = old_coarse.shape[0]
    f32 = jnp.float32

    own_coarse = coarse_ids[0]
    coarse_slot = (own_coarse // coarse_planes) * COARSE_CAP + ranks(own_coarse // coarse_planes)
    coarse_out = pl.pallas_call(
        pack_coarse_kernel,
        out_shape=jax.ShapeDtypeStruct((devices, species, rows // 2, lanes), f32),
        in_specs=[SMEM, VMEM],
        out_specs=VMEM,
        compiler_params=PARAMS,
        name="pack_coarse",
    )(coarse_slot, old_coarse)
    coarse_in = lax.all_to_all(coarse_out, "dev", split_axis=0, concat_axis=0, tiled=True)

    own = old_ids[0]
    own_box = jnp.where(own >= 0, own // planes, -1)
    fine_slot = jnp.where(own >= 0, own_box * FINE_CAP + ranks(own_box), -1)
    fine_out = pl.pallas_call(
        pack_fine_kernel,
        out_shape=jax.ShapeDtypeStruct((devices * FINE_CAP, species, rows, lanes), f32),
        in_specs=[SMEM, VMEM],
        out_specs=VMEM,
        compiler_params=PARAMS,
        name="pack_fine",
    )(fine_slot, old_fine)
    fine_in = lax.all_to_all(fine_out, "dev", split_axis=0, concat_axis=0, tiled=True)

    labels = lax.all_gather(jnp.concatenate([own, own_coarse]), "dev", tiled=False)
    all_ids, all_coarse = labels[:, :planes], labels[:, planes:]
    all_box = jnp.where(all_ids >= 0, all_ids // planes, -1)
    slot_of = jnp.arange(devices)[:, None] * FINE_CAP + ranks(all_box)
    wanted = me * planes + jnp.arange(planes)
    fine_at = jnp.max(jnp.where(all_ids[None] == wanted[:, None, None], slot_of[None], -1), axis=(1, 2))
    coarse_slot_of = jnp.arange(devices)[:, None] * COARSE_CAP + ranks(all_coarse // coarse_planes)
    coarse_wanted = me * coarse_planes + jnp.arange(coarse_planes)
    coarse_at = jnp.max(
        jnp.where(all_coarse[None] == coarse_wanted[:, None, None], coarse_slot_of[None], 0), axis=(1, 2)
    )

    edge_shapes = [jax.ShapeDtypeStruct((planes * species, lanes), f32)] * 2 + [
        jax.ShapeDtypeStruct((species, rows, lanes), f32)
    ] * 2
    state_shape = jax.ShapeDtypeStruct(old_fine.shape, f32)
    state, *edges = pl.pallas_call(
        build_kernel,
        out_shape=[state_shape] + edge_shapes,
        in_specs=[SMEM, SMEM, VMEM, VMEM],
        out_specs=[VMEM] * 5,
        compiler_params=PARAMS,
        name="build",
    )(fine_at, coarse_at, fine_in, coarse_in)

    for repeat in range(ITERS):
        last = repeat == ITERS - 1
        around = halo(*edges)
        state, *edges = pl.pallas_call(
            functools.partial(step_kernel, not last),
            out_shape=[state_shape] + ([] if last else edge_shapes),
            in_specs=[SMEM] + [VMEM] * 6,
            out_specs=[VMEM] * (1 if last else 5),
            compiler_params=PARAMS,
            name="step",
        )(diffusion, state, velocity, *around)
    return state


def solution(mesh):
    in_specs = (
        P("dev", None, "grp", None),
        P("grp", "dev"),
        P("dev", None, "grp", None),
        P("grp", "dev"),
        P("dev", None, "grp", None),
        P(),
    )
    out_specs = P("dev", None, "grp", None)
    return jax.shard_map(
        on_device, mesh=mesh, in_specs=in_specs, out_specs=out_specs, check_vma=False
    )
```

```python
import functools

import jax
import jax.numpy as jnp
from jax import lax
from jax.experimental import pallas as pl
from jax.experimental.pallas import tpu as pltpu
from jax.sharding import PartitionSpec as P

ITERS = 2
FINE_CAP = 4
COARSE_CAP = 2
DIRECT = 5
EXTRA = 2 * FINE_CAP + 1 - DIRECT
VMEM = pl.BlockSpec(memory_space=pltpu.VMEM)
SMEM = pl.BlockSpec(memory_space=pltpu.SMEM)
PARAMS = pltpu.CompilerParams(vmem_limit_bytes=56 * 1024 * 1024)


def ranks(boxes):
    count = boxes.shape[-1]
    earlier = jnp.arange(count)[None, :] < jnp.arange(count)[:, None]
    same = boxes[..., None, :] == boxes[..., :, None]
    return jnp.sum((same & earlier).astype(jnp.int32), axis=-1)


def plan_kernel(me_ref, units_ref, row_ref, column_ref):
    devices, lanes = units_ref.shape
    me = me_ref[0]
    units = units_ref[...]
    source = lax.broadcasted_iota(jnp.int32, units.shape, 0)
    lane = lax.broadcasted_iota(jnp.int32, units.shape, 1)
    surplus = pltpu.roll(jnp.maximum(units - DIRECT, 0), 0, 1, stride=1, stride_axis=0)
    none = jnp.full(units.shape, -1, jnp.int32)

    def one_round(r, carry):
        left, free, second, through, *chosen = carry
        ok = (left > 0) & (free > 0) & (second > 0)
        position = DIRECT - free
        item = surplus - left
        chosen = [jnp.where(ok & (item == i), r * 8 + position, table) for i, table in enumerate(chosen)]
        through = jnp.where(ok, source * 8 + position, through)
        used = ok.astype(jnp.int32)
        left, free, second = left - used, free - used, second - used
        free = pltpu.roll(free, lanes - 1, 1)
        second = pltpu.roll(pltpu.roll(second, devices - 1, 0), lanes - 1, 1)
        through = pltpu.roll(pltpu.roll(through, devices - 1, 0), lanes - 1, 1)
        return (left, free, second, through, *chosen)

    init = (surplus, jnp.maximum(DIRECT - units, 0), jnp.ones(units.shape, jnp.int32), none) + (none,) * EXTRA
    left, _, _, through, *chosen = lax.fori_loop(0, devices, one_round, init)
    for i in range(EXTRA):
        row_ref[i : i + 1] = jnp.max(jnp.where(source == me, chosen[i], -1), axis=0, keepdims=True)
    row_ref[EXTRA : EXTRA + 1] = jnp.max(left, axis=0, keepdims=True)
    column = none
    for i in range(EXTRA):
        mine = (lane < devices) & (lane == (source + me) % devices)
        found = jnp.max(jnp.where(mine, chosen[i], -1), axis=1, keepdims=True)
        column = jnp.where(lane == i, found, column)
    found = jnp.max(jnp.where(lane == me, through, -1), axis=1, keepdims=True)
    column_ref[...] = jnp.where(lane == EXTRA, found, column)


def pack_kernel(devices, slot_of, me_ref, fine_at_ref, coarse_at_ref, row_ref, fine_ref, coarse_ref, out_ref):
    planes = fine_ref.shape[0]
    coarse_planes, _, half, depth = coarse_ref.shape

    def fine_plane(k, carry):
        code = fine_at_ref[k]

        @pl.when(code >= 0)
        def _():
            for h in range(2):
                slot = slot_of(me_ref[0], row_ref, code // FINE_CAP, 2 * (code % FINE_CAP) + h)

                @pl.when(slot >= 0)
                def _():
                    out_ref[slot] = fine_ref[k, :, h * half : (h + 1) * half, :]

        return carry

    lax.fori_loop(0, planes, fine_plane, 0)

    def coarse_plane(k, carry):
        code = coarse_at_ref[k]

        @pl.when(code >= 0)
        def _():
            at = code // 2
            slot = slot_of(me_ref[0], row_ref, at // (DIRECT + EXTRA), at % (DIRECT + EXTRA))
            for j in range(2):

                @pl.when((slot >= 0) & (code % 2 == j))
                def _():
                    out_ref[slot, :, :, j * depth : (j + 1) * depth] = coarse_ref[k]

        return carry

    lax.fori_loop(0, coarse_planes, coarse_plane, 0)


def first_slot(devices, me, row_ref, box, unit):
    t = (me + box) % devices
    code = row_ref[jnp.maximum(unit - DIRECT, 0), t]
    relay = jnp.where(code >= 0, ((t + code // 8) % devices) * DIRECT + code % 8, -1)
    return jnp.where(unit < DIRECT, box * DIRECT + unit, relay)


def direct_slot(me, row_ref, box, unit):
    return jnp.where(unit < DIRECT, -1, box * EXTRA + unit - DIRECT)


def forward_kernel(me_ref, column_ref, in_ref, out_ref):
    devices = out_ref.shape[0]

    def body(a, carry):
        code = column_ref[a, EXTRA]

        @pl.when(code >= 0)
        def _():
            out_ref[(me_ref[0] - a + devices) % devices] = in_ref[(code // 8) * DIRECT + code % 8]

        return carry

    lax.fori_loop(0, devices, body, 0)


def rows_to_edges(flat_ref, ylow_ref, yhigh_ref, planes, species, rows):
    for s in range(species):
        for x in range(0, planes, 8):
            for edge_ref, at in ((ylow_ref, 0), (yhigh_ref, rows - 1)):
                start = (x * species + s) * rows + at
                edge_ref[s * planes + x : s * planes + x + 8] = flat_ref[pl.ds(start, 8, stride=species * rows), :]


def build_kernel(
    planned, shape, me_ref, column_ref, fine_at_ref, coarse_at_ref, first_ref, second_ref,
    out_ref, ylow_ref, yhigh_ref, xlow_ref, xhigh_ref,
):
    planes, species, rows, lanes = shape
    half = rows // 2
    devices = column_ref.shape[0]
    lane = lax.broadcasted_iota(jnp.int32, (half, lanes), 1)
    row = lax.broadcasted_iota(jnp.int32, (half, lanes), 0)
    sign = jnp.where(lane % 2 == 0, -0.25, 0.25)
    lane_first = lane % (lanes // 2) == 0
    lane_last = lane % (lanes // 2) == lanes // 2 - 1

    def late(source, unit):
        if not planned:
            return source * EXTRA + jnp.maximum(unit - DIRECT, 0)
        code = column_ref[source, jnp.maximum(unit - DIRECT, 0)]
        return jnp.where(unit < DIRECT, 0, (source + me_ref[0] + code // 8) % devices)

    def fetch(source, unit, use):
        @pl.when(unit < DIRECT)
        def _():
            use(first_ref, source * DIRECT + unit)

        @pl.when(unit >= DIRECT)
        def _():
            use(second_ref, late(source, unit))

    def body(c, carry):
        at = [fine_at_ref[2 * c], fine_at_ref[2 * c + 1]]

        @pl.when((at[0] < 0) | (at[1] < 0))
        def _():
            code = coarse_at_ref[c]
            index = (code % 2) * (lanes // 2) + lane // 2

            def interpolate(ref, slot):
                for s in range(species):
                    p = ref[slot, s]
                    below = jnp.where(row == 0, p, pltpu.roll(p, 1, 0))
                    above = jnp.where(row == half - 1, p, pltpu.roll(p, half - 1, 0))
                    left = jnp.where(lane_first, p, pltpu.roll(p, 1, 1))
                    right = jnp.where(lane_last, p, pltpu.roll(p, lanes - 1, 1))
                    slope_y = 0.125 * (above - below)
                    slope_z = 0.5 * (right - left)
                    gz = jnp.take_along_axis(slope_z, index, axis=1) * sign
                    even = jnp.take_along_axis(p - slope_y, index, axis=1) + gz
                    odd = jnp.take_along_axis(p + slope_y, index, axis=1) + gz
                    for child in range(2):
                        start = pl.multiple_of(((2 * c + child) * species + s) * rows, rows)
                        out_ref[pl.ds(start, half, stride=2), :] = even
                        out_ref[pl.ds(start + 1, half, stride=2), :] = odd

            fetch(code // 2 // (DIRECT + EXTRA), code // 2 % (DIRECT + EXTRA), interpolate)

        for child in range(2):

            @pl.when(at[child] >= 0)
            def _():
                for h in range(2):

                    def copy(ref, slot):
                        for s in range(species):
                            start = pl.multiple_of(((2 * c + child) * species + s) * rows + h * half, half)
                            out_ref[pl.ds(start, half), :] = ref[slot, s]

                    fetch(at[child] // FINE_CAP, 2 * (at[child] % FINE_CAP) + h, copy)

        return carry

    lax.fori_loop(0, planes // 2, body, 0)
    rows_to_edges(out_ref, ylow_ref, yhigh_ref, planes, species, rows)
    xlow_ref[...] = out_ref[0 : species * rows]
    xhigh_ref[...] = out_ref[(planes - 1) * species * rows : planes * species * rows]


def step_kernel(shape, diff_ref, u_ref, vel_ref, ylow_ref, yhigh_ref, xlow_ref, xhigh_ref, out_ref, *edge_refs):
    planes, species, rows, lanes = shape
    size = species * rows
    lane = lax.broadcasted_iota(jnp.int32, (rows, lanes), 1)
    row = lax.broadcasted_iota(jnp.int32, (rows, lanes), 0)

    def plane(x, below, above):
        positive = [jnp.maximum(vel_ref[x, k], 0.0) for k in range(3)]
        negative = [jnp.minimum(vel_ref[x, k], 0.0) for k in range(3)]
        keep = 1.0
        for k in range(3):
            keep = keep - (positive[k] - negative[k])
        for s in range(species):
            d = diff_ref[s]
            here = pl.ds(pl.multiple_of(x * size + s * rows, rows), rows)
            u = u_ref[here, :]
            edge = pl.ds(s * planes + x, 1)
            y_low = jnp.where(row == 0, ylow_ref[edge, :], pltpu.roll(u, 1, 0))
            y_high = jnp.where(row == rows - 1, yhigh_ref[edge, :], pltpu.roll(u, rows - 1, 0))
            z_low = jnp.where(lane == 0, u, pltpu.roll(u, 1, 1))
            z_high = jnp.where(lane == lanes - 1, u, pltpu.roll(u, lanes - 1, 1))
            new = u * (keep - 6.0 * d)
            for k, (low, high) in enumerate(((below(s), above(s)), (y_low, y_high), (z_low, z_high))):
                new = new + low * (d + positive[k]) + high * (d - negative[k])
            out_ref[here, :] = new

    def at(ref, x):
        return lambda s: ref[pl.ds(pl.multiple_of(x * size + s * rows, rows), rows), :]

    plane(0, at(xlow_ref, 0), at(u_ref, 1))

    def body(x, carry):
        plane(x, at(u_ref, x - 1), at(u_ref, x + 1))
        return carry

    lax.fori_loop(1, planes - 1, body, 0)
    plane(planes - 1, at(u_ref, planes - 2), at(xhigh_ref, 0))
    if edge_refs:
        rows_to_edges(out_ref, edge_refs[0], edge_refs[1], planes, species, rows)
        edge_refs[2][...] = out_ref[0:size]
        edge_refs[3][...] = out_ref[(planes - 1) * size : planes * size]


def halo(ylow, yhigh, xlow, xhigh):
    got = []
    for axis, low, high in (("grp", ylow, yhigh), ("dev", xlow, xhigh)):
        size = lax.axis_size(axis)
        up = [(i, (i + 1) % size) for i in range(size - 1)]
        got.append(lax.ppermute(high, axis, up))
        got.append(lax.ppermute(low, axis, [(b, a) for a, b in up]))
    return got


def on_device(old_fine, old_ids, old_coarse, coarse_ids, velocity, diffusion):
    devices = lax.axis_size("dev")
    me = lax.axis_index("dev")
    me_ref = me.reshape(1).astype(jnp.int32)
    planes, species, rows, lanes = old_fine.shape
    half = rows // 2
    coarse_planes = old_coarse.shape[0]
    unit_count = DIRECT + EXTRA
    f32 = jnp.float32
    i32 = jnp.int32

    def units_shape(count):
        return jax.ShapeDtypeStruct((count, species, half, lanes), f32)

    own, own_coarse = old_ids[0], coarse_ids[0]
    labels = jnp.broadcast_to(jnp.concatenate([own, own_coarse])[None], (devices, planes + coarse_planes))
    labels = lax.all_to_all(labels, "dev", split_axis=0, concat_axis=0, tiled=True)
    all_ids, all_coarse = labels[:, :planes], labels[:, planes:]
    all_box = jnp.where(all_ids >= 0, all_ids // planes, -1)
    all_coarse_box = all_coarse // coarse_planes
    flat_parents = jnp.where(all_ids >= 0, all_ids // 2, -1).reshape(-1)

    def needed(coarse):
        kept = jnp.sum((flat_parents == coarse[..., None]).astype(i32), axis=-1)
        return kept < 2

    box = jnp.arange(lanes) % devices
    fine_units = jnp.sum((all_box[:, None, :] == box[None, :, None]).astype(i32), axis=-1)
    asked = needed(all_coarse)[:, None, :] & (all_coarse_box[:, None, :] == box[None, :, None])
    units = 2 * fine_units + jnp.max(asked.astype(i32), axis=-1)
    row, column = pl.pallas_call(
        plan_kernel,
        out_shape=[jax.ShapeDtypeStruct((8, lanes), i32), jax.ShapeDtypeStruct((devices, lanes), i32)],
        in_specs=[SMEM, VMEM],
        out_specs=[VMEM] * 2,
        name="plan",
    )(me_ref, units)
    feasible = jnp.max(row[EXTRA, :devices]) == 0

    own_box = jnp.where(own >= 0, own // planes, -1)
    send_fine = jnp.where(own >= 0, own_box * FINE_CAP + ranks(own_box), -1)
    own_coarse_box = own_coarse // coarse_planes
    before = jnp.sum((own_box[None, :] == own_coarse_box[:, None]).astype(i32), axis=1)
    send_coarse = (own_coarse_box * unit_count + 2 * before) * 2 + ranks(own_coarse_box)
    send_coarse = jnp.where(needed(own_coarse), send_coarse, -1)

    order = jnp.arange(devices)[:, None]
    wanted = me * planes + jnp.arange(planes)
    fine_at = jnp.where(all_ids[None] == wanted[:, None, None], (order * FINE_CAP + ranks(all_box))[None], -1)
    fine_at = jnp.max(fine_at, axis=(1, 2))
    to_me = jnp.sum((all_box == me).astype(i32), axis=1, keepdims=True)
    coarse_wanted = me * coarse_planes + jnp.arange(coarse_planes)
    coarse_code = (order * unit_count + 2 * to_me) * 2 + ranks(all_coarse_box)
    coarse_at = jnp.where(all_coarse[None] == coarse_wanted[:, None, None], coarse_code[None], 0)
    coarse_at = jnp.max(coarse_at, axis=(1, 2))

    def pack(count, slot_of, name):
        return pl.pallas_call(
            functools.partial(pack_kernel, devices, slot_of),
            out_shape=units_shape(count),
            in_specs=[SMEM] * 4 + [VMEM] * 2,
            out_specs=VMEM,
            compiler_params=PARAMS,
            name=name,
        )(me_ref, send_fine, send_coarse, row, old_fine, old_coarse)

    first = pack(devices * DIRECT, functools.partial(first_slot, devices), "pack")
    first = lax.all_to_all(first, "dev", split_axis=0, concat_axis=0, tiled=True)

    size = species * rows
    edge_shapes = [jax.ShapeDtypeStruct((species * planes, lanes), f32)] * 2 + [
        jax.ShapeDtypeStruct((size, lanes), f32)
    ] * 2
    state_shape = jax.ShapeDtypeStruct((planes * size, lanes), f32)

    def build(planned, second):
        second = lax.all_to_all(second, "dev", split_axis=0, concat_axis=0, tiled=True)
        return pl.pallas_call(
            functools.partial(build_kernel, planned, old_fine.shape),
            out_shape=[state_shape] + edge_shapes,
            in_specs=[SMEM] * 4 + [VMEM] * 2,
            out_specs=[VMEM] * 5,
            compiler_params=PARAMS,
            name="build",
        )(me_ref, column, fine_at, coarse_at, first, second)

    def relayed():
        second = pl.pallas_call(
            forward_kernel,
            out_shape=units_shape(devices),
            in_specs=[SMEM] * 2 + [VMEM],
            out_specs=VMEM,
            compiler_params=PARAMS,
            name="forward",
        )(me_ref, column, first)
        return build(True, second)

    def direct():
        return build(False, pack(devices * EXTRA, direct_slot, "pack_rest"))

    state, *edges = lax.cond(feasible, relayed, direct)

    for repeat in range(ITERS):
        last = repeat == ITERS - 1
        around = halo(*edges)
        state, *edges = pl.pallas_call(
            functools.partial(step_kernel, old_fine.shape),
            out_shape=[state_shape] + ([] if last else edge_shapes),
            in_specs=[SMEM] + [VMEM] * 6,
            out_specs=[VMEM] * (1 if last else 5),
            compiler_params=PARAMS,
            name="step",
        )(diffusion, state, velocity, *around)
    return state.reshape(old_fine.shape)


def solution(mesh):
    in_specs = (
        P("dev", None, "grp", None),
        P("grp", "dev"),
        P("dev", None, "grp", None),
        P("grp", "dev"),
        P("dev", None, "grp", None),
        P(),
    )
    out_specs = P("dev", None, "grp", None)
    return jax.shard_map(
        on_device, mesh=mesh, in_specs=in_specs, out_specs=out_specs, check_vma=False
    )
```

```python
import functools

import jax
import jax.numpy as jnp
from jax import lax
from jax.experimental import pallas as pl
from jax.experimental.pallas import tpu as pltpu
from jax.sharding import PartitionSpec as P

ITERS = 2
FINE_CAP = 4
COARSE_CAP = 2
DIRECT = 5
EXTRA = 2 * FINE_CAP + 1 - DIRECT
CHUNKS = ((0, 6), (6, 9))
VMEM = pl.BlockSpec(memory_space=pltpu.VMEM)
SMEM = pl.BlockSpec(memory_space=pltpu.SMEM)
ANY = pl.BlockSpec(memory_space=pl.ANY)
PARAMS = pltpu.CompilerParams(vmem_limit_bytes=56 * 1024 * 1024)


def ranks(boxes):
    count = boxes.shape[-1]
    earlier = jnp.arange(count)[None, :] < jnp.arange(count)[:, None]
    same = boxes[..., None, :] == boxes[..., :, None]
    return jnp.sum((same & earlier).astype(jnp.int32), axis=-1)


def plan_kernel(me_ref, units_ref, row_ref, column_ref):
    devices, lanes = units_ref.shape
    me = me_ref[0]
    units = units_ref[...]
    source = lax.broadcasted_iota(jnp.int32, units.shape, 0)
    lane = lax.broadcasted_iota(jnp.int32, units.shape, 1)
    surplus = pltpu.roll(jnp.maximum(units - DIRECT, 0), 0, 1, stride=1, stride_axis=0)
    none = jnp.full(units.shape, -1, jnp.int32)

    def one_round(r, carry):
        left, free, second, through, *chosen = carry
        ok = (left > 0) & (free > 0) & (second > 0)
        position = DIRECT - free
        item = surplus - left
        chosen = [jnp.where(ok & (item == i), r * 8 + position, table) for i, table in enumerate(chosen)]
        through = jnp.where(ok, source * 8 + position, through)
        used = ok.astype(jnp.int32)
        left, free, second = left - used, free - used, second - used
        free = pltpu.roll(free, lanes - 1, 1)
        second = pltpu.roll(pltpu.roll(second, devices - 1, 0), lanes - 1, 1)
        through = pltpu.roll(pltpu.roll(through, devices - 1, 0), lanes - 1, 1)
        return (left, free, second, through, *chosen)

    init = (surplus, jnp.maximum(DIRECT - units, 0), jnp.ones(units.shape, jnp.int32), none) + (none,) * EXTRA
    left, _, _, through, *chosen = lax.fori_loop(0, devices, one_round, init)
    for i in range(EXTRA):
        row_ref[i : i + 1] = jnp.max(jnp.where(source == me, chosen[i], -1), axis=0, keepdims=True)
    row_ref[EXTRA : EXTRA + 1] = jnp.max(left, axis=0, keepdims=True)
    column = none
    for i in range(EXTRA):
        mine = (lane < devices) & (lane == (source + me) % devices)
        found = jnp.max(jnp.where(mine, chosen[i], -1), axis=1, keepdims=True)
        column = jnp.where(lane == i, found, column)
    found = jnp.max(jnp.where(lane == me, through, -1), axis=1, keepdims=True)
    column_ref[...] = jnp.where(lane == EXTRA, found, column)


def pack_kernel(slot_of, chunk, me_ref, fine_at_ref, coarse_at_ref, row_ref, fine_ref, coarse_ref, out_ref):
    planes = fine_ref.shape[0]
    coarse_planes, _, half, depth = coarse_ref.shape
    first, end = chunk

    def fine_plane(k, carry):
        code = fine_at_ref[k]

        @pl.when(code >= 0)
        def _():
            for h in range(2):
                slot = slot_of(me_ref[0], row_ref, code // FINE_CAP, 2 * (code % FINE_CAP) + h)

                @pl.when(slot >= 0)
                def _():
                    out_ref[slot] = fine_ref[k, first:end, h * half : (h + 1) * half, :]

        return carry

    lax.fori_loop(0, planes, fine_plane, 0)

    def coarse_plane(k, carry):
        code = coarse_at_ref[k]

        @pl.when(code >= 0)
        def _():
            at = code // 2
            slot = slot_of(me_ref[0], row_ref, at // (DIRECT + EXTRA), at % (DIRECT + EXTRA))
            for j in range(2):

                @pl.when((slot >= 0) & (code % 2 == j))
                def _():
                    out_ref[slot, :, :, j * depth : (j + 1) * depth] = coarse_ref[k, first:end]

        return carry

    lax.fori_loop(0, coarse_planes, coarse_plane, 0)


def first_slot(devices, me, row_ref, box, unit):
    t = (me + box) % devices
    code = row_ref[jnp.maximum(unit - DIRECT, 0), t]
    relay = jnp.where(code >= 0, ((t + code // 8) % devices) * DIRECT + code % 8, -1)
    return jnp.where(unit < DIRECT, box * DIRECT + unit, relay)


def direct_slot(me, row_ref, box, unit):
    return jnp.where(unit < DIRECT, -1, box * EXTRA + unit - DIRECT)


def forward_kernel(me_ref, column_ref, in_ref, out_ref):
    devices = out_ref.shape[0]

    def body(a, carry):
        code = column_ref[a, EXTRA]

        @pl.when(code >= 0)
        def _():
            out_ref[(me_ref[0] - a + devices) % devices] = in_ref[(code // 8) * DIRECT + code % 8]

        return carry

    lax.fori_loop(0, devices, body, 0)


def rows_to_edges(flat_ref, ylow_ref, yhigh_ref, planes, species, rows):
    for s in range(species):
        for x in range(0, planes, 8):
            for edge_ref, at in ((ylow_ref, 0), (yhigh_ref, rows - 1)):
                start = (x * species + s) * rows + at
                edge_ref[s * planes + x : s * planes + x + 8] = flat_ref[pl.ds(start, 8, stride=species * rows), :]


def build_kernel(
    shape, start, me_ref, column_ref, left_ref, fine_at_ref, coarse_at_ref, first_ref, second_ref, rest_ref,
    out_ref, ylow_ref, yhigh_ref, xlow_ref, xhigh_ref, held_ref, sem,
):
    planes, species, rows, lanes = shape
    half = rows // 2
    devices = column_ref.shape[0]
    lane = lax.broadcasted_iota(jnp.int32, (half, lanes), 1)
    row = lax.broadcasted_iota(jnp.int32, (half, lanes), 0)
    sign = jnp.where(lane % 2 == 0, -0.25, 0.25)
    lane_first = lane % (lanes // 2) == 0
    lane_last = lane % (lanes // 2) == lanes // 2 - 1

    planned = left_ref[0] == 0

    def fetch(source, unit, use):
        over = jnp.maximum(unit - DIRECT, 0)

        @pl.when(unit < DIRECT)
        def _():
            use(first_ref, source * DIRECT + unit)

        @pl.when((unit >= DIRECT) & planned)
        def _():
            use(second_ref, (source + me_ref[0] + column_ref[source, over] // 8) % devices)

        @pl.when((unit >= DIRECT) & jnp.logical_not(planned))
        def _():
            copy = pltpu.make_async_copy(
                rest_ref.at[pl.ds(source * EXTRA + over, 1), start : start + species], held_ref, sem
            )
            copy.start()
            copy.wait()
            use(held_ref, 0)

    def body(c, carry):
        at = [fine_at_ref[2 * c], fine_at_ref[2 * c + 1]]

        @pl.when((at[0] < 0) | (at[1] < 0))
        def _():
            code = coarse_at_ref[c]
            index = (code % 2) * (lanes // 2) + lane // 2

            def interpolate(ref, slot):
                for s in range(species):
                    p = ref[slot, s]
                    below = jnp.where(row == 0, p, pltpu.roll(p, 1, 0))
                    above = jnp.where(row == half - 1, p, pltpu.roll(p, half - 1, 0))
                    left = jnp.where(lane_first, p, pltpu.roll(p, 1, 1))
                    right = jnp.where(lane_last, p, pltpu.roll(p, lanes - 1, 1))
                    slope_y = 0.125 * (above - below)
                    slope_z = 0.5 * (right - left)
                    gz = jnp.take_along_axis(slope_z, index, axis=1) * sign
                    even = jnp.take_along_axis(p - slope_y, index, axis=1) + gz
                    odd = jnp.take_along_axis(p + slope_y, index, axis=1) + gz
                    for child in range(2):
                        base = pl.multiple_of(((2 * c + child) * species + s) * rows, rows)
                        out_ref[pl.ds(base, half, stride=2), :] = even
                        out_ref[pl.ds(base + 1, half, stride=2), :] = odd

            fetch(code // 2 // (DIRECT + EXTRA), code // 2 % (DIRECT + EXTRA), interpolate)

        for child in range(2):

            @pl.when(at[child] >= 0)
            def _():
                for h in range(2):

                    def copy(ref, slot):
                        for s in range(species):
                            base = pl.multiple_of(((2 * c + child) * species + s) * rows + h * half, half)
                            out_ref[pl.ds(base, half), :] = ref[slot, s]

                    fetch(at[child] // FINE_CAP, 2 * (at[child] % FINE_CAP) + h, copy)

        return carry

    lax.fori_loop(0, planes // 2, body, 0)
    rows_to_edges(out_ref, ylow_ref, yhigh_ref, planes, species, rows)
    xlow_ref[...] = out_ref[0 : species * rows]
    xhigh_ref[...] = out_ref[(planes - 1) * species * rows : planes * species * rows]


def advance(shape, start, diff_ref, u_ref, vel_ref, ylow_ref, yhigh_ref, xlow_ref, xhigh_ref, out_ref, after):
    planes, species, rows, lanes = shape
    size = species * rows
    lane = lax.broadcasted_iota(jnp.int32, (rows, lanes), 1)
    row = lax.broadcasted_iota(jnp.int32, (rows, lanes), 0)

    def plane(x, below, above):
        positive = [jnp.maximum(vel_ref[x, k], 0.0) for k in range(3)]
        negative = [jnp.minimum(vel_ref[x, k], 0.0) for k in range(3)]
        keep = 1.0
        for k in range(3):
            keep = keep - (positive[k] - negative[k])
        for s in range(species):
            d = diff_ref[start + s]
            here = pl.ds(pl.multiple_of(x * size + s * rows, rows), rows)
            u = u_ref[here, :]
            edge = pl.ds(s * planes + x, 1)
            y_low = jnp.where(row == 0, ylow_ref[edge, :], pltpu.roll(u, 1, 0))
            y_high = jnp.where(row == rows - 1, yhigh_ref[edge, :], pltpu.roll(u, rows - 1, 0))
            z_low = jnp.where(lane == 0, u, pltpu.roll(u, 1, 1))
            z_high = jnp.where(lane == lanes - 1, u, pltpu.roll(u, lanes - 1, 1))
            new = u * (keep - 6.0 * d)
            for k, (low, high) in enumerate(((below(s), above(s)), (y_low, y_high), (z_low, z_high))):
                new = new + low * (d + positive[k]) + high * (d - negative[k])
            out_ref[here, :] = new

    def at(ref, x):
        return lambda s: ref[pl.ds(pl.multiple_of(x * size + s * rows, rows), rows), :]

    def body(x, carry):
        plane(x, at(u_ref, x - 1), at(u_ref, x + 1))
        return carry

    plane(0, at(xlow_ref, 0), at(u_ref, 1))
    for x in range(0, planes, 8):
        lax.fori_loop(max(x, 1), min(x + 8, planes - 1), body, 0)
        if x + 8 == planes:
            plane(planes - 1, at(u_ref, planes - 2), at(xhigh_ref, 0))
        after(x)


def step_kernel(shape, start, diff_ref, u_ref, vel_ref, *refs):
    planes, species, rows, _ = shape
    size = species * rows
    *around, out_ref, ylow_ref, yhigh_ref, xlow_ref, xhigh_ref = refs
    advance(shape, start, diff_ref, u_ref, vel_ref, *around, out_ref, lambda x: None)
    rows_to_edges(out_ref, ylow_ref, yhigh_ref, planes, species, rows)
    xlow_ref[...] = out_ref[0:size]
    xhigh_ref[...] = out_ref[(planes - 1) * size : planes * size]


def last_step_kernel(shape, start, diff_ref, u_ref, vel_ref, *refs):
    planes, species, rows, _ = shape
    size = species * rows
    *around, out_ref, new_ref, sem = refs
    copies = []

    def send(x):
        for i in range(x, x + 8):
            copy = pltpu.make_async_copy(
                new_ref.at[i * size : (i + 1) * size], out_ref.at[i, start * rows : start * rows + size], sem.at[i]
            )
            copy.start()
            copies.append(copy)

    advance(shape, start, diff_ref, u_ref, vel_ref, *around[:4], new_ref, send)
    for copy in copies:
        copy.wait()


def empty_kernel(out_ref):
    pass


def cost(microseconds):
    return pl.CostEstimate(flops=0, bytes_accessed=int(microseconds * 3.6e6), transcendentals=0)


def halo(ylow, yhigh, xlow, xhigh):
    got = []
    for axis, low, high in (("grp", ylow, yhigh), ("dev", xlow, xhigh)):
        size = lax.axis_size(axis)
        up = [(i, (i + 1) % size) for i in range(size - 1)]
        got.append(lax.ppermute(high, axis, up))
        got.append(lax.ppermute(low, axis, [(b, a) for a, b in up]))
    return got


def on_device(old_fine, old_ids, old_coarse, coarse_ids, velocity, diffusion):
    devices = lax.axis_size("dev")
    me = lax.axis_index("dev")
    me_ref = me.reshape(1).astype(jnp.int32)
    planes, species, rows, lanes = old_fine.shape
    half = rows // 2
    coarse_planes = old_coarse.shape[0]
    unit_count = DIRECT + EXTRA
    f32 = jnp.float32
    i32 = jnp.int32

    def units_shape(count, many):
        return jax.ShapeDtypeStruct((count, many, half, lanes), f32)

    own, own_coarse = old_ids[0], coarse_ids[0]
    labels = jnp.broadcast_to(jnp.concatenate([own, own_coarse])[None], (devices, planes + coarse_planes))
    labels = lax.all_to_all(labels, "dev", split_axis=0, concat_axis=0, tiled=True)
    all_ids, all_coarse = labels[:, :planes], labels[:, planes:]
    all_box = jnp.where(all_ids >= 0, all_ids // planes, -1)
    all_coarse_box = all_coarse // coarse_planes
    flat_parents = jnp.where(all_ids >= 0, all_ids // 2, -1).reshape(-1)

    def needed(coarse):
        kept = jnp.sum((flat_parents == coarse[..., None]).astype(i32), axis=-1)
        return kept < 2

    box = jnp.arange(lanes) % devices
    fine_units = jnp.sum((all_box[:, None, :] == box[None, :, None]).astype(i32), axis=-1)
    asked = needed(all_coarse)[:, None, :] & (all_coarse_box[:, None, :] == box[None, :, None])
    units = 2 * fine_units + jnp.max(asked.astype(i32), axis=-1)
    row, column = pl.pallas_call(
        plan_kernel,
        out_shape=[jax.ShapeDtypeStruct((8, lanes), i32), jax.ShapeDtypeStruct((devices, lanes), i32)],
        in_specs=[SMEM, VMEM],
        out_specs=[VMEM] * 2,
        name="plan",
    )(me_ref, units)
    left = jnp.max(row[EXTRA, :devices]).reshape(1)

    own_box = jnp.where(own >= 0, own // planes, -1)
    send_fine = jnp.where(own >= 0, own_box * FINE_CAP + ranks(own_box), -1)
    own_coarse_box = own_coarse // coarse_planes
    before = jnp.sum((own_box[None, :] == own_coarse_box[:, None]).astype(i32), axis=1)
    send_coarse = (own_coarse_box * unit_count + 2 * before) * 2 + ranks(own_coarse_box)
    send_coarse = jnp.where(needed(own_coarse), send_coarse, -1)

    order = jnp.arange(devices)[:, None]
    wanted = me * planes + jnp.arange(planes)
    fine_at = jnp.where(all_ids[None] == wanted[:, None, None], (order * FINE_CAP + ranks(all_box))[None], -1)
    fine_at = jnp.max(fine_at, axis=(1, 2))
    to_me = jnp.sum((all_box == me).astype(i32), axis=1, keepdims=True)
    coarse_wanted = me * coarse_planes + jnp.arange(coarse_planes)
    coarse_code = (order * unit_count + 2 * to_me) * 2 + ranks(all_coarse_box)
    coarse_at = jnp.where(all_coarse[None] == coarse_wanted[:, None, None], coarse_code[None], 0)
    coarse_at = jnp.max(coarse_at, axis=(1, 2))

    def pack(count, slot_of, chunk, name):
        return pl.pallas_call(
            functools.partial(pack_kernel, slot_of, chunk),
            out_shape=units_shape(count, chunk[1] - chunk[0]),
            in_specs=[SMEM] * 4 + [VMEM] * 2,
            out_specs=VMEM,
            compiler_params=PARAMS,
            name=name,
        )(me_ref, send_fine, send_coarse, row, old_fine, old_coarse)

    def exchange(value):
        return lax.all_to_all(value, "dev", split_axis=0, concat_axis=0, tiled=True)

    def no_rest():
        return pl.pallas_call(
            empty_kernel,
            out_shape=units_shape(devices * EXTRA, species),
            out_specs=pl.BlockSpec(memory_space=pl.ANY),
            name="nothing",
        )()

    def rest_direct():
        return exchange(pack(devices * EXTRA, direct_slot, (0, species), "pack_rest"))

    rest = lax.cond(left[0] == 0, no_rest, rest_direct)

    def first_phase(chunk):
        return pack(devices * DIRECT, functools.partial(first_slot, devices), chunk, "pack")

    def second_phase(chunk, first):
        second = pl.pallas_call(
            forward_kernel,
            out_shape=units_shape(devices, chunk[1] - chunk[0]),
            in_specs=[SMEM] * 2 + [VMEM],
            out_specs=VMEM,
            compiler_params=PARAMS,
            cost_estimate=cost(3),
            name="forward",
        )(me_ref, column, first)
        return exchange(second)

    def halves(chunk, first, second):
        start, end = chunk
        count = end - start
        shape = (planes, count, rows, lanes)
        size = count * rows
        edge_shapes = [jax.ShapeDtypeStruct((count * planes, lanes), f32)] * 2 + [
            jax.ShapeDtypeStruct((size, lanes), f32)
        ] * 2
        state_shape = jax.ShapeDtypeStruct((planes * size, lanes), f32)
        state, *edges = pl.pallas_call(
            functools.partial(build_kernel, shape, start),
            out_shape=[state_shape] + edge_shapes,
            in_specs=[SMEM] * 5 + [VMEM] * 2 + [ANY],
            out_specs=[VMEM] * 5,
            scratch_shapes=[pltpu.VMEM((1, count, half, lanes), f32), pltpu.SemaphoreType.DMA],
            compiler_params=PARAMS,
            cost_estimate=cost(count),
            name="build",
        )(me_ref, column, left, fine_at, coarse_at, first, second, rest)
        for _ in range(ITERS - 1):
            state, *edges = pl.pallas_call(
                functools.partial(step_kernel, shape, start),
                out_shape=[state_shape] + edge_shapes,
                in_specs=[SMEM] + [VMEM] * 6,
                out_specs=[VMEM] * 5,
                compiler_params=PARAMS,
                cost_estimate=cost(count),
                name="step",
            )(diffusion, state, velocity, *halo(*edges))
        around = halo(*edges)

        def last(done):
            earlier = [] if done is None else [done]
            return pl.pallas_call(
                functools.partial(last_step_kernel, shape, start),
                out_shape=jax.ShapeDtypeStruct((planes, species * rows, lanes), f32),
                in_specs=[SMEM] + [VMEM] * 6 + [ANY] * len(earlier),
                out_specs=ANY,
                scratch_shapes=[pltpu.VMEM((planes * size, lanes), f32), pltpu.SemaphoreType.DMA((planes,))],
                input_output_aliases={7: 0} if earlier else {},
                compiler_params=PARAMS,
                cost_estimate=cost(count),
                name="last_step",
            )(diffusion, state, velocity, *around, *earlier)

        return around, last

    done, last, first = None, None, exchange(first_phase(CHUNKS[0]))
    for i, chunk in enumerate(CHUNKS):
        second = second_phase(chunk, first)
        if i + 1 < len(CHUNKS):
            packed, second = lax.optimization_barrier((first_phase(CHUNKS[i + 1]), second))
            upcoming = exchange(packed)
        if last is not None:
            done = last(done)
        around, last = halves(chunk, first, second)
        if i + 1 < len(CHUNKS):
            first, _ = lax.optimization_barrier((upcoming, around))
    done = last(done)
    return done.reshape(old_fine.shape)


def solution(mesh):
    in_specs = (
        P("dev", None, "grp", None),
        P("grp", "dev"),
        P("dev", None, "grp", None),
        P("grp", "dev"),
        P("dev", None, "grp", None),
        P(),
    )
    out_specs = P("dev", None, "grp", None)
    return jax.shard_map(
        on_device, mesh=mesh, in_specs=in_specs, out_specs=out_specs, check_vma=False
    )
```

```python
import functools

import jax
import jax.numpy as jnp
from jax import lax
from jax.experimental import pallas as pl
from jax.experimental.pallas import tpu as pltpu
from jax.sharding import PartitionSpec as P

ITERS = 2
FINE_CAP = 4
COARSE_CAP = 2
DIRECT = 5
EXTRA = 2 * FINE_CAP + 1 - DIRECT
VMEM = pl.BlockSpec(memory_space=pltpu.VMEM)
SMEM = pl.BlockSpec(memory_space=pltpu.SMEM)
ANY = pl.BlockSpec(memory_space=pl.ANY)
PARAMS = pltpu.CompilerParams(vmem_limit_bytes=56 * 1024 * 1024)
UNROLL = 4


def ranks(boxes):
    count = boxes.shape[-1]
    earlier = jnp.arange(count)[None, :] < jnp.arange(count)[:, None]
    same = boxes[..., None, :] == boxes[..., :, None]
    return jnp.sum((same & earlier).astype(jnp.int32), axis=-1)


def plan_kernel(me_ref, units_ref, row_ref, column_ref):
    devices, lanes = units_ref.shape
    me = me_ref[0]
    units = units_ref[...]
    source = lax.broadcasted_iota(jnp.int32, units.shape, 0)
    lane = lax.broadcasted_iota(jnp.int32, units.shape, 1)
    surplus = pltpu.roll(jnp.maximum(units - DIRECT, 0), 0, 1, stride=1, stride_axis=0)
    none = jnp.full(units.shape, -1, jnp.int32)

    def one_round(r, carry):
        left, free, second, through, *chosen = carry
        ok = (left > 0) & (free > 0) & (second > 0)
        position = DIRECT - free
        item = surplus - left
        chosen = [jnp.where(ok & (item == i), r * 8 + position, table) for i, table in enumerate(chosen)]
        through = jnp.where(ok, source * 8 + position, through)
        used = ok.astype(jnp.int32)
        left, free, second = left - used, free - used, second - used
        free = pltpu.roll(free, lanes - 1, 1)
        second = pltpu.roll(pltpu.roll(second, devices - 1, 0), lanes - 1, 1)
        through = pltpu.roll(pltpu.roll(through, devices - 1, 0), lanes - 1, 1)
        return (left, free, second, through, *chosen)

    init = (surplus, jnp.maximum(DIRECT - units, 0), jnp.ones(units.shape, jnp.int32), none) + (none,) * EXTRA
    left, _, _, through, *chosen = lax.fori_loop(0, devices, one_round, init)
    for i in range(EXTRA):
        row_ref[i : i + 1] = jnp.max(jnp.where(source == me, chosen[i], -1), axis=0, keepdims=True)
    row_ref[EXTRA : EXTRA + 1] = jnp.max(left, axis=0, keepdims=True)
    row_ref[EXTRA + 1 : EXTRA + 2] = jnp.max(jnp.where(source == me, units, 0), axis=0, keepdims=True)
    column = none
    for i in range(EXTRA):
        mine = (lane < devices) & (lane == (source + me) % devices)
        found = jnp.max(jnp.where(mine, chosen[i], -1), axis=1, keepdims=True)
        column = jnp.where(lane == i, found, column)
    found = jnp.max(jnp.where(lane == me, through, -1), axis=1, keepdims=True)
    column_ref[...] = jnp.where(lane == EXTRA, found, column)


def pack_direct_kernel(fine_at_ref, coarse_at_ref, fine_ref, coarse_ref, out_ref, pairs_ref):
    planes = fine_ref.shape[0]
    coarse_planes, _, half, depth = coarse_ref.shape

    def fine_plane(k, carry):
        code = fine_at_ref[k]
        for h in range(2):
            unit = 2 * (code % FINE_CAP) + h

            @pl.when((code >= 0) & (unit < DIRECT))
            def _():
                out_ref[(code // FINE_CAP) * DIRECT + unit] = fine_ref[k, :, h * half : (h + 1) * half, :]

        return carry

    lax.fori_loop(0, planes, fine_plane, 0)

    def coarse_plane(k, carry):
        code = coarse_at_ref[k]
        for j in range(COARSE_CAP):

            @pl.when(code % COARSE_CAP == j)
            def _():
                pairs_ref[code // COARSE_CAP, :, :, j * depth : (j + 1) * depth] = coarse_ref[k]

        return carry

    lax.fori_loop(0, coarse_planes, coarse_plane, 0)


def pack_late_kernel(me_ref, row_ref, fine_at_ref, fine_ref, pairs_ref, _, out_ref, fine_sem, coarse_sem):
    planes, _, rows, _ = fine_ref.shape
    devices = pairs_ref.shape[0]
    half = rows // 2

    def slot_of(box, unit):
        t = (me_ref[0] + box) % devices
        code = row_ref[jnp.maximum(unit - DIRECT, 0), t]
        relay = jnp.where(code >= 0, ((t + code // 8) % devices) * DIRECT + code % 8, -1)
        return jnp.where(unit < DIRECT, box * DIRECT + unit, relay)

    def each(act):
        def fine_plane(k, carry):
            code = fine_at_ref[k]

            @pl.when((code >= 0) & (2 * (code % FINE_CAP) + 1 >= DIRECT))
            def _():
                for h in range(2):
                    unit = 2 * (code % FINE_CAP) + h
                    slot = slot_of(code // FINE_CAP, unit)

                    @pl.when((unit >= DIRECT) & (slot >= 0))
                    def _():
                        source = fine_ref.at[k, :, h * half : (h + 1) * half, :]
                        act(pltpu.make_async_copy(source, out_ref.at[slot], fine_sem.at[2 * k + h]))

            return carry

        lax.fori_loop(0, planes, fine_plane, 0)

        def coarse_pair(box, carry):
            units = row_ref[EXTRA + 1, box]
            slot = slot_of(box, jnp.maximum(units - 1, 0))

            @pl.when((units % 2 == 1) & (slot >= 0))
            def _():
                act(pltpu.make_async_copy(pairs_ref.at[box], out_ref.at[slot], coarse_sem.at[box]))

            return carry

        lax.fori_loop(0, devices, coarse_pair, 0)

    each(lambda copy: copy.start())
    each(lambda copy: copy.wait())


def pack_rest_kernel(row_ref, fine_at_ref, fine_ref, pairs_ref, out_ref):
    planes, _, rows, _ = fine_ref.shape
    devices = pairs_ref.shape[0]
    half = rows // 2

    def fine_plane(k, carry):
        code = fine_at_ref[k]
        for h in range(2):
            unit = 2 * (code % FINE_CAP) + h

            @pl.when((code >= 0) & (unit >= DIRECT))
            def _():
                out_ref[(code // FINE_CAP) * EXTRA + unit - DIRECT] = fine_ref[k, :, h * half : (h + 1) * half, :]

        return carry

    lax.fori_loop(0, planes, fine_plane, 0)

    def coarse_pair(box, carry):
        units = row_ref[EXTRA + 1, box]

        @pl.when((units % 2 == 1) & (units > DIRECT))
        def _():
            out_ref[box * EXTRA + units - 1 - DIRECT] = pairs_ref[box]

        return carry

    lax.fori_loop(0, devices, coarse_pair, 0)


def forward_kernel(me_ref, column_ref, in_ref, out_ref):
    devices = out_ref.shape[0]

    def body(a, carry):
        code = column_ref[a, EXTRA]

        @pl.when(code >= 0)
        def _():
            out_ref[(me_ref[0] - a + devices) % devices] = in_ref[(code // 8) * DIRECT + code % 8]

        return carry

    lax.fori_loop(0, devices, body, 0)


def rows_to_edges(flat_ref, ylow_ref, yhigh_ref, planes, species, rows):
    for s in range(species):
        for x in range(0, planes, 8):
            for edge_ref, at in ((ylow_ref, 0), (yhigh_ref, rows - 1)):
                start = (x * species + s) * rows + at
                edge_ref[s * planes + x : s * planes + x + 8] = flat_ref[pl.ds(start, 8, stride=species * rows), :]


def interpolate(ref, slot, part, store):
    _, species, half, lanes = ref.shape
    lane = lax.broadcasted_iota(jnp.int32, (half, lanes), 1)
    row = lax.broadcasted_iota(jnp.int32, (half, lanes), 0)
    sign = jnp.where(lane % 2 == 0, -0.25, 0.25)
    lane_first = lane % (lanes // 2) == 0
    lane_last = lane % (lanes // 2) == lanes // 2 - 1
    index = part * (lanes // 2) + lane // 2
    for s in range(species):
        p = ref[slot, s]
        below = jnp.where(row == 0, p, pltpu.roll(p, 1, 0))
        above = jnp.where(row == half - 1, p, pltpu.roll(p, half - 1, 0))
        left = jnp.where(lane_first, p, pltpu.roll(p, 1, 1))
        right = jnp.where(lane_last, p, pltpu.roll(p, lanes - 1, 1))
        slope_y = 0.125 * (above - below)
        slope_z = 0.5 * (right - left)
        gz = jnp.take_along_axis(slope_z, index, axis=1) * sign
        even = jnp.take_along_axis(p - slope_y, index, axis=1) + gz
        odd = jnp.take_along_axis(p + slope_y, index, axis=1) + gz
        store(s, even, odd)


def build_kernel(shape, fine_at_ref, coarse_at_ref, first_ref, out_ref, ylow_ref, yhigh_ref):
    planes, species, rows, lanes = shape
    half = rows // 2

    def body(c, carry):
        at = [fine_at_ref[2 * c], fine_at_ref[2 * c + 1]]
        code = coarse_at_ref[c]
        unit = code // 2 % (DIRECT + EXTRA)

        @pl.when(((at[0] < 0) | (at[1] < 0)) & (unit < DIRECT))
        def _():
            def store(s, even, odd):
                for child in range(2):
                    base = pl.multiple_of(((2 * c + child) * species + s) * rows, rows)
                    out_ref[pl.ds(base, half, stride=2), :] = even
                    out_ref[pl.ds(base + 1, half, stride=2), :] = odd

            interpolate(first_ref, code // 2 // (DIRECT + EXTRA) * DIRECT + unit, code % 2, store)

        for child in range(2):
            for h in range(2):
                late = 2 * (at[child] % FINE_CAP) + h

                @pl.when((at[child] >= 0) & (late < DIRECT))
                def _():
                    slot = at[child] // FINE_CAP * DIRECT + late
                    for s in range(species):
                        base = pl.multiple_of(((2 * c + child) * species + s) * rows + h * half, half)
                        out_ref[pl.ds(base, half), :] = first_ref[slot, s]

        return carry

    lax.fori_loop(0, planes // 2, body, 0)
    rows_to_edges(out_ref, ylow_ref, yhigh_ref, planes, species, rows)


def build_late_kernel(
    me_ref, column_ref, left_ref, fine_at_ref, coarse_at_ref, second_ref, rest_ref, _, ylow_in_ref, yhigh_in_ref,
    state_ref, ylow_ref, yhigh_ref, xlow_ref, xhigh_ref, held_ref, plane_ref, sem, late_sem,
):
    planes, species, rows, lanes = state_ref.shape
    half = rows // 2
    devices = column_ref.shape[0]
    planned = left_ref[0] == 0
    ylow_ref[...] = ylow_in_ref[...]
    yhigh_ref[...] = yhigh_in_ref[...]

    def now(source, target):
        copy = pltpu.make_async_copy(source, target, sem)
        copy.start()
        copy.wait()

    def relayed(source, unit):
        return (source + me_ref[0] + column_ref[source, unit - DIRECT] // 8) % devices

    def bring(source, unit):
        now(rest_ref.at[pl.ds(source * EXTRA + unit - DIRECT, 1)], held_ref)

    def parent(c, carry):
        at = [fine_at_ref[2 * c], fine_at_ref[2 * c + 1]]
        code = coarse_at_ref[c]
        unit = code // 2 % (DIRECT + EXTRA)
        source = code // 2 // (DIRECT + EXTRA)

        @pl.when(((at[0] < 0) | (at[1] < 0)) & (unit >= DIRECT))
        def _():
            def store(s, even, odd):
                plane_ref[s, pl.ds(0, half, stride=2), :] = even
                plane_ref[s, pl.ds(1, half, stride=2), :] = odd

            @pl.when(planned)
            def _():
                held_ref[0] = second_ref[relayed(source, unit)]

            @pl.when(jnp.logical_not(planned))
            def _():
                bring(source, unit)

            interpolate(held_ref, 0, code % 2, store)
            for child in range(2):

                @pl.when(at[child] < 0)
                def _():
                    x = 2 * c + child
                    now(plane_ref, state_ref.at[x])
                    for s in range(species):
                        ylow_ref[pl.ds(s * planes + x, 1), :] = plane_ref[s, 0:1]
                        yhigh_ref[pl.ds(s * planes + x, 1), :] = plane_ref[s, rows - 1 : rows]

        return carry

    lax.fori_loop(0, planes // 2, parent, 0)

    def each(begin):
        def plane(x, carry):
            at = fine_at_ref[x]

            @pl.when((at >= 0) & (2 * (at % FINE_CAP) + 1 >= DIRECT))
            def _():
                source = at // FINE_CAP
                for h in range(2):
                    unit = 2 * (at % FINE_CAP) + h
                    target = state_ref.at[x, :, h * half : (h + 1) * half, :]
                    edge_ref, edge = ((ylow_ref, 0), (yhigh_ref, half - 1))[h]

                    def set_edge(ref, slot):
                        for s in range(species):
                            edge_ref[pl.ds(s * planes + x, 1), :] = ref[slot, s, edge : edge + 1]

                    @pl.when((unit >= DIRECT) & planned)
                    def _():
                        slot = relayed(source, jnp.maximum(unit, DIRECT))
                        copy = pltpu.make_async_copy(second_ref.at[slot], target, late_sem.at[2 * x + h])
                        if begin:
                            copy.start()
                            set_edge(second_ref, slot)
                        else:
                            copy.wait()

                    if begin:

                        @pl.when((unit >= DIRECT) & jnp.logical_not(planned))
                        def _():
                            bring(source, jnp.maximum(unit, DIRECT))
                            now(held_ref.at[0], target)
                            set_edge(held_ref, 0)

            return carry

        lax.fori_loop(0, planes, plane, 0)

    each(True)
    each(False)
    now(state_ref.at[0], xlow_ref)
    now(state_ref.at[planes - 1], xhigh_ref)


def advance(shape, diff_ref, u_ref, vel_ref, ylow_ref, yhigh_ref, xlow_ref, xhigh_ref, out_ref, after):
    planes, species, rows, lanes = shape
    size = species * rows
    lane = lax.broadcasted_iota(jnp.int32, (rows, lanes), 1)
    row = lax.broadcasted_iota(jnp.int32, (rows, lanes), 0)

    def plane(x, below, above):
        positive = [jnp.maximum(vel_ref[x, k], 0.0) for k in range(3)]
        negative = [jnp.minimum(vel_ref[x, k], 0.0) for k in range(3)]
        keep = 1.0
        for k in range(3):
            keep = keep - (positive[k] - negative[k])
        for s in range(species):
            d = diff_ref[s]
            here = pl.ds(pl.multiple_of(x * size + s * rows, rows), rows)
            u = u_ref[here, :]
            edge = pl.ds(s * planes + x, 1)
            y_low = jnp.where(row == 0, ylow_ref[edge, :], pltpu.roll(u, 1, 0))
            y_high = jnp.where(row == rows - 1, yhigh_ref[edge, :], pltpu.roll(u, rows - 1, 0))
            z_low = jnp.where(lane == 0, u, pltpu.roll(u, 1, 1))
            z_high = jnp.where(lane == lanes - 1, u, pltpu.roll(u, lanes - 1, 1))
            new = u * (keep - 6.0 * d)
            for k, (low, high) in enumerate(((below(s), above(s)), (y_low, y_high), (z_low, z_high))):
                new = new + low * (d + positive[k]) + high * (d - negative[k])
            out_ref[here, :] = new

    def at(ref, x):
        return lambda s: ref[pl.ds(pl.multiple_of(x * size + s * rows, rows), rows), :]

    def group(x, first, last):
        for i in range(UNROLL):
            below = at(xlow_ref, 0) if first and i == 0 else at(u_ref, x + i - 1)
            above = at(xhigh_ref, 0) if last and i == UNROLL - 1 else at(u_ref, x + i + 1)
            plane(x + i, below, above)
        after(x)

    def body(g, carry):
        group(g * UNROLL, False, False)
        return carry

    group(0, True, False)
    lax.fori_loop(1, planes // UNROLL - 1, body, 0)
    group(planes - UNROLL, False, True)


def step_kernel(shape, diff_ref, u_ref, vel_ref, *refs):
    planes, species, rows, _ = shape
    size = species * rows
    *around, out_ref, ylow_ref, yhigh_ref, xlow_ref, xhigh_ref = refs
    advance(shape, diff_ref, u_ref, vel_ref, *around, out_ref, lambda x: None)
    rows_to_edges(out_ref, ylow_ref, yhigh_ref, planes, species, rows)
    xlow_ref[...] = out_ref[0:size]
    xhigh_ref[...] = out_ref[(planes - 1) * size : planes * size]


def last_step_kernel(shape, diff_ref, u_ref, vel_ref, *refs):
    planes, species, rows, _ = shape
    size = UNROLL * species * rows
    *around, out_ref, new_ref, sem = refs

    def copy(g):
        part = pl.ds(pl.multiple_of(g * size, size), size)
        return pltpu.make_async_copy(new_ref.at[part], out_ref.at[part], sem.at[g])

    advance(shape, diff_ref, u_ref, vel_ref, *around, new_ref, lambda x: copy(x // UNROLL).start())

    def finish(g, carry):
        copy(g).wait()
        return carry

    lax.fori_loop(0, planes // UNROLL, finish, 0)


def empty_kernel(out_ref):
    pass


def cost(microseconds):
    return pl.CostEstimate(flops=0, bytes_accessed=int(microseconds * 3.6e6), transcendentals=0)


def halo(ylow, yhigh, xlow, xhigh):
    got = []
    for axis, low, high in (("grp", ylow, yhigh), ("dev", xlow, xhigh)):
        size = lax.axis_size(axis)
        up = [(i, (i + 1) % size) for i in range(size - 1)]
        got.append(lax.ppermute(high, axis, up))
        got.append(lax.ppermute(low, axis, [(b, a) for a, b in up]))
    return got


def on_device(old_fine, old_ids, old_coarse, coarse_ids, velocity, diffusion):
    devices = lax.axis_size("dev")
    me = lax.axis_index("dev")
    me_ref = me.reshape(1).astype(jnp.int32)
    planes, species, rows, lanes = old_fine.shape
    half = rows // 2
    coarse_planes = old_coarse.shape[0]
    unit_count = DIRECT + EXTRA
    f32 = jnp.float32
    i32 = jnp.int32

    def units_shape(count):
        return jax.ShapeDtypeStruct((count, species, half, lanes), f32)

    own, own_coarse = old_ids[0], coarse_ids[0]
    own_box = jnp.where(own >= 0, own // planes, -1)
    send_fine = jnp.where(own >= 0, own_box * FINE_CAP + ranks(own_box), -1)
    own_coarse_box = own_coarse // coarse_planes
    send_coarse = own_coarse_box * COARSE_CAP + ranks(own_coarse_box)
    packed, pairs = pl.pallas_call(
        pack_direct_kernel,
        out_shape=[units_shape(devices * DIRECT), units_shape(devices)],
        in_specs=[SMEM] * 2 + [VMEM] * 2,
        out_specs=[VMEM] * 2,
        compiler_params=PARAMS,
        cost_estimate=cost(8),
        name="pack_direct",
    )(send_fine, send_coarse, old_fine, old_coarse)

    labels = jnp.broadcast_to(jnp.concatenate([own, own_coarse])[None], (devices, planes + coarse_planes))
    labels = lax.all_to_all(labels, "dev", split_axis=0, concat_axis=0, tiled=True)
    all_ids, all_coarse = labels[:, :planes], labels[:, planes:]
    all_box = jnp.where(all_ids >= 0, all_ids // planes, -1)
    all_coarse_box = all_coarse // coarse_planes
    flat_parents = jnp.where(all_ids >= 0, all_ids // 2, -1).reshape(-1)

    def needed(coarse):
        kept = jnp.sum((flat_parents == coarse[..., None]).astype(i32), axis=-1)
        return kept < 2

    box = jnp.arange(lanes) % devices
    fine_units = jnp.sum((all_box[:, None, :] == box[None, :, None]).astype(i32), axis=-1)
    asked = needed(all_coarse)[:, None, :] & (all_coarse_box[:, None, :] == box[None, :, None])
    units = 2 * fine_units + jnp.max(asked.astype(i32), axis=-1)
    row, column = pl.pallas_call(
        plan_kernel,
        out_shape=[jax.ShapeDtypeStruct((8, lanes), i32), jax.ShapeDtypeStruct((devices, lanes), i32)],
        in_specs=[SMEM, VMEM],
        out_specs=[VMEM] * 2,
        name="plan",
    )(me_ref, units)
    left = jnp.max(row[EXTRA, :devices]).reshape(1)

    order = jnp.arange(devices)[:, None]
    wanted = me * planes + jnp.arange(planes)
    fine_at = jnp.where(all_ids[None] == wanted[:, None, None], (order * FINE_CAP + ranks(all_box))[None], -1)
    fine_at = jnp.max(fine_at, axis=(1, 2))
    to_me = jnp.sum((all_box == me).astype(i32), axis=1, keepdims=True)
    coarse_wanted = me * coarse_planes + jnp.arange(coarse_planes)
    coarse_code = (order * unit_count + 2 * to_me) * 2 + ranks(all_coarse_box)
    coarse_at = jnp.where(all_coarse[None] == coarse_wanted[:, None, None], coarse_code[None], 0)
    coarse_at = jnp.max(coarse_at, axis=(1, 2))

    def exchange(value):
        return lax.all_to_all(value, "dev", split_axis=0, concat_axis=0, tiled=True)

    packed = pl.pallas_call(
        pack_late_kernel,
        out_shape=units_shape(devices * DIRECT),
        in_specs=[SMEM] * 3 + [ANY] * 3,
        out_specs=ANY,
        scratch_shapes=[pltpu.SemaphoreType.DMA((2 * planes,)), pltpu.SemaphoreType.DMA((devices,))],
        input_output_aliases={5: 0},
        name="pack_late",
    )(me_ref, row, send_fine, old_fine, pairs, packed)

    def no_rest():
        return pl.pallas_call(empty_kernel, out_shape=units_shape(devices * EXTRA), out_specs=ANY, name="nothing")()

    def rest_direct():
        rest = pl.pallas_call(
            pack_rest_kernel,
            out_shape=units_shape(devices * EXTRA),
            in_specs=[SMEM] * 2 + [VMEM] * 2,
            out_specs=VMEM,
            compiler_params=PARAMS,
            name="pack_rest",
        )(row, send_fine, old_fine, pairs)
        return exchange(rest)

    rest = lax.cond(left[0] == 0, no_rest, rest_direct)
    packed, rest = lax.optimization_barrier((packed, rest))
    first = exchange(packed)
    second = pl.pallas_call(
        forward_kernel,
        out_shape=units_shape(devices),
        in_specs=[SMEM] * 2 + [VMEM],
        out_specs=VMEM,
        compiler_params=PARAMS,
        cost_estimate=cost(3),
        name="forward",
    )(me_ref, column, first)
    second = exchange(second)

    size = species * rows
    edge_shapes = [jax.ShapeDtypeStruct((species * planes, lanes), f32)] * 2
    xedge_shapes = [jax.ShapeDtypeStruct((size, lanes), f32)] * 2
    state_shape = jax.ShapeDtypeStruct((planes * size, lanes), f32)
    state, ylow, yhigh = pl.pallas_call(
        functools.partial(build_kernel, old_fine.shape),
        out_shape=[state_shape] + edge_shapes,
        in_specs=[SMEM] * 2 + [VMEM],
        out_specs=[VMEM] * 3,
        compiler_params=PARAMS,
        cost_estimate=cost(10),
        name="build",
    )(fine_at, coarse_at, first)
    plane_shape = jax.ShapeDtypeStruct((species, rows, lanes), f32)
    state, ylow, yhigh, xlow, xhigh = pl.pallas_call(
        build_late_kernel,
        out_shape=[jax.ShapeDtypeStruct(old_fine.shape, f32)] + edge_shapes + [plane_shape] * 2,
        in_specs=[SMEM] * 5 + [VMEM, ANY, ANY] + [VMEM] * 2,
        out_specs=[ANY] + [VMEM] * 4,
        scratch_shapes=[
            pltpu.VMEM((1, species, half, lanes), f32),
            pltpu.VMEM((species, rows, lanes), f32),
            pltpu.SemaphoreType.DMA,
            pltpu.SemaphoreType.DMA((2 * planes,)),
        ],
        input_output_aliases={7: 0},
        compiler_params=PARAMS,
        cost_estimate=cost(4),
        name="build_late",
    )(me_ref, column, left, fine_at, coarse_at, second, rest, state.reshape(old_fine.shape), ylow, yhigh)
    state = state.reshape(state_shape.shape)
    edges = [ylow, yhigh, xlow.reshape(size, lanes), xhigh.reshape(size, lanes)]

    for repeat in range(ITERS):
        last = repeat == ITERS - 1
        state = pl.pallas_call(
            functools.partial(last_step_kernel if last else step_kernel, old_fine.shape),
            out_shape=[state_shape] + ([] if last else edge_shapes + xedge_shapes),
            in_specs=[SMEM] + [VMEM] * 6,
            out_specs=[ANY] if last else [VMEM] * 5,
            scratch_shapes=[
                pltpu.VMEM(state_shape.shape, f32), pltpu.SemaphoreType.DMA((planes // UNROLL,))
            ] if last else [],
            compiler_params=PARAMS,
            cost_estimate=cost(10),
            name="last_step" if last else "step",
        )(diffusion, state, velocity, *halo(*edges))
        state, *edges = state
    return state.reshape(old_fine.shape)


def solution(mesh):
    in_specs = (
        P("dev", None, "grp", None),
        P("grp", "dev"),
        P("dev", None, "grp", None),
        P("grp", "dev"),
        P("dev", None, "grp", None),
        P(),
    )
    out_specs = P("dev", None, "grp", None)
    return jax.shard_map(
        on_device, mesh=mesh, in_specs=in_specs, out_specs=out_specs, check_vma=False
    )
```

```python
import functools

import jax
import jax.numpy as jnp
from jax import lax
from jax.experimental import pallas as pl
from jax.experimental.pallas import tpu as pltpu
from jax.sharding import PartitionSpec as P

ITERS = 2
FINE_CAP = 4
COARSE_CAP = 2
DIRECT = 5
EXTRA = 2 * FINE_CAP + 1 - DIRECT
VMEM = pl.BlockSpec(memory_space=pltpu.VMEM)
SMEM = pl.BlockSpec(memory_space=pltpu.SMEM)
ANY = pl.BlockSpec(memory_space=pl.ANY)
PARAMS = pltpu.CompilerParams(vmem_limit_bytes=56 * 1024 * 1024)
UNROLL = 4


def ranks(boxes):
    count = boxes.shape[-1]
    earlier = jnp.arange(count)[None, :] < jnp.arange(count)[:, None]
    same = boxes[..., None, :] == boxes[..., :, None]
    return jnp.sum((same & earlier).astype(jnp.int32), axis=-1)


def plan_kernel(me_ref, units_ref, row_ref, column_ref):
    devices, lanes = units_ref.shape
    me = me_ref[0]
    units = units_ref[...]
    source = lax.broadcasted_iota(jnp.int32, units.shape, 0)
    lane = lax.broadcasted_iota(jnp.int32, units.shape, 1)
    surplus = pltpu.roll(jnp.maximum(units - DIRECT, 0), 0, 1, stride=1, stride_axis=0)
    none = jnp.full(units.shape, -1, jnp.int32)

    def one_round(r, carry):
        left, free, second, through, *chosen = carry
        ok = (left > 0) & (free > 0) & (second > 0)
        position = DIRECT - free
        item = surplus - left
        chosen = [jnp.where(ok & (item == i), r * 8 + position, table) for i, table in enumerate(chosen)]
        through = jnp.where(ok, source * 8 + position, through)
        used = ok.astype(jnp.int32)
        left, free, second = left - used, free - used, second - used
        free = pltpu.roll(free, lanes - 1, 1)
        second = pltpu.roll(pltpu.roll(second, devices - 1, 0), lanes - 1, 1)
        through = pltpu.roll(pltpu.roll(through, devices - 1, 0), lanes - 1, 1)
        return (left, free, second, through, *chosen)

    init = (surplus, jnp.maximum(DIRECT - units, 0), jnp.ones(units.shape, jnp.int32), none) + (none,) * EXTRA
    left, _, _, through, *chosen = lax.fori_loop(0, devices, one_round, init)
    for i in range(EXTRA):
        row_ref[i : i + 1] = jnp.max(jnp.where(source == me, chosen[i], -1), axis=0, keepdims=True)
    row_ref[EXTRA : EXTRA + 1] = jnp.max(left, axis=0, keepdims=True)
    column = none
    for i in range(EXTRA):
        mine = (lane < devices) & (lane == (source + me) % devices)
        found = jnp.max(jnp.where(mine, chosen[i], -1), axis=1, keepdims=True)
        column = jnp.where(lane == i, found, column)
    found = jnp.max(jnp.where(lane == me, through, -1), axis=1, keepdims=True)
    column_ref[...] = jnp.where(lane == EXTRA, found, column)


def pack_kernel(devices, slot_of, me_ref, fine_at_ref, coarse_at_ref, row_ref, fine_ref, coarse_ref, out_ref):
    planes = fine_ref.shape[0]
    coarse_planes, _, half, depth = coarse_ref.shape

    def fine_plane(k, carry):
        code = fine_at_ref[k]

        @pl.when(code >= 0)
        def _():
            for h in range(2):
                slot = slot_of(me_ref[0], row_ref, code // FINE_CAP, 2 * (code % FINE_CAP) + h)

                @pl.when(slot >= 0)
                def _():
                    out_ref[slot] = fine_ref[k, :, h * half : (h + 1) * half, :]

        return carry

    lax.fori_loop(0, planes, fine_plane, 0)

    def coarse_plane(k, carry):
        code = coarse_at_ref[k]

        @pl.when(code >= 0)
        def _():
            at = code // 2
            slot = slot_of(me_ref[0], row_ref, at // (DIRECT + EXTRA), at % (DIRECT + EXTRA))
            for j in range(2):

                @pl.when((slot >= 0) & (code % 2 == j))
                def _():
                    out_ref[slot, :, :, j * depth : (j + 1) * depth] = coarse_ref[k]

        return carry

    lax.fori_loop(0, coarse_planes, coarse_plane, 0)


def first_slot(devices, me, row_ref, box, unit):
    t = (me + box) % devices
    code = row_ref[jnp.maximum(unit - DIRECT, 0), t]
    relay = jnp.where(code >= 0, ((t + code // 8) % devices) * DIRECT + code % 8, -1)
    return jnp.where(unit < DIRECT, box * DIRECT + unit, relay)


def direct_slot(me, row_ref, box, unit):
    return jnp.where(unit < DIRECT, -1, box * EXTRA + unit - DIRECT)


def forward_kernel(me_ref, column_ref, in_ref, out_ref):
    devices = out_ref.shape[0]

    def body(a, carry):
        code = column_ref[a, EXTRA]

        @pl.when(code >= 0)
        def _():
            out_ref[(me_ref[0] - a + devices) % devices] = in_ref[(code // 8) * DIRECT + code % 8]

        return carry

    lax.fori_loop(0, devices, body, 0)


def rows_to_edges(flat_ref, edge_ref, offset, row, planes, species, rows):
    for s in range(species):
        for x in range(0, planes, 8):
            at = offset + s * planes + x
            edge_ref[at : at + 8] = flat_ref[pl.ds((x * species + s) * rows + row, 8, stride=species * rows), :]


def interpolate(ref, slot, part, store):
    _, species, half, lanes = ref.shape
    lane = lax.broadcasted_iota(jnp.int32, (half, lanes), 1)
    row = lax.broadcasted_iota(jnp.int32, (half, lanes), 0)
    sign = jnp.where(lane % 2 == 0, -0.25, 0.25)
    lane_first = lane % (lanes // 2) == 0
    lane_last = lane % (lanes // 2) == lanes // 2 - 1
    index = part * (lanes // 2) + lane // 2
    for s in range(species):
        p = ref[slot, s]
        below = jnp.where(row == 0, p, pltpu.roll(p, 1, 0))
        above = jnp.where(row == half - 1, p, pltpu.roll(p, half - 1, 0))
        left = jnp.where(lane_first, p, pltpu.roll(p, 1, 1))
        right = jnp.where(lane_last, p, pltpu.roll(p, lanes - 1, 1))
        slope_y = 0.125 * (above - below)
        slope_z = 0.5 * (right - left)
        gz = jnp.take_along_axis(slope_z, index, axis=1) * sign
        even = jnp.take_along_axis(p - slope_y, index, axis=1) + gz
        odd = jnp.take_along_axis(p + slope_y, index, axis=1) + gz
        store(s, even, odd)


def build_kernel(shape, fine_at_ref, coarse_at_ref, first_ref, out_ref, ylow_ref, yhigh_ref, xlow_ref, xhigh_ref):
    planes, species, rows, lanes = shape
    half = rows // 2

    def body(c, carry):
        at = [fine_at_ref[2 * c], fine_at_ref[2 * c + 1]]
        code = coarse_at_ref[c]
        unit = code // 2 % (DIRECT + EXTRA)

        @pl.when(((at[0] < 0) | (at[1] < 0)) & (unit < DIRECT))
        def _():
            def store(s, even, odd):
                for child in range(2):
                    base = pl.multiple_of(((2 * c + child) * species + s) * rows, rows)
                    out_ref[pl.ds(base, half, stride=2), :] = even
                    out_ref[pl.ds(base + 1, half, stride=2), :] = odd

            interpolate(first_ref, code // 2 // (DIRECT + EXTRA) * DIRECT + unit, code % 2, store)

        for child in range(2):
            for h in range(2):
                late = 2 * (at[child] % FINE_CAP) + h

                @pl.when((at[child] >= 0) & (late < DIRECT))
                def _():
                    slot = at[child] // FINE_CAP * DIRECT + late
                    for s in range(species):
                        base = pl.multiple_of(((2 * c + child) * species + s) * rows + h * half, half)
                        out_ref[pl.ds(base, half), :] = first_ref[slot, s]

        return carry

    lax.fori_loop(0, planes // 2, body, 0)
    for r in range(ITERS):
        rows_to_edges(out_ref, ylow_ref, r * species * planes, r, planes, species, rows)
        rows_to_edges(out_ref, yhigh_ref, r * species * planes, rows - ITERS + r, planes, species, rows)
    deep = ITERS * species * rows
    xlow_ref[...] = out_ref[0:deep]
    xhigh_ref[...] = out_ref[planes * species * rows - deep : planes * species * rows]


def late_units(shape, me_ref, column_ref, left_ref, fine_at_ref, coarse_at_ref, second_ref, rest_ref, held_ref,
               plane_ref, sem, half_plane, whole_plane):
    planes, _, rows, _ = shape
    half = rows // 2
    devices = column_ref.shape[0]
    planned = left_ref[0] == 0

    def relayed(source, unit):
        return (source + me_ref[0] + column_ref[source, jnp.maximum(unit - DIRECT, 0)] // 8) % devices

    def bring(source, unit):
        copy = pltpu.make_async_copy(
            rest_ref.at[pl.ds(source * EXTRA + jnp.maximum(unit - DIRECT, 0), 1)], held_ref, sem
        )
        copy.start()
        copy.wait()

    def parent(c, carry):
        at = [fine_at_ref[2 * c], fine_at_ref[2 * c + 1]]
        code = coarse_at_ref[c]
        unit = code // 2 % (DIRECT + EXTRA)
        source = code // 2 // (DIRECT + EXTRA)

        @pl.when(((at[0] < 0) | (at[1] < 0)) & (unit >= DIRECT))
        def _():
            def store(s, even, odd):
                plane_ref[s, pl.ds(0, half, stride=2), :] = even
                plane_ref[s, pl.ds(1, half, stride=2), :] = odd

            @pl.when(planned)
            def _():
                held_ref[0] = second_ref[relayed(source, unit)]

            @pl.when(jnp.logical_not(planned))
            def _():
                bring(source, unit)

            interpolate(held_ref, 0, code % 2, store)
            for child in range(2):

                @pl.when(at[child] < 0)
                def _():
                    whole_plane(2 * c + child)

        return carry

    lax.fori_loop(0, planes // 2, parent, 0)

    def plane(x, carry):
        at = fine_at_ref[x]

        @pl.when((at >= 0) & (2 * (at % FINE_CAP) + 1 >= DIRECT))
        def _():
            for h in range(2):
                unit = 2 * (at % FINE_CAP) + h

                @pl.when((unit >= DIRECT) & planned)
                def _():
                    half_plane(x, h, second_ref, relayed(at // FINE_CAP, unit))

                @pl.when((unit >= DIRECT) & jnp.logical_not(planned))
                def _():
                    bring(at // FINE_CAP, unit)
                    half_plane(x, h, held_ref, 0)

        return carry

    lax.fori_loop(0, planes, plane, 0)


def edges_kernel(
    shape, me_ref, column_ref, left_ref, fine_at_ref, coarse_at_ref, second_ref, rest_ref,
    ylow_in_ref, yhigh_in_ref, xlow_in_ref, xhigh_in_ref,
    ylow_ref, yhigh_ref, xlow_ref, xhigh_ref, held_ref, plane_ref, sem,
):
    planes, species, rows, _ = shape
    half = rows // 2
    size = species * rows
    ylow_ref[...] = ylow_in_ref[...]
    yhigh_ref[...] = yhigh_in_ref[...]
    xlow_ref[...] = xlow_in_ref[...]
    xhigh_ref[...] = xhigh_in_ref[...]

    def half_edges(x, h, value):
        edge_ref, first = ((ylow_ref, 0), (yhigh_ref, half - ITERS))[h]
        for s in range(species):
            for r in range(ITERS):
                edge_ref[pl.ds((r * species + s) * planes + x, 1), :] = value(s, slice(first + r, first + r + 1))
        for near, xedge_ref, at in ((x < ITERS, xlow_ref, x), (x >= planes - ITERS, xhigh_ref, x - planes + ITERS)):

            @pl.when(near)
            def _():
                for s in range(species):
                    base = pl.multiple_of(at * size + s * rows + h * half, half)
                    xedge_ref[pl.ds(base, half), :] = value(s, slice(0, half))

    def half_plane(x, h, ref, slot):
        half_edges(x, h, lambda s, part: ref[slot, s, part])

    def whole_plane(x):
        for h in range(2):
            half_edges(x, h, lambda s, part: plane_ref[s, h * half + part.start : h * half + part.stop])

    late_units(
        shape, me_ref, column_ref, left_ref, fine_at_ref, coarse_at_ref, second_ref, rest_ref, held_ref, plane_ref,
        sem, half_plane, whole_plane,
    )


def corners_kernel(planes, species, ylow_ref, yhigh_ref, xlow_ref, xhigh_ref, down_ref, up_ref):
    deep = xlow_ref.shape[0]
    down_ref[0:deep] = xlow_ref[...]
    up_ref[0:deep] = xhigh_ref[...]
    for message_ref, x in ((down_ref, 0), (up_ref, planes - 1)):
        for s in range(species):
            low = ((ITERS - 1) * species + s) * planes + x
            high = s * planes + x
            message_ref[deep + s : deep + s + 1] = ylow_ref[low : low + 1]
            message_ref[deep + 16 + s : deep + 16 + s + 1] = yhigh_ref[high : high + 1]
        for at in (deep + species, deep + 16 + species):
            message_ref[at : at + 16 - species] = jnp.zeros((16 - species, message_ref.shape[1]), jnp.float32)


def velocity_edges_kernel(vel_ref, ylow_ref, yhigh_ref, xlow_ref, xhigh_ref, *, shape):
    planes, directions, rows, _ = shape
    size = directions * rows
    rows_to_edges(vel_ref, ylow_ref, 0, 0, planes, directions, rows)
    rows_to_edges(vel_ref, yhigh_ref, 0, rows - 1, planes, directions, rows)
    xlow_ref[...] = vel_ref[0:size]
    xhigh_ref[...] = vel_ref[(planes - 1) * size : planes * size]


class Flow:
    def __init__(self, velocity):
        self.positive = [jnp.maximum(v, 0.0) for v in velocity]
        self.negative = [jnp.minimum(v, 0.0) for v in velocity]
        self.keep = 1.0
        for low, high in zip(self.positive, self.negative):
            self.keep = self.keep - (low - high)

    def step(self, u, neighbours, d):
        new = u * (self.keep - 6.0 * d)
        for k, (low, high) in enumerate(neighbours):
            new = new + low * (d + self.positive[k]) + high * (d - self.negative[k])
        return new


def steps_kernel(
    shape, me_ref, column_ref, left_ref, fine_at_ref, coarse_at_ref, inside_ref, diff_ref, second_ref, rest_ref, state_ref,
    vel_ref, ylow_own_ref, yhigh_own_ref, ylow_ref, yhigh_ref, xlow_ref, xhigh_ref, vylow_ref, vyhigh_ref, vxlow_ref,
    vxhigh_ref, out_ref, u0_ref, u1_ref, row_low_ref, row_high_ref, plane_low_ref, plane_high_ref, held_ref, plane_ref, sem,
    out_sem,
):
    planes, species, rows, lanes = shape
    half = rows // 2
    size = species * rows
    copy = pltpu.make_async_copy(state_ref, u0_ref, sem)
    copy.start()
    copy.wait()

    def half_plane(x, h, ref, slot):
        for s in range(species):
            base = pl.multiple_of(x * size + s * rows + h * half, half)
            u0_ref[pl.ds(base, half), :] = ref[slot, s]

    def whole_plane(x):
        for s in range(species):
            u0_ref[pl.ds(pl.multiple_of(x * size + s * rows, rows), rows), :] = plane_ref[s]

    late_units(
        shape, me_ref, column_ref, left_ref, fine_at_ref, coarse_at_ref, second_ref, rest_ref, held_ref, plane_ref,
        sem, half_plane, whole_plane,
    )

    def along(u, first, last, dim):
        count = u.shape[dim]
        at = lax.broadcasted_iota(jnp.int32, u.shape, dim)
        low = jnp.where(at == 0, first, pltpu.roll(u, 1, dim))
        high = jnp.where(at == count - 1, last, pltpu.roll(u, count - 1, dim))
        return low, high

    deep = ITERS * size
    for (near_ref, near, far, own_ref, own, v_ref, corner, target_ref, inside) in (
        (ylow_ref, 1, 0, ylow_own_ref, 0, vylow_ref, deep, row_low_ref, 0),
        (yhigh_ref, 0, 1, yhigh_own_ref, 1, vyhigh_ref, deep + 16, row_high_ref, 1),
    ):
        for x in range(0, planes, 16):
            flow = Flow([v_ref[k * planes + x : k * planes + x + 16] for k in range(3)])
            for s in range(species):

                def band(ref, r):
                    start = (r * species + s) * planes + x
                    return ref[start : start + 16]

                u = band(near_ref, near)
                start = (near * species + s) * planes
                if x == 0:
                    first = xlow_ref[corner + s : corner + s + 1]
                else:
                    first = near_ref[start + x - 1 : start + x]
                if x + 16 == planes:
                    last = xhigh_ref[corner + s : corner + s + 1]
                else:
                    last = near_ref[start + x + 16 : start + x + 17]
                outer, inner = band(near_ref, far), band(own_ref, own)
                across = (outer, inner) if inside == 0 else (inner, outer)
                new = flow.step(u, (along(u, first, last, 0), across, along(u, u, u, 1)), diff_ref[s])
                target_ref[s * planes + x : s * planes + x + 16] = new * inside_ref[inside]

    def at(ref, x):
        return lambda s: ref[pl.ds(pl.multiple_of(x * size + s * rows, rows), rows), :]

    def edge(ref, offset, x):
        return lambda s: ref[pl.ds(offset + s * planes + x, 1), :]

    def plane(velocity, center, below, above, y_low, y_high, store):
        flow = Flow(velocity)
        for s in range(species):
            u = center(s)
            sides = ((below(s), above(s)), along(u, y_low(s), y_high(s), 0), along(u, u, u, 1))
            store(s, flow.step(u, sides, diff_ref[s]))

    for (halo_ref, near, below, above, v_ref, target_ref, inside) in (
        (xlow_ref, 1, at(xlow_ref, 0), at(u0_ref, 0), vxlow_ref, plane_low_ref, 2),
        (xhigh_ref, 0, at(u0_ref, planes - 1), at(xhigh_ref, 1), vxhigh_ref, plane_high_ref, 3),
    ):

        def store(s, new):
            target_ref[s * rows : (s + 1) * rows] = new * inside_ref[inside]

        def corner(offset):
            return lambda s: halo_ref[deep + offset + s : deep + offset + s + 1]

        velocity = [v_ref[k * rows : (k + 1) * rows] for k in range(3)]
        plane(velocity, at(halo_ref, near), below, above, corner(0), corner(16), store)

    def advance(u_ref, new_ref, low, high, y_low, y_high, after):
        def group(x, first, last):
            for i in range(UNROLL):

                def store(s, new):
                    new_ref[pl.ds(pl.multiple_of((x + i) * size + s * rows, rows), rows), :] = new

                plane(
                    [vel_ref[x + i, k] for k in range(3)],
                    at(u_ref, x + i),
                    low if first and i == 0 else at(u_ref, x + i - 1),
                    high if last and i == UNROLL - 1 else at(u_ref, x + i + 1),
                    edge(*y_low, x + i),
                    edge(*y_high, x + i),
                    store,
                )
            after(x // UNROLL)

        def body(g, carry):
            group(g * UNROLL, False, False)
            return carry

        group(0, True, False)
        lax.fori_loop(1, planes // UNROLL - 1, body, 0)
        group(planes - UNROLL, False, True)

    def send(g):
        part = pl.ds(pl.multiple_of(g * UNROLL * size, UNROLL * size), UNROLL * size)
        return pltpu.make_async_copy(u0_ref.at[part], out_ref.at[part], out_sem.at[g])

    advance(
        u0_ref, u1_ref, at(xlow_ref, 1), at(xhigh_ref, 0), (ylow_ref, species * planes), (yhigh_ref, 0), lambda g: None
    )
    advance(
        u1_ref, u0_ref, at(plane_low_ref, 0), at(plane_high_ref, 0), (row_low_ref, 0), (row_high_ref, 0),
        lambda g: send(g).start(),
    )

    def finish(g, carry):
        send(g).wait()
        return carry

    lax.fori_loop(0, planes // UNROLL, finish, 0)


def empty_kernel(out_ref):
    pass


def cost(microseconds):
    return pl.CostEstimate(flops=0, bytes_accessed=int(microseconds * 3.6e6), transcendentals=0)


def neighbours(axis, low, high):
    size = lax.axis_size(axis)
    up = [(i, (i + 1) % size) for i in range(size - 1)]
    return lax.ppermute(high, axis, up), lax.ppermute(low, axis, [(b, a) for a, b in up])


def on_device(old_fine, old_ids, old_coarse, coarse_ids, velocity, diffusion):
    devices = lax.axis_size("dev")
    me = lax.axis_index("dev")
    me_ref = me.reshape(1).astype(jnp.int32)
    planes, species, rows, lanes = old_fine.shape
    half = rows // 2
    coarse_planes = old_coarse.shape[0]
    unit_count = DIRECT + EXTRA
    f32 = jnp.float32
    i32 = jnp.int32

    def units_shape(count):
        return jax.ShapeDtypeStruct((count, species, half, lanes), f32)

    own, own_coarse = old_ids[0], coarse_ids[0]
    labels = jnp.broadcast_to(jnp.concatenate([own, own_coarse])[None], (devices, planes + coarse_planes))
    labels = lax.all_to_all(labels, "dev", split_axis=0, concat_axis=0, tiled=True)
    all_ids, all_coarse = labels[:, :planes], labels[:, planes:]
    all_box = jnp.where(all_ids >= 0, all_ids // planes, -1)
    all_coarse_box = all_coarse // coarse_planes
    flat_parents = jnp.where(all_ids >= 0, all_ids // 2, -1).reshape(-1)

    def needed(coarse):
        kept = jnp.sum((flat_parents == coarse[..., None]).astype(i32), axis=-1)
        return kept < 2

    box = jnp.arange(lanes) % devices
    fine_units = jnp.sum((all_box[:, None, :] == box[None, :, None]).astype(i32), axis=-1)
    asked = needed(all_coarse)[:, None, :] & (all_coarse_box[:, None, :] == box[None, :, None])
    units = 2 * fine_units + jnp.max(asked.astype(i32), axis=-1)
    row, column = pl.pallas_call(
        plan_kernel,
        out_shape=[jax.ShapeDtypeStruct((8, lanes), i32), jax.ShapeDtypeStruct((devices, lanes), i32)],
        in_specs=[SMEM, VMEM],
        out_specs=[VMEM] * 2,
        name="plan",
    )(me_ref, units)
    left = jnp.max(row[EXTRA, :devices]).reshape(1)

    own_box = jnp.where(own >= 0, own // planes, -1)
    send_fine = jnp.where(own >= 0, own_box * FINE_CAP + ranks(own_box), -1)
    own_coarse_box = own_coarse // coarse_planes
    before = jnp.sum((own_box[None, :] == own_coarse_box[:, None]).astype(i32), axis=1)
    send_coarse = (own_coarse_box * unit_count + 2 * before) * 2 + ranks(own_coarse_box)
    send_coarse = jnp.where(needed(own_coarse), send_coarse, -1)

    order = jnp.arange(devices)[:, None]
    wanted = me * planes + jnp.arange(planes)
    fine_at = jnp.where(all_ids[None] == wanted[:, None, None], (order * FINE_CAP + ranks(all_box))[None], -1)
    fine_at = jnp.max(fine_at, axis=(1, 2))
    to_me = jnp.sum((all_box == me).astype(i32), axis=1, keepdims=True)
    coarse_wanted = me * coarse_planes + jnp.arange(coarse_planes)
    coarse_code = (order * unit_count + 2 * to_me) * 2 + ranks(all_coarse_box)
    coarse_at = jnp.where(all_coarse[None] == coarse_wanted[:, None, None], coarse_code[None], 0)
    coarse_at = jnp.max(coarse_at, axis=(1, 2))

    def exchange(value):
        return lax.all_to_all(value, "dev", split_axis=0, concat_axis=0, tiled=True)

    def pack(count, slot_of, name):
        return pl.pallas_call(
            functools.partial(pack_kernel, devices, slot_of),
            out_shape=units_shape(count),
            in_specs=[SMEM] * 4 + [VMEM] * 2,
            out_specs=VMEM,
            compiler_params=PARAMS,
            name=name,
        )(me_ref, send_fine, send_coarse, row, old_fine, old_coarse)

    packed = pack(devices * DIRECT, functools.partial(first_slot, devices), "pack")

    def no_rest():
        return pl.pallas_call(empty_kernel, out_shape=units_shape(devices * EXTRA), out_specs=ANY, name="nothing")()

    def rest_direct():
        return exchange(pack(devices * EXTRA, direct_slot, "pack_rest"))

    rest = lax.cond(left[0] == 0, no_rest, rest_direct)
    packed, rest, flow = lax.optimization_barrier((packed, rest, velocity))
    first = exchange(packed)

    def edge_shapes(deep, count):
        along_y = jax.ShapeDtypeStruct((deep * count * planes, lanes), f32)
        along_x = jax.ShapeDtypeStruct((deep * count * rows, lanes), f32)
        return [along_y, along_y, along_x, along_x]

    directions = flow.shape[1]
    vylow, vyhigh, vxlow, vxhigh = pl.pallas_call(
        functools.partial(velocity_edges_kernel, shape=flow.shape),
        out_shape=edge_shapes(1, directions),
        in_specs=[VMEM],
        out_specs=[VMEM] * 4,
        compiler_params=PARAMS,
        name="velocity_edges",
    )(flow.reshape(planes * directions * rows, lanes))
    flow_edges = [*neighbours("grp", vylow, vyhigh), *neighbours("dev", vxlow, vxhigh)]
    first, *flow_edges = lax.optimization_barrier((first, *flow_edges))
    second = pl.pallas_call(
        forward_kernel,
        out_shape=units_shape(devices),
        in_specs=[SMEM] * 2 + [VMEM],
        out_specs=VMEM,
        compiler_params=PARAMS,
        cost_estimate=cost(3),
        name="forward",
    )(me_ref, column, first)
    second = exchange(second)

    size = species * rows
    state_shape = jax.ShapeDtypeStruct((planes * size, lanes), f32)
    state, *edges = pl.pallas_call(
        functools.partial(build_kernel, old_fine.shape),
        out_shape=[state_shape] + edge_shapes(ITERS, species),
        in_specs=[SMEM] * 2 + [VMEM],
        out_specs=[VMEM] * 5,
        compiler_params=PARAMS,
        cost_estimate=cost(10),
        name="build",
    )(fine_at, coarse_at, first)
    late_scratch = [
        pltpu.VMEM((1, species, half, lanes), f32),
        pltpu.VMEM((species, rows, lanes), f32),
        pltpu.SemaphoreType.DMA,
    ]
    ylow_own, yhigh_own, xlow_own, xhigh_own = pl.pallas_call(
        functools.partial(edges_kernel, old_fine.shape),
        out_shape=edge_shapes(ITERS, species),
        in_specs=[SMEM] * 5 + [VMEM, ANY] + [VMEM] * 4,
        out_specs=[VMEM] * 4,
        scratch_shapes=late_scratch,
        compiler_params=PARAMS,
        cost_estimate=cost(4),
        name="edges",
    )(me_ref, column, left, fine_at, coarse_at, second, rest, *edges)
    ylow, yhigh = neighbours("grp", ylow_own, yhigh_own)
    message = jax.ShapeDtypeStruct((ITERS * size + 32, lanes), f32)
    down, up = pl.pallas_call(
        functools.partial(corners_kernel, planes, species),
        out_shape=[message] * 2,
        in_specs=[VMEM] * 4,
        out_specs=[VMEM] * 2,
        compiler_params=PARAMS,
        name="corners",
    )(ylow, yhigh, xlow_own, xhigh_own)
    xlow, xhigh = neighbours("dev", down, up)
    grp, dev = lax.axis_index("grp"), lax.axis_index("dev")
    inside = jnp.stack([grp > 0, grp < lax.axis_size("grp") - 1, dev > 0, dev < devices - 1]).astype(f32)
    row_edge = pltpu.VMEM((species * planes, lanes), f32)
    plane_edge = pltpu.VMEM((size, lanes), f32)
    done = pl.pallas_call(
        functools.partial(steps_kernel, old_fine.shape),
        out_shape=state_shape,
        in_specs=[SMEM] * 7 + [VMEM, ANY, ANY] + [VMEM] * 11,
        out_specs=ANY,
        scratch_shapes=[pltpu.VMEM(state_shape.shape, f32)] * 2
        + [row_edge] * 2
        + [plane_edge] * 2
        + late_scratch
        + [pltpu.SemaphoreType.DMA((planes // UNROLL,))],
        compiler_params=PARAMS,
        name="steps",
    )(
        me_ref, column, left, fine_at, coarse_at, inside, diffusion, second, rest, state, velocity,
        ylow_own, yhigh_own, ylow, yhigh, xlow, xhigh, *flow_edges,
    )
    return done.reshape(old_fine.shape)


def solution(mesh):
    in_specs = (
        P("dev", None, "grp", None),
        P("grp", "dev"),
        P("dev", None, "grp", None),
        P("grp", "dev"),
        P("dev", None, "grp", None),
        P(),
    )
    out_specs = P("dev", None, "grp", None)
    return jax.shard_map(
        on_device, mesh=mesh, in_specs=in_specs, out_specs=out_specs, check_vma=False
    )
```

```python
import functools

import jax
import jax.numpy as jnp
from jax import lax
from jax.experimental import pallas as pl
from jax.experimental.pallas import tpu as pltpu
from jax.sharding import PartitionSpec as P

ITERS = 2
FINE_CAP = 4
COARSE_CAP = 2
DIRECT = 5
EXTRA = 2 * FINE_CAP + 1 - DIRECT
VMEM = pl.BlockSpec(memory_space=pltpu.VMEM)
SMEM = pl.BlockSpec(memory_space=pltpu.SMEM)
ANY = pl.BlockSpec(memory_space=pl.ANY)
PARAMS = pltpu.CompilerParams(vmem_limit_bytes=56 * 1024 * 1024)
UNROLL = 4


def ranks(boxes):
    count = boxes.shape[-1]
    earlier = jnp.arange(count)[None, :] < jnp.arange(count)[:, None]
    same = boxes[..., None, :] == boxes[..., :, None]
    return jnp.sum((same & earlier).astype(jnp.int32), axis=-1)


def plan_kernel(me_ref, units_ref, row_ref, column_ref):
    devices, lanes = units_ref.shape
    me = me_ref[0]
    units = units_ref[...]
    source = lax.broadcasted_iota(jnp.int32, units.shape, 0)
    lane = lax.broadcasted_iota(jnp.int32, units.shape, 1)
    surplus = pltpu.roll(jnp.maximum(units - DIRECT, 0), 0, 1, stride=1, stride_axis=0)
    none = jnp.full(units.shape, -1, jnp.int32)

    def one_round(r, carry):
        left, free, second, through, *chosen = carry
        ok = (left > 0) & (free > 0) & (second > 0)
        position = DIRECT - free
        item = surplus - left
        chosen = [jnp.where(ok & (item == i), r * 8 + position, table) for i, table in enumerate(chosen)]
        through = jnp.where(ok, source * 8 + position, through)
        used = ok.astype(jnp.int32)
        left, free, second = left - used, free - used, second - used
        free = pltpu.roll(free, lanes - 1, 1)
        second = pltpu.roll(pltpu.roll(second, devices - 1, 0), lanes - 1, 1)
        through = pltpu.roll(pltpu.roll(through, devices - 1, 0), lanes - 1, 1)
        return (left, free, second, through, *chosen)

    init = (surplus, jnp.maximum(DIRECT - units, 0), jnp.ones(units.shape, jnp.int32), none) + (none,) * EXTRA
    left, _, _, through, *chosen = lax.fori_loop(0, devices, one_round, init)
    for i in range(EXTRA):
        row_ref[i : i + 1] = jnp.max(jnp.where(source == me, chosen[i], -1), axis=0, keepdims=True)
    row_ref[EXTRA : EXTRA + 1] = jnp.max(left, axis=0, keepdims=True)
    column = none
    for i in range(EXTRA):
        mine = (lane < devices) & (lane == (source + me) % devices)
        found = jnp.max(jnp.where(mine, chosen[i], -1), axis=1, keepdims=True)
        column = jnp.where(lane == i, found, column)
    found = jnp.max(jnp.where(lane == me, through, -1), axis=1, keepdims=True)
    column_ref[...] = jnp.where(lane == EXTRA, found, column)


def pack_kernel(
    devices, first, me_ref, fine_at_ref, coarse_at_ref, row_ref, fine_in_ref, coarse_ref, out_ref, fine_ref, sem
):
    planes = fine_ref.shape[0]
    coarse_planes, _, half, depth = coarse_ref.shape
    part = planes // sem.shape[0]

    def bring(i):
        planes_of = pl.ds(i * part, part)
        return pltpu.make_async_copy(fine_in_ref.at[planes_of], fine_ref.at[planes_of], sem.at[i])

    def slot_of(box, unit):
        if first:
            return first_slot(devices, me_ref[0], row_ref, box, unit)
        return jnp.where(unit < DIRECT, -1, box * EXTRA + unit - DIRECT)

    for i in range(sem.shape[0]):
        bring(i).start()

    def coarse_plane(k, carry):
        code = coarse_at_ref[k]

        @pl.when(code >= 0)
        def _():
            at = code // 2
            slot = slot_of(at // (DIRECT + EXTRA), at % (DIRECT + EXTRA))
            for j in range(2):

                @pl.when((slot >= 0) & (code % 2 == j))
                def _():
                    out_ref[slot, :, :, j * depth : (j + 1) * depth] = coarse_ref[k]

        return carry

    lax.fori_loop(0, coarse_planes, coarse_plane, 0)

    def fine_plane(k, carry):
        code = fine_at_ref[k]
        box, rank = code // FINE_CAP, code % FINE_CAP
        whole = DIRECT // 2

        if first:

            @pl.when((code >= 0) & (rank < whole))
            def _():
                for h in range(2):
                    out_ref[box * DIRECT + 2 * rank + h] = fine_ref[k, :, h * half : (h + 1) * half, :]

        @pl.when((code >= 0) & (rank >= whole))
        def _():
            for h in range(2):
                slot = slot_of(box, 2 * rank + h)

                @pl.when(slot >= 0)
                def _():
                    out_ref[slot] = fine_ref[k, :, h * half : (h + 1) * half, :]

        return carry

    for i in range(sem.shape[0]):
        bring(i).wait()
        lax.fori_loop(i * part, (i + 1) * part, fine_plane, 0)


def first_slot(devices, me, row_ref, box, unit):
    t = (me + box) % devices
    code = row_ref[jnp.maximum(unit - DIRECT, 0), t]
    relay = jnp.where(code >= 0, ((t + code // 8) % devices) * DIRECT + code % 8, -1)
    return jnp.where(unit < DIRECT, box * DIRECT + unit, relay)


def forward_kernel(me_ref, column_ref, in_ref, out_ref, sem):
    devices = out_ref.shape[0]

    def each(act):
        def body(a, carry):
            code = column_ref[a, EXTRA]

            @pl.when(code >= 0)
            def _():
                box = (me_ref[0] - a + devices) % devices
                act(pltpu.make_async_copy(in_ref.at[(code // 8) * DIRECT + code % 8], out_ref.at[box], sem.at[a]))

            return carry

        lax.fori_loop(0, devices, body, 0)

    each(lambda copy: copy.start())
    each(lambda copy: copy.wait())


def rows_to_edges(flat_ref, edge_ref, offset, row, planes, species, rows):
    for s in range(species):
        for x in range(0, planes, 8):
            at = offset + s * planes + x
            edge_ref[at : at + 8] = flat_ref[pl.ds((x * species + s) * rows + row, 8, stride=species * rows), :]


def interpolate(ref, slot, part, store):
    _, species, half, lanes = ref.shape
    lane = lax.broadcasted_iota(jnp.int32, (half, lanes), 1)
    row = lax.broadcasted_iota(jnp.int32, (half, lanes), 0)
    sign = jnp.where(lane % 2 == 0, -0.25, 0.25)
    lane_first = lane % (lanes // 2) == 0
    lane_last = lane % (lanes // 2) == lanes // 2 - 1
    index = part * (lanes // 2) + lane // 2
    for s in range(species):
        p = ref[slot, s]
        below = jnp.where(row == 0, p, pltpu.roll(p, 1, 0))
        above = jnp.where(row == half - 1, p, pltpu.roll(p, half - 1, 0))
        left = jnp.where(lane_first, p, pltpu.roll(p, 1, 1))
        right = jnp.where(lane_last, p, pltpu.roll(p, lanes - 1, 1))
        slope_y = 0.125 * (above - below)
        slope_z = 0.5 * (right - left)
        gz = jnp.take_along_axis(slope_z, index, axis=1) * sign
        even = jnp.take_along_axis(p - slope_y, index, axis=1) + gz
        odd = jnp.take_along_axis(p + slope_y, index, axis=1) + gz
        store(s, even, odd)


def build_kernel(shape, fine_at_ref, coarse_at_ref, first_ref, out_ref, ylow_ref, yhigh_ref, xlow_ref, xhigh_ref):
    planes, species, rows, lanes = shape
    half = rows // 2

    def body(c, carry):
        at = [fine_at_ref[2 * c], fine_at_ref[2 * c + 1]]
        code = coarse_at_ref[c]
        unit = code // 2 % (DIRECT + EXTRA)

        @pl.when(((at[0] < 0) | (at[1] < 0)) & (unit < DIRECT))
        def _():
            def store(s, even, odd):
                for child in range(2):
                    base = pl.multiple_of(((2 * c + child) * species + s) * rows, rows)
                    out_ref[pl.ds(base, half, stride=2), :] = even
                    out_ref[pl.ds(base + 1, half, stride=2), :] = odd

            interpolate(first_ref, code // 2 // (DIRECT + EXTRA) * DIRECT + unit, code % 2, store)

        for child in range(2):
            for h in range(2):
                late = 2 * (at[child] % FINE_CAP) + h

                @pl.when((at[child] >= 0) & (late < DIRECT))
                def _():
                    slot = at[child] // FINE_CAP * DIRECT + late
                    for s in range(species):
                        base = pl.multiple_of(((2 * c + child) * species + s) * rows + h * half, half)
                        out_ref[pl.ds(base, half), :] = first_ref[slot, s]

        return carry

    lax.fori_loop(0, planes // 2, body, 0)
    for r in range(ITERS):
        rows_to_edges(out_ref, ylow_ref, r * species * planes, r, planes, species, rows)
        rows_to_edges(out_ref, yhigh_ref, r * species * planes, rows - ITERS + r, planes, species, rows)
    deep = ITERS * species * rows
    xlow_ref[...] = out_ref[0:deep]
    xhigh_ref[...] = out_ref[planes * species * rows - deep : planes * species * rows]


def late_units(shape, late_ref, left_ref, fine_at_ref, coarse_at_ref, second_ref, rest_ref, held_ref,
               plane_ref, sem, half_plane, whole_plane):
    planes, _, rows, _ = shape
    half = rows // 2
    planned = left_ref[0] == 0

    def children(c, ref, slot):
        def store(s, even, odd):
            plane_ref[s, pl.ds(0, half, stride=2), :] = even
            plane_ref[s, pl.ds(1, half, stride=2), :] = odd

        interpolate(ref, slot, coarse_at_ref[c] % 2, store)
        for child in range(2):

            @pl.when(fine_at_ref[2 * c + child] < 0)
            def _():
                whole_plane(2 * c + child)

    def from_relay(m, carry):
        what = late_ref[m]

        @pl.when((what >= 0) & (what < 2 * planes))
        def _():
            for h in range(2):

                @pl.when(what % 2 == h)
                def _():
                    half_plane(what // 2, h, second_ref, m)

        for more in range(2):
            parent = late_ref[(1 + more) * late_ref.shape[0] // 3 + m]

            @pl.when(parent >= 0)
            def _():
                children(parent, second_ref, m)

        return carry

    @pl.when(planned)
    def _():
        lax.fori_loop(0, second_ref.shape[0], from_relay, 0)

    def bring(source, unit):
        copy = pltpu.make_async_copy(
            rest_ref.at[pl.ds(source * EXTRA + jnp.maximum(unit - DIRECT, 0), 1)], held_ref, sem
        )
        copy.start()
        copy.wait()

    def direct(c, carry):
        code = coarse_at_ref[c]
        unit = code // 2 % (DIRECT + EXTRA)

        @pl.when(((fine_at_ref[2 * c] < 0) | (fine_at_ref[2 * c + 1] < 0)) & (unit >= DIRECT))
        def _():
            bring(code // 2 // (DIRECT + EXTRA), unit)
            children(c, held_ref, 0)

        for x in (2 * c, 2 * c + 1):
            at = fine_at_ref[x]
            for h in range(2):
                late = 2 * (at % FINE_CAP) + h

                @pl.when((at >= 0) & (late >= DIRECT))
                def _():
                    bring(at // FINE_CAP, late)
                    half_plane(x, h, held_ref, 0)

        return carry

    @pl.when(jnp.logical_not(planned))
    def _():
        lax.fori_loop(0, planes // 2, direct, 0)


def edges_kernel(
    shape, late_ref, left_ref, fine_at_ref, coarse_at_ref, second_ref, rest_ref,
    ylow_in_ref, yhigh_in_ref, xlow_in_ref, xhigh_in_ref,
    ylow_ref, yhigh_ref, xlow_ref, xhigh_ref, low_low_ref, low_high_ref, high_low_ref, high_high_ref, held_ref, plane_ref,
    sem,
):
    planes, species, rows, _ = shape
    half = rows // 2
    size = species * rows
    ylow_ref[...] = ylow_in_ref[...]
    yhigh_ref[...] = yhigh_in_ref[...]
    xlow_ref[...] = xlow_in_ref[...]
    xhigh_ref[...] = xhigh_in_ref[...]

    def half_edges(x, h, value):
        edge_ref, first = ((ylow_ref, 0), (yhigh_ref, half - ITERS))[h]
        for s in range(species):
            for r in range(ITERS):
                edge_ref[pl.ds((r * species + s) * planes + x, 1), :] = value(s, slice(first + r, first + r + 1))
        for near, xedge_ref, at in ((x < ITERS, xlow_ref, x), (x >= planes - ITERS, xhigh_ref, x - planes + ITERS)):

            @pl.when(near)
            def _():
                for s in range(species):
                    base = pl.multiple_of(at * size + s * rows + h * half, half)
                    xedge_ref[pl.ds(base, half), :] = value(s, slice(0, half))

    def half_plane(x, h, ref, slot):
        half_edges(x, h, lambda s, part: ref[slot, s, part])

    def whole_plane(x):
        for h in range(2):
            half_edges(x, h, lambda s, part: plane_ref[s, h * half + part.start : h * half + part.stop])

    late_units(
        shape, late_ref, left_ref, fine_at_ref, coarse_at_ref, second_ref, rest_ref, held_ref, plane_ref,
        sem, half_plane, whole_plane,
    )
    first, last = 0, (ITERS - 1) * species * planes
    for corner_ref, edge_ref, at in (
        (low_low_ref, ylow_ref, first),
        (low_high_ref, yhigh_ref, last),
        (high_low_ref, ylow_ref, first + planes - 1),
        (high_high_ref, yhigh_ref, last + planes - 1),
    ):
        corner_ref[...] = jnp.zeros_like(corner_ref)
        for s in range(species):
            corner_ref[s : s + 1] = edge_ref[at + s * planes : at + s * planes + 1]


def velocity_edges_kernel(vel_ref, ylow_ref, yhigh_ref, xlow_ref, xhigh_ref, *, shape):
    planes, directions, rows, _ = shape
    size = directions * rows
    rows_to_edges(vel_ref, ylow_ref, 0, 0, planes, directions, rows)
    rows_to_edges(vel_ref, yhigh_ref, 0, rows - 1, planes, directions, rows)
    xlow_ref[...] = vel_ref[0:size]
    xhigh_ref[...] = vel_ref[(planes - 1) * size : planes * size]


class Flow:
    def __init__(self, velocity):
        self.positive = [jnp.maximum(v, 0.0) for v in velocity]
        self.negative = [jnp.minimum(v, 0.0) for v in velocity]
        self.keep = 1.0
        for low, high in zip(self.positive, self.negative):
            self.keep = self.keep - (low - high)

    def step(self, u, neighbours, d):
        new = u * (self.keep - 6.0 * d)
        for k, (low, high) in enumerate(neighbours):
            new = new + low * (d + self.positive[k]) + high * (d - self.negative[k])
        return new


def steps_kernel(
    shape, late_ref, left_ref, fine_at_ref, coarse_at_ref, inside_ref, diff_ref, second_ref, rest_ref, state_ref,
    vel_ref, ylow_own_ref, yhigh_own_ref, ylow_ref, yhigh_ref, xlow_ref, xhigh_ref, low_low_ref, low_high_ref, high_low_ref,
    high_high_ref, vylow_ref, vyhigh_ref, vxlow_ref, vxhigh_ref, out_ref, u0_ref, u1_ref, row_low_ref, row_high_ref, plane_low_ref, plane_high_ref, held_ref, plane_ref, sem,
    out_sem,
):
    planes, species, rows, lanes = shape
    half = rows // 2
    size = species * rows
    copy = pltpu.make_async_copy(state_ref, u0_ref, sem)
    copy.start()

    def along(u, first, last, dim):
        count = u.shape[dim]
        at = lax.broadcasted_iota(jnp.int32, u.shape, dim)
        low = jnp.where(at == 0, first, pltpu.roll(u, 1, dim))
        high = jnp.where(at == count - 1, last, pltpu.roll(u, count - 1, dim))
        return low, high

    for (near_ref, near, far, own_ref, own, v_ref, corner, target_ref, inside) in (
        (ylow_ref, 1, 0, ylow_own_ref, 0, vylow_ref, (low_low_ref, high_low_ref), row_low_ref, 0),
        (yhigh_ref, 0, 1, yhigh_own_ref, 1, vyhigh_ref, (low_high_ref, high_high_ref), row_high_ref, 1),
    ):
        for x in range(0, planes, 16):
            flow = Flow([v_ref[k * planes + x : k * planes + x + 16] for k in range(3)])
            for s in range(species):

                def band(ref, r):
                    start = (r * species + s) * planes + x
                    return ref[start : start + 16]

                u = band(near_ref, near)
                start = (near * species + s) * planes
                if x == 0:
                    first = corner[0][s : s + 1]
                else:
                    first = near_ref[start + x - 1 : start + x]
                if x + 16 == planes:
                    last = corner[1][s : s + 1]
                else:
                    last = near_ref[start + x + 16 : start + x + 17]
                outer, inner = band(near_ref, far), band(own_ref, own)
                across = (outer, inner) if inside == 0 else (inner, outer)
                new = flow.step(u, (along(u, first, last, 0), across, along(u, u, u, 1)), diff_ref[s])
                target_ref[s * planes + x : s * planes + x + 16] = new * inside_ref[inside]

    def at(ref, x):
        return lambda s: ref[pl.ds(pl.multiple_of(x * size + s * rows, rows), rows), :]

    def edge(ref, offset, x):
        return lambda s: ref[pl.ds(offset + s * planes + x, 1), :]

    def plane(velocity, center, below, above, y_low, y_high, store):
        flow = Flow(velocity)
        for s in range(species):
            u = center(s)
            sides = ((below(s), above(s)), along(u, y_low(s), y_high(s), 0), along(u, u, u, 1))
            store(s, flow.step(u, sides, diff_ref[s]))

    copy.wait()

    def half_plane(x, h, ref, slot):
        for s in range(species):
            base = pl.multiple_of(x * size + s * rows + h * half, half)
            u0_ref[pl.ds(base, half), :] = ref[slot, s]

    def whole_plane(x):
        for s in range(species):
            u0_ref[pl.ds(pl.multiple_of(x * size + s * rows, rows), rows), :] = plane_ref[s]

    late_units(
        shape, late_ref, left_ref, fine_at_ref, coarse_at_ref, second_ref, rest_ref, held_ref, plane_ref,
        sem, half_plane, whole_plane,
    )

    for (halo_ref, near, below, above, v_ref, target_ref, (corner_low_ref, corner_high_ref, inside)) in (
        (xlow_ref, 1, at(xlow_ref, 0), at(u0_ref, 0), vxlow_ref, plane_low_ref, (low_low_ref, low_high_ref, 2)),
        (xhigh_ref, 0, at(u0_ref, planes - 1), at(xhigh_ref, 1), vxhigh_ref, plane_high_ref, (high_low_ref, high_high_ref, 3)),
    ):

        def store(s, new):
            target_ref[s * rows : (s + 1) * rows] = new * inside_ref[inside]

        def corner(ref):
            return lambda s: ref[s : s + 1]

        velocity = [v_ref[k * rows : (k + 1) * rows] for k in range(3)]
        plane(velocity, at(halo_ref, near), below, above, corner(corner_low_ref), corner(corner_high_ref), store)

    def advance(u_ref, new_ref, low, high, y_low, y_high, after):
        def group(x, first, last):
            for i in range(UNROLL):

                def store(s, new):
                    new_ref[pl.ds(pl.multiple_of((x + i) * size + s * rows, rows), rows), :] = new

                plane(
                    [vel_ref[x + i, k] for k in range(3)],
                    at(u_ref, x + i),
                    low if first and i == 0 else at(u_ref, x + i - 1),
                    high if last and i == UNROLL - 1 else at(u_ref, x + i + 1),
                    edge(*y_low, x + i),
                    edge(*y_high, x + i),
                    store,
                )
            after(x // UNROLL)

        def body(g, carry):
            group(g * UNROLL, False, False)
            return carry

        group(0, True, False)
        lax.fori_loop(1, planes // UNROLL - 1, body, 0)
        group(planes - UNROLL, False, True)

    def send(g):
        part = pl.ds(pl.multiple_of(g * UNROLL * size, UNROLL * size), UNROLL * size)
        return pltpu.make_async_copy(u0_ref.at[part], out_ref.at[part], out_sem.at[g])

    advance(
        u0_ref, u1_ref, at(xlow_ref, 1), at(xhigh_ref, 0), (ylow_ref, species * planes), (yhigh_ref, 0), lambda g: None
    )
    advance(
        u1_ref, u0_ref, at(plane_low_ref, 0), at(plane_high_ref, 0), (row_low_ref, 0), (row_high_ref, 0),
        lambda g: send(g).start(),
    )

    def finish(g, carry):
        send(g).wait()
        return carry

    lax.fori_loop(0, planes // UNROLL, finish, 0)


def empty_kernel(out_ref):
    pass


def cost(microseconds):
    return pl.CostEstimate(flops=0, bytes_accessed=int(microseconds * 3.6e6), transcendentals=0)


def neighbours(axis, low, high):
    size = lax.axis_size(axis)
    up = [(i, (i + 1) % size) for i in range(size - 1)]
    return lax.ppermute(high, axis, up), lax.ppermute(low, axis, [(b, a) for a, b in up])


def diagonal(value, grp_step, dev_step):
    groups, devices = lax.axis_size("grp"), lax.axis_size("dev")
    pairs = []
    for g in range(groups):
        for d in range(devices):
            to_g, to_d = g + grp_step, d + dev_step
            if 0 <= to_g < groups and 0 <= to_d < devices:
                pairs.append((g * devices + d, to_g * devices + to_d))
    return lax.ppermute(value, ("grp", "dev"), pairs)


def on_device(old_fine, old_ids, old_coarse, coarse_ids, velocity, diffusion):
    devices = lax.axis_size("dev")
    me = lax.axis_index("dev")
    me_ref = me.reshape(1).astype(jnp.int32)
    planes, species, rows, lanes = old_fine.shape
    half = rows // 2
    coarse_planes = old_coarse.shape[0]
    unit_count = DIRECT + EXTRA
    f32 = jnp.float32
    i32 = jnp.int32

    def units_shape(count):
        return jax.ShapeDtypeStruct((count, species, half, lanes), f32)

    own, own_coarse = old_ids[0], coarse_ids[0]
    labels = jnp.broadcast_to(jnp.concatenate([own, own_coarse])[None], (devices, planes + coarse_planes))
    labels = lax.all_to_all(labels, "dev", split_axis=0, concat_axis=0, tiled=True)
    all_ids, all_coarse = labels[:, :planes], labels[:, planes:]
    all_box = jnp.where(all_ids >= 0, all_ids // planes, -1)
    all_coarse_box = all_coarse // coarse_planes
    flat_parents = jnp.where(all_ids >= 0, all_ids // 2, -1).reshape(-1)

    def needed(coarse):
        kept = jnp.sum((flat_parents == coarse[..., None]).astype(i32), axis=-1)
        return kept < 2

    box = jnp.arange(lanes) % devices
    fine_units = jnp.sum((all_box[:, None, :] == box[None, :, None]).astype(i32), axis=-1)
    asked = needed(all_coarse)[:, None, :] & (all_coarse_box[:, None, :] == box[None, :, None])
    units = 2 * fine_units + jnp.max(asked.astype(i32), axis=-1)
    row, column = pl.pallas_call(
        plan_kernel,
        out_shape=[jax.ShapeDtypeStruct((8, lanes), i32), jax.ShapeDtypeStruct((devices, lanes), i32)],
        in_specs=[SMEM, VMEM],
        out_specs=[VMEM] * 2,
        name="plan",
    )(me_ref, units)
    left = jnp.max(row[EXTRA, :devices]).reshape(1)

    own_box = jnp.where(own >= 0, own // planes, -1)
    send_fine = jnp.where(own >= 0, own_box * FINE_CAP + ranks(own_box), -1)
    own_coarse_box = own_coarse // coarse_planes
    before = jnp.sum((own_box[None, :] == own_coarse_box[:, None]).astype(i32), axis=1)
    send_coarse = (own_coarse_box * unit_count + 2 * before) * 2 + ranks(own_coarse_box)
    send_coarse = jnp.where(needed(own_coarse), send_coarse, -1)

    order = jnp.arange(devices)[:, None]
    wanted = me * planes + jnp.arange(planes)
    fine_at = jnp.where(all_ids[None] == wanted[:, None, None], (order * FINE_CAP + ranks(all_box))[None], -1)
    fine_at = jnp.max(fine_at, axis=(1, 2))
    to_me = jnp.sum((all_box == me).astype(i32), axis=1, keepdims=True)
    coarse_wanted = me * coarse_planes + jnp.arange(coarse_planes)
    coarse_code = (order * unit_count + 2 * to_me) * 2 + ranks(all_coarse_box)
    coarse_at = jnp.where(all_coarse[None] == coarse_wanted[:, None, None], coarse_code[None], 0)
    coarse_at = jnp.max(coarse_at, axis=(1, 2))

    def exchange(value):
        return lax.all_to_all(value, "dev", split_axis=0, concat_axis=0, tiled=True)

    def pack(count, first, name):
        return pl.pallas_call(
            functools.partial(pack_kernel, devices, first),
            out_shape=units_shape(count),
            in_specs=[SMEM] * 4 + [ANY, VMEM],
            out_specs=VMEM,
            scratch_shapes=[pltpu.VMEM(old_fine.shape, f32), pltpu.SemaphoreType.DMA((4,))],
            compiler_params=PARAMS,
            name=name,
        )(me_ref, send_fine, send_coarse, row, old_fine, old_coarse)

    packed = pack(devices * DIRECT, True, "pack")

    def no_rest():
        return pl.pallas_call(empty_kernel, out_shape=units_shape(devices * EXTRA), out_specs=ANY, name="nothing")()

    def rest_direct():
        return exchange(pack(devices * EXTRA, False, "pack_rest"))

    rest = lax.cond(left[0] == 0, no_rest, rest_direct)
    packed, rest, flow = lax.optimization_barrier((packed, rest, velocity))
    first = exchange(packed)

    def edge_shapes(deep, count):
        along_y = jax.ShapeDtypeStruct((deep * count * planes, lanes), f32)
        along_x = jax.ShapeDtypeStruct((deep * count * rows, lanes), f32)
        return [along_y, along_y, along_x, along_x]

    directions = flow.shape[1]
    vylow, vyhigh, vxlow, vxhigh = pl.pallas_call(
        functools.partial(velocity_edges_kernel, shape=flow.shape),
        out_shape=edge_shapes(1, directions),
        in_specs=[VMEM],
        out_specs=[VMEM] * 4,
        compiler_params=PARAMS,
        name="velocity_edges",
    )(flow.reshape(planes * directions * rows, lanes))
    flow_edges = [*neighbours("grp", vylow, vyhigh), *neighbours("dev", vxlow, vxhigh)]
    first, *flow_edges = lax.optimization_barrier((first, *flow_edges))
    second = pl.pallas_call(
        forward_kernel,
        out_shape=units_shape(devices),
        in_specs=[SMEM] * 2 + [ANY],
        out_specs=VMEM,
        scratch_shapes=[pltpu.SemaphoreType.DMA((devices,))],
        compiler_params=PARAMS,
        cost_estimate=cost(3),
        name="forward",
    )(me_ref, column, first)
    second = exchange(second)

    size = species * rows
    state_shape = jax.ShapeDtypeStruct((planes * size, lanes), f32)
    state, *edges = pl.pallas_call(
        functools.partial(build_kernel, old_fine.shape),
        out_shape=[state_shape] + edge_shapes(ITERS, species),
        in_specs=[SMEM] * 2 + [VMEM],
        out_specs=[VMEM] * 5,
        compiler_params=PARAMS,
        cost_estimate=cost(10),
        name="build",
    )(fine_at, coarse_at, first)
    relay_of = (jnp.arange(devices)[:, None] + me + column[:, :EXTRA] // 8) % devices

    def through(source, unit, used):
        over = jnp.arange(EXTRA) == (unit - DIRECT)[:, None]
        hit = (source[:, None, None] == jnp.arange(devices)[None, :, None]) & over[:, None, :]
        relay = jnp.max(jnp.where(hit, relay_of[None], -1), axis=(1, 2))
        return jnp.where(used & (unit >= DIRECT), relay, -1)

    order = jnp.arange(devices)
    halves = jnp.arange(2 * planes)
    at = jnp.repeat(fine_at, 2)
    relay = through(at // FINE_CAP, 2 * (at % FINE_CAP) + halves % 2, at >= 0)
    late_fine = jnp.max(jnp.where(relay[:, None] == order[None], halves[:, None], -1), axis=0)
    parents = jnp.arange(coarse_planes)
    code = coarse_at // 2
    fresh = jnp.min(fine_at.reshape(coarse_planes, 2), axis=1) < 0
    relay = through(code // unit_count, code % unit_count, fresh)
    late_parents = [
        jnp.max(jnp.where((relay[:, None] == order[None]) & (coarse_at % 2 == j)[:, None], parents[:, None], -1), axis=0)
        for j in range(COARSE_CAP)
    ]
    late = jnp.concatenate([late_fine, *late_parents])
    late_scratch = [
        pltpu.VMEM((1, species, half, lanes), f32),
        pltpu.VMEM((species, rows, lanes), f32),
        pltpu.SemaphoreType.DMA,
    ]
    corner_shape = jax.ShapeDtypeStruct((16, lanes), f32)
    ylow_own, yhigh_own, xlow_own, xhigh_own, *corners = pl.pallas_call(
        functools.partial(edges_kernel, old_fine.shape),
        out_shape=edge_shapes(ITERS, species) + [corner_shape] * 4,
        in_specs=[SMEM] * 4 + [VMEM, ANY] + [VMEM] * 4,
        out_specs=[VMEM] * 8,
        scratch_shapes=late_scratch,
        compiler_params=PARAMS,
        cost_estimate=cost(4),
        name="edges",
    )(late, left, fine_at, coarse_at, second, rest, *edges)
    ylow, yhigh = neighbours("grp", ylow_own, yhigh_own)
    xlow, xhigh = neighbours("dev", xlow_own, xhigh_own)
    low_low, low_high, high_low, high_high = corners
    corners = [diagonal(high_high, 1, 1), diagonal(high_low, -1, 1), diagonal(low_high, 1, -1), diagonal(low_low, -1, -1)]
    grp, dev = lax.axis_index("grp"), lax.axis_index("dev")
    inside = jnp.stack([grp > 0, grp < lax.axis_size("grp") - 1, dev > 0, dev < devices - 1]).astype(f32)
    row_edge = pltpu.VMEM((species * planes, lanes), f32)
    plane_edge = pltpu.VMEM((size, lanes), f32)
    done = pl.pallas_call(
        functools.partial(steps_kernel, old_fine.shape),
        out_shape=state_shape,
        in_specs=[SMEM] * 6 + [VMEM, ANY, ANY] + [VMEM] * 15,
        out_specs=ANY,
        scratch_shapes=[pltpu.VMEM(state_shape.shape, f32)] * 2
        + [row_edge] * 2
        + [plane_edge] * 2
        + late_scratch
        + [pltpu.SemaphoreType.DMA((planes // UNROLL,))],
        compiler_params=PARAMS,
        name="steps",
    )(
        late, left, fine_at, coarse_at, inside, diffusion, second, rest, state, velocity,
        ylow_own, yhigh_own, ylow, yhigh, xlow, xhigh, *corners, *flow_edges,
    )
    return done.reshape(old_fine.shape)


def solution(mesh):
    in_specs = (
        P("dev", None, "grp", None),
        P("grp", "dev"),
        P("dev", None, "grp", None),
        P("grp", "dev"),
        P("dev", None, "grp", None),
        P(),
    )
    out_specs = P("dev", None, "grp", None)
    return jax.shard_map(
        on_device, mesh=mesh, in_specs=in_specs, out_specs=out_specs, check_vma=False
    )
```

```python
import functools

import jax
import jax.numpy as jnp
from jax import lax
from jax.experimental import pallas as pl
from jax.experimental.pallas import tpu as pltpu
from jax.sharding import PartitionSpec as P

ITERS = 2
FINE_CAP = 4
COARSE_CAP = 2
DIRECT = 5
EXTRA = 2 * FINE_CAP + 1 - DIRECT
VMEM = pl.BlockSpec(memory_space=pltpu.VMEM)
SMEM = pl.BlockSpec(memory_space=pltpu.SMEM)
ANY = pl.BlockSpec(memory_space=pl.ANY)
PARAMS = pltpu.CompilerParams(vmem_limit_bytes=56 * 1024 * 1024)
UNROLL = 4


def ranks(boxes):
    count = boxes.shape[-1]
    earlier = jnp.arange(count)[None, :] < jnp.arange(count)[:, None]
    same = boxes[..., None, :] == boxes[..., :, None]
    return jnp.sum((same & earlier).astype(jnp.int32), axis=-1)


def plan_kernel(me_ref, units_ref, row_ref, column_ref):
    devices, lanes = units_ref.shape
    me = me_ref[0]
    units = units_ref[...]
    source = lax.broadcasted_iota(jnp.int32, units.shape, 0)
    lane = lax.broadcasted_iota(jnp.int32, units.shape, 1)
    surplus = pltpu.roll(jnp.maximum(units - DIRECT, 0), 0, 1, stride=1, stride_axis=0)
    none = jnp.full(units.shape, -1, jnp.int32)

    def one_round(r, carry):
        left, free, second, through, *chosen = carry
        ok = (left > 0) & (free > 0) & (second > 0)
        position = DIRECT - free
        item = surplus - left
        chosen = [jnp.where(ok & (item == i), r * 8 + position, table) for i, table in enumerate(chosen)]
        through = jnp.where(ok, source * 8 + position, through)
        used = ok.astype(jnp.int32)
        left, free, second = left - used, free - used, second - used
        free = pltpu.roll(free, lanes - 1, 1)
        second = pltpu.roll(pltpu.roll(second, devices - 1, 0), lanes - 1, 1)
        through = pltpu.roll(pltpu.roll(through, devices - 1, 0), lanes - 1, 1)
        return (left, free, second, through, *chosen)

    init = (surplus, jnp.maximum(DIRECT - units, 0), jnp.ones(units.shape, jnp.int32), none) + (none,) * EXTRA
    left, _, _, through, *chosen = lax.fori_loop(0, devices, one_round, init)
    for i in range(EXTRA):
        row_ref[i : i + 1] = jnp.max(jnp.where(source == me, chosen[i], -1), axis=0, keepdims=True)
    row_ref[EXTRA : EXTRA + 1] = jnp.max(left, axis=0, keepdims=True)
    column = none
    for i in range(EXTRA):
        mine = (lane < devices) & (lane == (source + me) % devices)
        found = jnp.max(jnp.where(mine, chosen[i], -1), axis=1, keepdims=True)
        column = jnp.where(lane == i, found, column)
    found = jnp.max(jnp.where(lane == me, through, -1), axis=1, keepdims=True)
    column_ref[...] = jnp.where(lane == EXTRA, found, column)


def pack_kernel(
    devices, first, me_ref, fine_at_ref, coarse_at_ref, row_ref, fine_in_ref, coarse_ref, out_ref, fine_ref, sem
):
    planes = fine_ref.shape[0]
    coarse_planes, _, half, depth = coarse_ref.shape
    part = planes // sem.shape[0]

    def bring(i):
        planes_of = pl.ds(i * part, part)
        return pltpu.make_async_copy(fine_in_ref.at[planes_of], fine_ref.at[planes_of], sem.at[i])

    def slot_of(box, unit):
        if first:
            return first_slot(devices, me_ref[0], row_ref, box, unit)
        return jnp.where(unit < DIRECT, -1, box * EXTRA + unit - DIRECT)

    for i in range(sem.shape[0]):
        bring(i).start()

    def coarse_plane(k, carry):
        code = coarse_at_ref[k]

        @pl.when(code >= 0)
        def _():
            at = code // 2
            slot = slot_of(at // (DIRECT + EXTRA), at % (DIRECT + EXTRA))
            for j in range(2):

                @pl.when((slot >= 0) & (code % 2 == j))
                def _():
                    out_ref[slot, :, :, j * depth : (j + 1) * depth] = coarse_ref[k]

        return carry

    lax.fori_loop(0, coarse_planes, coarse_plane, 0)

    def fine_plane(k, carry):
        code = fine_at_ref[k]
        box, rank = code // FINE_CAP, code % FINE_CAP
        whole = DIRECT // 2

        if first:

            @pl.when((code >= 0) & (rank < whole))
            def _():
                for h in range(2):
                    out_ref[box * DIRECT + 2 * rank + h] = fine_ref[k, :, h * half : (h + 1) * half, :]

        @pl.when((code >= 0) & (rank >= whole))
        def _():
            for h in range(2):
                slot = slot_of(box, 2 * rank + h)

                @pl.when(slot >= 0)
                def _():
                    out_ref[slot] = fine_ref[k, :, h * half : (h + 1) * half, :]

        return carry

    for i in range(sem.shape[0]):
        bring(i).wait()
        lax.fori_loop(i * part, (i + 1) * part, fine_plane, 0)


def first_slot(devices, me, row_ref, box, unit):
    t = (me + box) % devices
    code = row_ref[jnp.maximum(unit - DIRECT, 0), t]
    relay = jnp.where(code >= 0, ((t + code // 8) % devices) * DIRECT + code % 8, -1)
    return jnp.where(unit < DIRECT, box * DIRECT + unit, relay)


def forward_kernel(me_ref, column_ref, in_ref, out_ref, sem):
    devices = out_ref.shape[0]

    def each(act):
        def body(a, carry):
            code = column_ref[a, EXTRA]

            @pl.when(code >= 0)
            def _():
                box = (me_ref[0] - a + devices) % devices
                act(pltpu.make_async_copy(in_ref.at[(code // 8) * DIRECT + code % 8], out_ref.at[box], sem.at[a]))

            return carry

        lax.fori_loop(0, devices, body, 0)

    each(lambda copy: copy.start())
    each(lambda copy: copy.wait())


def rows_to_edges(flat_ref, edge_ref, offset, row, planes, species, rows):
    for s in range(species):
        for x in range(0, planes, 8):
            at = offset + s * planes + x
            edge_ref[at : at + 8] = flat_ref[pl.ds((x * species + s) * rows + row, 8, stride=species * rows), :]


def interpolate(ref, slot, part, store):
    _, species, half, lanes = ref.shape
    lane = lax.broadcasted_iota(jnp.int32, (half, lanes), 1)
    row = lax.broadcasted_iota(jnp.int32, (half, lanes), 0)
    sign = jnp.where(lane % 2 == 0, -0.25, 0.25)
    lane_first = lane % (lanes // 2) == 0
    lane_last = lane % (lanes // 2) == lanes // 2 - 1
    index = part * (lanes // 2) + lane // 2
    for s in range(species):
        p = ref[slot, s]
        below = jnp.where(row == 0, p, pltpu.roll(p, 1, 0))
        above = jnp.where(row == half - 1, p, pltpu.roll(p, half - 1, 0))
        left = jnp.where(lane_first, p, pltpu.roll(p, 1, 1))
        right = jnp.where(lane_last, p, pltpu.roll(p, lanes - 1, 1))
        slope_y = 0.125 * (above - below)
        slope_z = 0.5 * (right - left)
        gz = jnp.take_along_axis(slope_z, index, axis=1) * sign
        even = jnp.take_along_axis(p - slope_y, index, axis=1) + gz
        odd = jnp.take_along_axis(p + slope_y, index, axis=1) + gz
        store(s, even, odd)


def build_kernel(shape, fine_at_ref, coarse_at_ref, first_ref, out_ref, ylow_ref, yhigh_ref, xlow_ref, xhigh_ref):
    planes, species, rows, lanes = shape
    half = rows // 2

    def body(c, carry):
        at = [fine_at_ref[2 * c], fine_at_ref[2 * c + 1]]
        code = coarse_at_ref[c]
        unit = code // 2 % (DIRECT + EXTRA)

        @pl.when(((at[0] < 0) | (at[1] < 0)) & (unit < DIRECT))
        def _():
            def store(s, even, odd):
                for child in range(2):
                    base = pl.multiple_of(((2 * c + child) * species + s) * rows, rows)
                    out_ref[pl.ds(base, half, stride=2), :] = even
                    out_ref[pl.ds(base + 1, half, stride=2), :] = odd

            interpolate(first_ref, code // 2 // (DIRECT + EXTRA) * DIRECT + unit, code % 2, store)

        for child in range(2):
            for h in range(2):
                late = 2 * (at[child] % FINE_CAP) + h

                @pl.when((at[child] >= 0) & (late < DIRECT))
                def _():
                    slot = at[child] // FINE_CAP * DIRECT + late
                    for s in range(species):
                        base = pl.multiple_of(((2 * c + child) * species + s) * rows + h * half, half)
                        out_ref[pl.ds(base, half), :] = first_ref[slot, s]

        return carry

    lax.fori_loop(0, planes // 2, body, 0)
    for r in range(ITERS):
        rows_to_edges(out_ref, ylow_ref, r * species * planes, r, planes, species, rows)
        rows_to_edges(out_ref, yhigh_ref, r * species * planes, rows - ITERS + r, planes, species, rows)
    deep = ITERS * species * rows
    xlow_ref[...] = out_ref[0:deep]
    xhigh_ref[...] = out_ref[planes * species * rows - deep : planes * species * rows]


def late_units(shape, late_ref, left_ref, fine_at_ref, coarse_at_ref, second_ref, rest_ref, held_ref,
               plane_ref, sem, half_plane, whole_plane):
    planes, _, rows, _ = shape
    half = rows // 2
    planned = left_ref[0] == 0

    def children(c, ref, slot):
        def store(s, even, odd):
            plane_ref[s, pl.ds(0, half, stride=2), :] = even
            plane_ref[s, pl.ds(1, half, stride=2), :] = odd

        interpolate(ref, slot, coarse_at_ref[c] % 2, store)
        for child in range(2):

            @pl.when(fine_at_ref[2 * c + child] < 0)
            def _():
                whole_plane(2 * c + child)

    def from_relay(m, carry):
        what = late_ref[m]

        @pl.when((what >= 0) & (what < 2 * planes))
        def _():
            for h in range(2):

                @pl.when(what % 2 == h)
                def _():
                    half_plane(what // 2, h, second_ref, m)

        for more in range(2):
            parent = late_ref[(1 + more) * late_ref.shape[0] // 3 + m]

            @pl.when(parent >= 0)
            def _():
                children(parent, second_ref, m)

        return carry

    @pl.when(planned)
    def _():
        lax.fori_loop(0, second_ref.shape[0], from_relay, 0)

    def bring(source, unit):
        copy = pltpu.make_async_copy(
            rest_ref.at[pl.ds(source * EXTRA + jnp.maximum(unit - DIRECT, 0), 1)], held_ref, sem
        )
        copy.start()
        copy.wait()

    def direct(c, carry):
        code = coarse_at_ref[c]
        unit = code // 2 % (DIRECT + EXTRA)

        @pl.when(((fine_at_ref[2 * c] < 0) | (fine_at_ref[2 * c + 1] < 0)) & (unit >= DIRECT))
        def _():
            bring(code // 2 // (DIRECT + EXTRA), unit)
            children(c, held_ref, 0)

        for x in (2 * c, 2 * c + 1):
            at = fine_at_ref[x]
            for h in range(2):
                late = 2 * (at % FINE_CAP) + h

                @pl.when((at >= 0) & (late >= DIRECT))
                def _():
                    bring(at // FINE_CAP, late)
                    half_plane(x, h, held_ref, 0)

        return carry

    @pl.when(jnp.logical_not(planned))
    def _():
        lax.fori_loop(0, planes // 2, direct, 0)


def edges_kernel(
    shape, late_ref, left_ref, fine_at_ref, coarse_at_ref, second_ref, rest_ref,
    ylow_in_ref, yhigh_in_ref, xlow_in_ref, xhigh_in_ref,
    ylow_ref, yhigh_ref, xlow_ref, xhigh_ref, held_ref, plane_ref, sem,
):
    planes, species, rows, _ = shape
    half = rows // 2
    size = species * rows
    ylow_ref[...] = ylow_in_ref[...]
    yhigh_ref[...] = yhigh_in_ref[...]
    xlow_ref[...] = xlow_in_ref[...]
    xhigh_ref[...] = xhigh_in_ref[...]

    def half_edges(x, h, value):
        edge_ref, first = ((ylow_ref, 0), (yhigh_ref, half - ITERS))[h]
        for s in range(species):
            for r in range(ITERS):
                edge_ref[pl.ds((r * species + s) * planes + x, 1), :] = value(s, slice(first + r, first + r + 1))
        for near, xedge_ref, at in ((x < ITERS, xlow_ref, x), (x >= planes - ITERS, xhigh_ref, x - planes + ITERS)):

            @pl.when(near)
            def _():
                for s in range(species):
                    base = pl.multiple_of(at * size + s * rows + h * half, half)
                    xedge_ref[pl.ds(base, half), :] = value(s, slice(0, half))

    def half_plane(x, h, ref, slot):
        half_edges(x, h, lambda s, part: ref[slot, s, part])

    def whole_plane(x):
        for h in range(2):
            half_edges(x, h, lambda s, part: plane_ref[s, h * half + part.start : h * half + part.stop])

    late_units(
        shape, late_ref, left_ref, fine_at_ref, coarse_at_ref, second_ref, rest_ref, held_ref, plane_ref,
        sem, half_plane, whole_plane,
    )


def corners_kernel(planes, species, ylow_ref, yhigh_ref, xlow_ref, xhigh_ref, down_ref, up_ref):
    deep = xlow_ref.shape[0]
    down_ref[0:deep] = xlow_ref[...]
    up_ref[0:deep] = xhigh_ref[...]
    for message_ref, x in ((down_ref, 0), (up_ref, planes - 1)):
        for s in range(species):
            low = ((ITERS - 1) * species + s) * planes + x
            high = s * planes + x
            message_ref[deep + s : deep + s + 1] = ylow_ref[low : low + 1]
            message_ref[deep + 16 + s : deep + 16 + s + 1] = yhigh_ref[high : high + 1]
        for at in (deep + species, deep + 16 + species):
            message_ref[at : at + 16 - species] = jnp.zeros((16 - species, message_ref.shape[1]), jnp.float32)


def velocity_edges_kernel(vel_ref, ylow_ref, yhigh_ref, xlow_ref, xhigh_ref, *, shape):
    planes, directions, rows, _ = shape
    size = directions * rows
    rows_to_edges(vel_ref, ylow_ref, 0, 0, planes, directions, rows)
    rows_to_edges(vel_ref, yhigh_ref, 0, rows - 1, planes, directions, rows)
    xlow_ref[...] = vel_ref[0:size]
    xhigh_ref[...] = vel_ref[(planes - 1) * size : planes * size]


class Flow:
    def __init__(self, velocity):
        self.positive = [jnp.maximum(v, 0.0) for v in velocity]
        self.negative = [jnp.minimum(v, 0.0) for v in velocity]
        self.keep = 1.0
        for low, high in zip(self.positive, self.negative):
            self.keep = self.keep - (low - high)

    def step(self, u, neighbours, d):
        new = u * (self.keep - 6.0 * d)
        for k, (low, high) in enumerate(neighbours):
            new = new + low * (d + self.positive[k]) + high * (d - self.negative[k])
        return new


def along(u, first, last, dim):
    count = u.shape[dim]
    at = lax.broadcasted_iota(jnp.int32, u.shape, dim)
    low = jnp.where(at == 0, first, pltpu.roll(u, 1, dim))
    high = jnp.where(at == count - 1, last, pltpu.roll(u, count - 1, dim))
    return low, high


def advance_plane(diff_ref, velocity, center, below, above, y_low, y_high, store):
    flow = Flow(velocity)
    for s in range(diff_ref.shape[0]):
        u = center(s)
        sides = ((below(s), above(s)), along(u, y_low(s), y_high(s), 0), along(u, u, u, 1))
        store(s, flow.step(u, sides, diff_ref[s]))


def planes_of(ref, x, rows, size):
    return lambda s: ref[pl.ds(pl.multiple_of(x * size + s * rows, rows), rows), :]


def advance(shape, diff_ref, vel_ref, u_ref, new_ref, low, high, y_low, y_high, after):
    planes, species, rows, _ = shape
    size = species * rows

    def group(x, first, last):
        for i in range(UNROLL):

            def store(s, new):
                new_ref[pl.ds(pl.multiple_of((x + i) * size + s * rows, rows), rows), :] = new

            advance_plane(
                diff_ref,
                [vel_ref[x + i, k] for k in range(3)],
                planes_of(u_ref, x + i, rows, size),
                low if first and i == 0 else planes_of(u_ref, x + i - 1, rows, size),
                high if last and i == UNROLL - 1 else planes_of(u_ref, x + i + 1, rows, size),
                y_low(x + i),
                y_high(x + i),
                store,
            )
        after(x // UNROLL)

    def body(g, carry):
        group(g * UNROLL, False, False)
        return carry

    group(0, True, False)
    lax.fori_loop(1, planes // UNROLL - 1, body, 0)
    group(planes - UNROLL, False, True)


def send_group(shape, from_ref, to_ref, sem, g):
    size = UNROLL * shape[1] * shape[2]
    part = pl.ds(pl.multiple_of(g * size, size), size)
    return pltpu.make_async_copy(from_ref.at[part], to_ref.at[part], sem.at[g])


def finish_groups(shape, from_ref, to_ref, sem):
    def finish(g, carry):
        send_group(shape, from_ref, to_ref, sem, g).wait()
        return carry

    lax.fori_loop(0, shape[0] // UNROLL, finish, 0)


def first_step_kernel(
    shape, late_ref, left_ref, fine_at_ref, coarse_at_ref, diff_ref, second_ref, rest_ref, state_ref, vel_ref, out_ref,
    u0_ref, u1_ref, held_ref, plane_ref, sem, out_sem,
):
    _, species, rows, _ = shape
    half = rows // 2
    size = species * rows
    copy = pltpu.make_async_copy(state_ref, u0_ref, sem)
    copy.start()
    copy.wait()

    def half_plane(x, h, ref, slot):
        for s in range(species):
            base = pl.multiple_of(x * size + s * rows + h * half, half)
            u0_ref[pl.ds(base, half), :] = ref[slot, s]

    def whole_plane(x):
        for s in range(species):
            u0_ref[pl.ds(pl.multiple_of(x * size + s * rows, rows), rows), :] = plane_ref[s]

    late_units(
        shape, late_ref, left_ref, fine_at_ref, coarse_at_ref, second_ref, rest_ref, held_ref, plane_ref,
        sem, half_plane, whole_plane,
    )

    def nothing(s):
        return 0.0

    advance(
        shape, diff_ref, vel_ref, u0_ref, u1_ref, nothing, nothing, lambda x: nothing, lambda x: nothing,
        lambda g: send_group(shape, u1_ref, out_ref, out_sem, g).start(),
    )
    finish_groups(shape, u1_ref, out_ref, out_sem)


def second_step_kernel(
    shape, inside_ref, diff_ref, first_ref, vel_ref, ylow_own_ref, yhigh_own_ref, xlow_own_ref, xhigh_own_ref, ylow_ref,
    yhigh_ref, xlow_ref, xhigh_ref, vylow_own_ref, vyhigh_own_ref, vylow_ref, vyhigh_ref, vxlow_ref, vxhigh_ref,
    out_ref, u1_ref, u2_ref, row_low_ref, row_high_ref, plane_low_ref, plane_high_ref, sem, out_sem,
):
    planes, species, rows, lanes = shape
    size = species * rows
    deep = ITERS * size
    copy = pltpu.make_async_copy(first_ref, u1_ref, sem)
    copy.start()

    for (near_ref, near, far, own_ref, own, v_ref, corner, target_ref, inside) in (
        (ylow_ref, 1, 0, ylow_own_ref, 0, vylow_ref, deep, row_low_ref, 0),
        (yhigh_ref, 0, 1, yhigh_own_ref, 1, vyhigh_ref, deep + 16, row_high_ref, 1),
    ):
        for x in range(0, planes, 16):
            flow = Flow([v_ref[k * planes + x : k * planes + x + 16] for k in range(3)])
            for s in range(species):

                def band(ref, r):
                    start = (r * species + s) * planes + x
                    return ref[start : start + 16]

                u = band(near_ref, near)
                start = (near * species + s) * planes
                if x == 0:
                    first = xlow_ref[corner + s : corner + s + 1]
                else:
                    first = near_ref[start + x - 1 : start + x]
                if x + 16 == planes:
                    last = xhigh_ref[corner + s : corner + s + 1]
                else:
                    last = near_ref[start + x + 16 : start + x + 17]
                outer, inner = band(near_ref, far), band(own_ref, own)
                across = (outer, inner) if inside == 0 else (inner, outer)
                new = flow.step(u, (along(u, first, last, 0), across, along(u, u, u, 1)), diff_ref[s])
                target_ref[s * planes + x : s * planes + x + 16] = new * inside_ref[inside]

    def at(ref, x):
        return planes_of(ref, x, rows, size)

    for (halo_ref, near, below, above, v_ref, target_ref, inside) in (
        (xlow_ref, 1, at(xlow_ref, 0), at(xlow_own_ref, 0), vxlow_ref, plane_low_ref, 2),
        (xhigh_ref, 0, at(xhigh_own_ref, ITERS - 1), at(xhigh_ref, 1), vxhigh_ref, plane_high_ref, 3),
    ):

        def store(s, new):
            target_ref[s * rows : (s + 1) * rows] = new * inside_ref[inside]

        def corner(offset):
            return lambda s: halo_ref[deep + offset + s : deep + offset + s + 1]

        velocity = [v_ref[k * rows : (k + 1) * rows] for k in range(3)]
        advance_plane(diff_ref, velocity, at(halo_ref, near), below, above, corner(0), corner(16), store)

    copy.wait()
    for x in range(0, planes, 8):
        up = jnp.maximum(vylow_own_ref[planes + x : planes + x + 8], 0.0)
        down = jnp.minimum(vyhigh_own_ref[planes + x : planes + x + 8], 0.0)
        for s in range(species):
            low = pl.ds((x * species + s) * rows, 8, stride=size)
            high = pl.ds((x * species + s) * rows + rows - 1, 8, stride=size)
            start = species * planes + s * planes + x
            u1_ref[low, :] = u1_ref[low, :] + (diff_ref[s] + up) * ylow_ref[start : start + 8]
            start = s * planes + x
            u1_ref[high, :] = u1_ref[high, :] + (diff_ref[s] - down) * yhigh_ref[start : start + 8]
    up = jnp.maximum(vel_ref[0, 0], 0.0)
    down = jnp.minimum(vel_ref[planes - 1, 0], 0.0)
    for s in range(species):
        low = slice(s * rows, (s + 1) * rows)
        high = slice((planes - 1) * size + s * rows, (planes - 1) * size + (s + 1) * rows)
        u1_ref[low] = u1_ref[low] + (diff_ref[s] + up) * at(xlow_ref, 1)(s)
        u1_ref[high] = u1_ref[high] + (diff_ref[s] - down) * at(xhigh_ref, 0)(s)

    def edge(ref):
        return lambda x: lambda s: ref[pl.ds(s * planes + x, 1), :]

    advance(
        shape, diff_ref, vel_ref, u1_ref, u2_ref, at(plane_low_ref, 0), at(plane_high_ref, 0), edge(row_low_ref),
        edge(row_high_ref), lambda g: send_group(shape, u2_ref, out_ref, out_sem, g).start(),
    )
    finish_groups(shape, u2_ref, out_ref, out_sem)


def empty_kernel(out_ref):
    pass


def cost(microseconds):
    return pl.CostEstimate(flops=0, bytes_accessed=int(microseconds * 3.6e6), transcendentals=0)


def neighbours(axis, low, high):
    size = lax.axis_size(axis)
    up = [(i, (i + 1) % size) for i in range(size - 1)]
    return lax.ppermute(high, axis, up), lax.ppermute(low, axis, [(b, a) for a, b in up])


def on_device(old_fine, old_ids, old_coarse, coarse_ids, velocity, diffusion):
    devices = lax.axis_size("dev")
    me = lax.axis_index("dev")
    me_ref = me.reshape(1).astype(jnp.int32)
    planes, species, rows, lanes = old_fine.shape
    half = rows // 2
    coarse_planes = old_coarse.shape[0]
    unit_count = DIRECT + EXTRA
    f32 = jnp.float32
    i32 = jnp.int32

    def units_shape(count):
        return jax.ShapeDtypeStruct((count, species, half, lanes), f32)

    own, own_coarse = old_ids[0], coarse_ids[0]
    labels = jnp.broadcast_to(jnp.concatenate([own, own_coarse])[None], (devices, planes + coarse_planes))
    labels = lax.all_to_all(labels, "dev", split_axis=0, concat_axis=0, tiled=True)
    all_ids, all_coarse = labels[:, :planes], labels[:, planes:]
    all_box = jnp.where(all_ids >= 0, all_ids // planes, -1)
    all_coarse_box = all_coarse // coarse_planes
    flat_parents = jnp.where(all_ids >= 0, all_ids // 2, -1).reshape(-1)

    def needed(coarse):
        kept = jnp.sum((flat_parents == coarse[..., None]).astype(i32), axis=-1)
        return kept < 2

    box = jnp.arange(lanes) % devices
    fine_units = jnp.sum((all_box[:, None, :] == box[None, :, None]).astype(i32), axis=-1)
    asked = needed(all_coarse)[:, None, :] & (all_coarse_box[:, None, :] == box[None, :, None])
    units = 2 * fine_units + jnp.max(asked.astype(i32), axis=-1)
    row, column = pl.pallas_call(
        plan_kernel,
        out_shape=[jax.ShapeDtypeStruct((8, lanes), i32), jax.ShapeDtypeStruct((devices, lanes), i32)],
        in_specs=[SMEM, VMEM],
        out_specs=[VMEM] * 2,
        name="plan",
    )(me_ref, units)
    left = jnp.max(row[EXTRA, :devices]).reshape(1)

    own_box = jnp.where(own >= 0, own // planes, -1)
    send_fine = jnp.where(own >= 0, own_box * FINE_CAP + ranks(own_box), -1)
    own_coarse_box = own_coarse // coarse_planes
    before = jnp.sum((own_box[None, :] == own_coarse_box[:, None]).astype(i32), axis=1)
    send_coarse = (own_coarse_box * unit_count + 2 * before) * 2 + ranks(own_coarse_box)
    send_coarse = jnp.where(needed(own_coarse), send_coarse, -1)

    order = jnp.arange(devices)[:, None]
    wanted = me * planes + jnp.arange(planes)
    fine_at = jnp.where(all_ids[None] == wanted[:, None, None], (order * FINE_CAP + ranks(all_box))[None], -1)
    fine_at = jnp.max(fine_at, axis=(1, 2))
    to_me = jnp.sum((all_box == me).astype(i32), axis=1, keepdims=True)
    coarse_wanted = me * coarse_planes + jnp.arange(coarse_planes)
    coarse_code = (order * unit_count + 2 * to_me) * 2 + ranks(all_coarse_box)
    coarse_at = jnp.where(all_coarse[None] == coarse_wanted[:, None, None], coarse_code[None], 0)
    coarse_at = jnp.max(coarse_at, axis=(1, 2))

    def exchange(value):
        return lax.all_to_all(value, "dev", split_axis=0, concat_axis=0, tiled=True)

    def pack(count, first, name):
        return pl.pallas_call(
            functools.partial(pack_kernel, devices, first),
            out_shape=units_shape(count),
            in_specs=[SMEM] * 4 + [ANY, VMEM],
            out_specs=VMEM,
            scratch_shapes=[pltpu.VMEM(old_fine.shape, f32), pltpu.SemaphoreType.DMA((4,))],
            compiler_params=PARAMS,
            name=name,
        )(me_ref, send_fine, send_coarse, row, old_fine, old_coarse)

    packed = pack(devices * DIRECT, True, "pack")

    def no_rest():
        return pl.pallas_call(empty_kernel, out_shape=units_shape(devices * EXTRA), out_specs=ANY, name="nothing")()

    def rest_direct():
        return exchange(pack(devices * EXTRA, False, "pack_rest"))

    rest = lax.cond(left[0] == 0, no_rest, rest_direct)
    packed, rest, flow = lax.optimization_barrier((packed, rest, velocity))
    first = exchange(packed)

    def edge_shapes(deep, count):
        along_y = jax.ShapeDtypeStruct((deep * count * planes, lanes), f32)
        along_x = jax.ShapeDtypeStruct((deep * count * rows, lanes), f32)
        return [along_y, along_y, along_x, along_x]

    directions = flow.shape[1]
    vylow, vyhigh, vxlow, vxhigh = pl.pallas_call(
        functools.partial(velocity_edges_kernel, shape=flow.shape),
        out_shape=edge_shapes(1, directions),
        in_specs=[VMEM],
        out_specs=[VMEM] * 4,
        compiler_params=PARAMS,
        name="velocity_edges",
    )(flow.reshape(planes * directions * rows, lanes))
    flow_edges = [*neighbours("grp", vylow, vyhigh), *neighbours("dev", vxlow, vxhigh)]
    first, *flow_edges = lax.optimization_barrier((first, *flow_edges))
    second = pl.pallas_call(
        forward_kernel,
        out_shape=units_shape(devices),
        in_specs=[SMEM] * 2 + [ANY],
        out_specs=VMEM,
        scratch_shapes=[pltpu.SemaphoreType.DMA((devices,))],
        compiler_params=PARAMS,
        cost_estimate=cost(3),
        name="forward",
    )(me_ref, column, first)
    second = exchange(second)

    size = species * rows
    state_shape = jax.ShapeDtypeStruct((planes * size, lanes), f32)
    state, *edges = pl.pallas_call(
        functools.partial(build_kernel, old_fine.shape),
        out_shape=[state_shape] + edge_shapes(ITERS, species),
        in_specs=[SMEM] * 2 + [VMEM],
        out_specs=[VMEM] * 5,
        compiler_params=PARAMS,
        cost_estimate=cost(10),
        name="build",
    )(fine_at, coarse_at, first)
    relay_of = (jnp.arange(devices)[:, None] + me + column[:, :EXTRA] // 8) % devices

    def through(source, unit, used):
        over = jnp.arange(EXTRA) == (unit - DIRECT)[:, None]
        hit = (source[:, None, None] == jnp.arange(devices)[None, :, None]) & over[:, None, :]
        relay = jnp.max(jnp.where(hit, relay_of[None], -1), axis=(1, 2))
        return jnp.where(used & (unit >= DIRECT), relay, -1)

    order = jnp.arange(devices)
    halves = jnp.arange(2 * planes)
    at = jnp.repeat(fine_at, 2)
    relay = through(at // FINE_CAP, 2 * (at % FINE_CAP) + halves % 2, at >= 0)
    late_fine = jnp.max(jnp.where(relay[:, None] == order[None], halves[:, None], -1), axis=0)
    parents = jnp.arange(coarse_planes)
    code = coarse_at // 2
    fresh = jnp.min(fine_at.reshape(coarse_planes, 2), axis=1) < 0
    relay = through(code // unit_count, code % unit_count, fresh)
    late_parents = [
        jnp.max(jnp.where((relay[:, None] == order[None]) & (coarse_at % 2 == j)[:, None], parents[:, None], -1), axis=0)
        for j in range(COARSE_CAP)
    ]
    late = jnp.concatenate([late_fine, *late_parents])
    late_scratch = [
        pltpu.VMEM((1, species, half, lanes), f32),
        pltpu.VMEM((species, rows, lanes), f32),
        pltpu.SemaphoreType.DMA,
    ]
    ylow_own, yhigh_own, xlow_own, xhigh_own = pl.pallas_call(
        functools.partial(edges_kernel, old_fine.shape),
        out_shape=edge_shapes(ITERS, species),
        in_specs=[SMEM] * 4 + [VMEM, ANY] + [VMEM] * 4,
        out_specs=[VMEM] * 4,
        scratch_shapes=late_scratch,
        compiler_params=PARAMS,
        cost_estimate=cost(4),
        name="edges",
    )(late, left, fine_at, coarse_at, second, rest, *edges)
    ylow, yhigh = neighbours("grp", ylow_own, yhigh_own)
    state_scratch = pltpu.VMEM(state_shape.shape, f32)
    group_sems = pltpu.SemaphoreType.DMA((planes // UNROLL,))
    stepped = pl.pallas_call(
        functools.partial(first_step_kernel, old_fine.shape),
        out_shape=state_shape,
        in_specs=[SMEM] * 5 + [VMEM, ANY, ANY, VMEM],
        out_specs=ANY,
        scratch_shapes=[state_scratch] * 2 + late_scratch + [group_sems],
        compiler_params=PARAMS,
        cost_estimate=cost(10),
        name="first_step",
    )(late, left, fine_at, coarse_at, diffusion, second, rest, state, velocity)
    ylow, yhigh, stepped = lax.optimization_barrier((ylow, yhigh, stepped))
    message = jax.ShapeDtypeStruct((ITERS * size + 32, lanes), f32)
    down, up = pl.pallas_call(
        functools.partial(corners_kernel, planes, species),
        out_shape=[message] * 2,
        in_specs=[VMEM] * 4,
        out_specs=[VMEM] * 2,
        compiler_params=PARAMS,
        name="corners",
    )(ylow, yhigh, xlow_own, xhigh_own)
    xlow, xhigh = neighbours("dev", down, up)
    grp, dev = lax.axis_index("grp"), lax.axis_index("dev")
    inside = jnp.stack([grp > 0, grp < lax.axis_size("grp") - 1, dev > 0, dev < devices - 1]).astype(f32)
    row_edge = pltpu.VMEM((species * planes, lanes), f32)
    plane_edge = pltpu.VMEM((size, lanes), f32)
    done = pl.pallas_call(
        functools.partial(second_step_kernel, old_fine.shape),
        out_shape=state_shape,
        in_specs=[SMEM] * 2 + [ANY] + [VMEM] * 15,
        out_specs=ANY,
        scratch_shapes=[state_scratch] * 2
        + [row_edge] * 2
        + [plane_edge] * 2
        + [pltpu.SemaphoreType.DMA, group_sems],
        compiler_params=PARAMS,
        cost_estimate=cost(10),
        name="second_step",
    )(
        inside, diffusion, stepped, velocity, ylow_own, yhigh_own, xlow_own, xhigh_own, ylow, yhigh, xlow, xhigh,
        vylow, vyhigh, *flow_edges,
    )
    return done.reshape(old_fine.shape)


def solution(mesh):
    in_specs = (
        P("dev", None, "grp", None),
        P("grp", "dev"),
        P("dev", None, "grp", None),
        P("grp", "dev"),
        P("dev", None, "grp", None),
        P(),
    )
    out_specs = P("dev", None, "grp", None)
    return jax.shard_map(
        on_device, mesh=mesh, in_specs=in_specs, out_specs=out_specs, check_vma=False
    )
```

```python
import functools

import jax
import jax.numpy as jnp
from jax import lax
from jax.experimental import pallas as pl
from jax.experimental.pallas import tpu as pltpu
from jax.sharding import PartitionSpec as P

ITERS = 2
FINE_CAP = 4
COARSE_CAP = 2
DIRECT = 5
EXTRA = 2 * FINE_CAP + 1 - DIRECT
VMEM = pl.BlockSpec(memory_space=pltpu.VMEM)
SMEM = pl.BlockSpec(memory_space=pltpu.SMEM)
ANY = pl.BlockSpec(memory_space=pl.ANY)
PARAMS = pltpu.CompilerParams(vmem_limit_bytes=56 * 1024 * 1024)
UNROLL = 4


def ranks(boxes):
    count = boxes.shape[-1]
    earlier = jnp.arange(count)[None, :] < jnp.arange(count)[:, None]
    same = boxes[..., None, :] == boxes[..., :, None]
    return jnp.sum((same & earlier).astype(jnp.int32), axis=-1)


def plan_kernel(me_ref, units_ref, row_ref, column_ref):
    devices, lanes = units_ref.shape
    me = me_ref[0]
    units = units_ref[...]
    source = lax.broadcasted_iota(jnp.int32, units.shape, 0)
    lane = lax.broadcasted_iota(jnp.int32, units.shape, 1)
    surplus = pltpu.roll(jnp.maximum(units - DIRECT, 0), 0, 1, stride=1, stride_axis=0)
    none = jnp.full(units.shape, -1, jnp.int32)

    def one_round(r, carry):
        left, free, second, through, *chosen = carry
        ok = (left > 0) & (free > 0) & (second > 0)
        position = DIRECT - free
        item = surplus - left
        chosen = [jnp.where(ok & (item == i), r * 8 + position, table) for i, table in enumerate(chosen)]
        through = jnp.where(ok, source * 8 + position, through)
        used = ok.astype(jnp.int32)
        left, free, second = left - used, free - used, second - used
        free = pltpu.roll(free, lanes - 1, 1)
        second = pltpu.roll(pltpu.roll(second, devices - 1, 0), lanes - 1, 1)
        through = pltpu.roll(pltpu.roll(through, devices - 1, 0), lanes - 1, 1)
        return (left, free, second, through, *chosen)

    init = (surplus, jnp.maximum(DIRECT - units, 0), jnp.ones(units.shape, jnp.int32), none) + (none,) * EXTRA
    left, _, _, through, *chosen = lax.fori_loop(0, devices, one_round, init)
    for i in range(EXTRA):
        row_ref[i : i + 1] = jnp.max(jnp.where(source == me, chosen[i], -1), axis=0, keepdims=True)
    row_ref[EXTRA : EXTRA + 1] = jnp.max(left, axis=0, keepdims=True)
    column = none
    for i in range(EXTRA):
        mine = (lane < devices) & (lane == (source + me) % devices)
        found = jnp.max(jnp.where(mine, chosen[i], -1), axis=1, keepdims=True)
        column = jnp.where(lane == i, found, column)
    found = jnp.max(jnp.where(lane == me, through, -1), axis=1, keepdims=True)
    column_ref[...] = jnp.where(lane == EXTRA, found, column)


def pack_kernel(
    devices, first, me_ref, fine_at_ref, coarse_at_ref, row_ref, fine_in_ref, coarse_ref, out_ref, fine_ref, sem
):
    planes = fine_ref.shape[0]
    coarse_planes, _, half, depth = coarse_ref.shape
    part = planes // sem.shape[0]

    def bring(i):
        planes_of = pl.ds(i * part, part)
        return pltpu.make_async_copy(fine_in_ref.at[planes_of], fine_ref.at[planes_of], sem.at[i])

    def slot_of(box, unit):
        if first:
            return first_slot(devices, me_ref[0], row_ref, box, unit)
        return jnp.where(unit < DIRECT, -1, box * EXTRA + unit - DIRECT)

    for i in range(sem.shape[0]):
        bring(i).start()

    def coarse_plane(k, carry):
        code = coarse_at_ref[k]

        @pl.when(code >= 0)
        def _():
            at = code // 2
            slot = slot_of(at // (DIRECT + EXTRA), at % (DIRECT + EXTRA))
            for j in range(2):

                @pl.when((slot >= 0) & (code % 2 == j))
                def _():
                    out_ref[slot, :, :, j * depth : (j + 1) * depth] = coarse_ref[k]

        return carry

    lax.fori_loop(0, coarse_planes, coarse_plane, 0)

    def fine_plane(k, carry):
        code = fine_at_ref[k]
        box, rank = code // FINE_CAP, code % FINE_CAP
        whole = DIRECT // 2

        if first:

            @pl.when((code >= 0) & (rank < whole))
            def _():
                for h in range(2):
                    out_ref[box * DIRECT + 2 * rank + h] = fine_ref[k, :, h * half : (h + 1) * half, :]

        @pl.when((code >= 0) & (rank >= whole))
        def _():
            for h in range(2):
                slot = slot_of(box, 2 * rank + h)

                @pl.when(slot >= 0)
                def _():
                    out_ref[slot] = fine_ref[k, :, h * half : (h + 1) * half, :]

        return carry

    for i in range(sem.shape[0]):
        bring(i).wait()
        lax.fori_loop(i * part, (i + 1) * part, fine_plane, 0)


def first_slot(devices, me, row_ref, box, unit):
    t = (me + box) % devices
    code = row_ref[jnp.maximum(unit - DIRECT, 0), t]
    relay = jnp.where(code >= 0, ((t + code // 8) % devices) * DIRECT + code % 8, -1)
    return jnp.where(unit < DIRECT, box * DIRECT + unit, relay)


def forward_kernel(me_ref, column_ref, in_ref, out_ref, sem):
    devices = out_ref.shape[0]

    def each(act):
        def body(a, carry):
            code = column_ref[a, EXTRA]

            @pl.when(code >= 0)
            def _():
                box = (me_ref[0] - a + devices) % devices
                act(pltpu.make_async_copy(in_ref.at[(code // 8) * DIRECT + code % 8], out_ref.at[box], sem.at[a]))

            return carry

        lax.fori_loop(0, devices, body, 0)

    each(lambda copy: copy.start())
    each(lambda copy: copy.wait())


def rows_to_edges(flat_ref, edge_ref, offset, row, planes, species, rows):
    for s in range(species):
        for x in range(0, planes, 8):
            at = offset + s * planes + x
            edge_ref[at : at + 8] = flat_ref[pl.ds((x * species + s) * rows + row, 8, stride=species * rows), :]


def interpolate(ref, slot, part, store):
    _, species, half, lanes = ref.shape
    lane = lax.broadcasted_iota(jnp.int32, (half, lanes), 1)
    row = lax.broadcasted_iota(jnp.int32, (half, lanes), 0)
    sign = jnp.where(lane % 2 == 0, -0.25, 0.25)
    lane_first = lane % (lanes // 2) == 0
    lane_last = lane % (lanes // 2) == lanes // 2 - 1
    index = part * (lanes // 2) + lane // 2
    for s in range(species):
        p = ref[slot, s]
        below = jnp.where(row == 0, p, pltpu.roll(p, 1, 0))
        above = jnp.where(row == half - 1, p, pltpu.roll(p, half - 1, 0))
        left = jnp.where(lane_first, p, pltpu.roll(p, 1, 1))
        right = jnp.where(lane_last, p, pltpu.roll(p, lanes - 1, 1))
        slope_y = 0.125 * (above - below)
        slope_z = 0.5 * (right - left)
        gz = jnp.take_along_axis(slope_z, index, axis=1) * sign
        even = jnp.take_along_axis(p - slope_y, index, axis=1) + gz
        odd = jnp.take_along_axis(p + slope_y, index, axis=1) + gz
        store(s, even, odd)


def build_kernel(shape, fine_at_ref, coarse_at_ref, first_ref, out_ref, ylow_ref, yhigh_ref, xlow_ref, xhigh_ref):
    planes, species, rows, lanes = shape
    half = rows // 2

    def body(c, carry):
        at = [fine_at_ref[2 * c], fine_at_ref[2 * c + 1]]
        code = coarse_at_ref[c]
        unit = code // 2 % (DIRECT + EXTRA)

        @pl.when(((at[0] < 0) | (at[1] < 0)) & (unit < DIRECT))
        def _():
            def store(s, even, odd):
                for child in range(2):
                    base = pl.multiple_of(((2 * c + child) * species + s) * rows, rows)
                    out_ref[pl.ds(base, half, stride=2), :] = even
                    out_ref[pl.ds(base + 1, half, stride=2), :] = odd

            interpolate(first_ref, code // 2 // (DIRECT + EXTRA) * DIRECT + unit, code % 2, store)

        for child in range(2):
            for h in range(2):
                late = 2 * (at[child] % FINE_CAP) + h

                @pl.when((at[child] >= 0) & (late < DIRECT))
                def _():
                    slot = at[child] // FINE_CAP * DIRECT + late
                    for s in range(species):
                        base = pl.multiple_of(((2 * c + child) * species + s) * rows + h * half, half)
                        out_ref[pl.ds(base, half), :] = first_ref[slot, s]

        return carry

    lax.fori_loop(0, planes // 2, body, 0)
    for r in range(ITERS):
        rows_to_edges(out_ref, ylow_ref, r * species * planes, r, planes, species, rows)
        rows_to_edges(out_ref, yhigh_ref, r * species * planes, rows - ITERS + r, planes, species, rows)
    deep = ITERS * species * rows
    xlow_ref[...] = out_ref[0:deep]
    xhigh_ref[...] = out_ref[planes * species * rows - deep : planes * species * rows]


def late_units(shape, late_ref, left_ref, fine_at_ref, coarse_at_ref, second_ref, rest_ref, held_ref,
               plane_ref, sem, half_plane, whole_plane):
    planes, _, rows, _ = shape
    half = rows // 2
    planned = left_ref[0] == 0

    def children(c, ref, slot):
        def store(s, even, odd):
            plane_ref[s, pl.ds(0, half, stride=2), :] = even
            plane_ref[s, pl.ds(1, half, stride=2), :] = odd

        interpolate(ref, slot, coarse_at_ref[c] % 2, store)
        for child in range(2):

            @pl.when(fine_at_ref[2 * c + child] < 0)
            def _():
                whole_plane(2 * c + child)

    def from_relay(m, carry):
        what = late_ref[m]

        @pl.when((what >= 0) & (what < 2 * planes))
        def _():
            for h in range(2):

                @pl.when(what % 2 == h)
                def _():
                    half_plane(what // 2, h, second_ref, m)

        for more in range(2):
            parent = late_ref[(1 + more) * late_ref.shape[0] // 3 + m]

            @pl.when(parent >= 0)
            def _():
                children(parent, second_ref, m)

        return carry

    @pl.when(planned)
    def _():
        lax.fori_loop(0, second_ref.shape[0], from_relay, 0)

    def bring(source, unit):
        copy = pltpu.make_async_copy(
            rest_ref.at[pl.ds(source * EXTRA + jnp.maximum(unit - DIRECT, 0), 1)], held_ref, sem
        )
        copy.start()
        copy.wait()

    def direct(c, carry):
        code = coarse_at_ref[c]
        unit = code // 2 % (DIRECT + EXTRA)

        @pl.when(((fine_at_ref[2 * c] < 0) | (fine_at_ref[2 * c + 1] < 0)) & (unit >= DIRECT))
        def _():
            bring(code // 2 // (DIRECT + EXTRA), unit)
            children(c, held_ref, 0)

        for x in (2 * c, 2 * c + 1):
            at = fine_at_ref[x]
            for h in range(2):
                late = 2 * (at % FINE_CAP) + h

                @pl.when((at >= 0) & (late >= DIRECT))
                def _():
                    bring(at // FINE_CAP, late)
                    half_plane(x, h, held_ref, 0)

        return carry

    @pl.when(jnp.logical_not(planned))
    def _():
        lax.fori_loop(0, planes // 2, direct, 0)


def edges_kernel(
    shape, late_ref, left_ref, fine_at_ref, coarse_at_ref, second_ref, rest_ref,
    ylow_in_ref, yhigh_in_ref, xlow_in_ref, xhigh_in_ref,
    ylow_ref, yhigh_ref, xlow_ref, xhigh_ref, held_ref, plane_ref, sem,
):
    planes, species, rows, _ = shape
    half = rows // 2
    size = species * rows
    ylow_ref[...] = ylow_in_ref[...]
    yhigh_ref[...] = yhigh_in_ref[...]
    xlow_ref[...] = xlow_in_ref[...]
    xhigh_ref[...] = xhigh_in_ref[...]

    def half_edges(x, h, value):
        edge_ref, first = ((ylow_ref, 0), (yhigh_ref, half - ITERS))[h]
        for s in range(species):
            for r in range(ITERS):
                edge_ref[pl.ds((r * species + s) * planes + x, 1), :] = value(s, slice(first + r, first + r + 1))
        for near, xedge_ref, at in ((x < ITERS, xlow_ref, x), (x >= planes - ITERS, xhigh_ref, x - planes + ITERS)):

            @pl.when(near)
            def _():
                for s in range(species):
                    base = pl.multiple_of(at * size + s * rows + h * half, half)
                    xedge_ref[pl.ds(base, half), :] = value(s, slice(0, half))

    def half_plane(x, h, ref, slot):
        half_edges(x, h, lambda s, part: ref[slot, s, part])

    def whole_plane(x):
        for h in range(2):
            half_edges(x, h, lambda s, part: plane_ref[s, h * half + part.start : h * half + part.stop])

    late_units(
        shape, late_ref, left_ref, fine_at_ref, coarse_at_ref, second_ref, rest_ref, held_ref, plane_ref,
        sem, half_plane, whole_plane,
    )


def corners_kernel(planes, species, ylow_ref, yhigh_ref, xlow_ref, xhigh_ref, down_ref, up_ref):
    deep = xlow_ref.shape[0]
    down_ref[0:deep] = xlow_ref[...]
    up_ref[0:deep] = xhigh_ref[...]
    for message_ref, x in ((down_ref, 0), (up_ref, planes - 1)):
        for s in range(species):
            low = ((ITERS - 1) * species + s) * planes + x
            high = s * planes + x
            message_ref[deep + s : deep + s + 1] = ylow_ref[low : low + 1]
            message_ref[deep + 16 + s : deep + 16 + s + 1] = yhigh_ref[high : high + 1]
        for at in (deep + species, deep + 16 + species):
            message_ref[at : at + 16 - species] = jnp.zeros((16 - species, message_ref.shape[1]), jnp.float32)


def velocity_edges_kernel(vel_ref, ylow_ref, yhigh_ref, xlow_ref, xhigh_ref, *, shape):
    planes, directions, rows, _ = shape
    size = directions * rows
    rows_to_edges(vel_ref, ylow_ref, 0, 0, planes, directions, rows)
    rows_to_edges(vel_ref, yhigh_ref, 0, rows - 1, planes, directions, rows)
    xlow_ref[...] = vel_ref[0:size]
    xhigh_ref[...] = vel_ref[(planes - 1) * size : planes * size]


class Flow:
    def __init__(self, velocity):
        self.positive = [jnp.maximum(v, 0.0) for v in velocity]
        self.negative = [jnp.minimum(v, 0.0) for v in velocity]
        self.keep = 1.0
        for low, high in zip(self.positive, self.negative):
            self.keep = self.keep - (low - high)

    def step(self, u, neighbours, d):
        new = u * (self.keep - 6.0 * d)
        for k, (low, high) in enumerate(neighbours):
            new = new + low * (d + self.positive[k]) + high * (d - self.negative[k])
        return new


def along(u, first, last, dim):
    count = u.shape[dim]
    at = lax.broadcasted_iota(jnp.int32, u.shape, dim)
    low = jnp.where(at == 0, first, pltpu.roll(u, 1, dim))
    high = jnp.where(at == count - 1, last, pltpu.roll(u, count - 1, dim))
    return low, high


def advance_plane(diff_ref, velocity, center, below, above, y_low, y_high, store):
    flow = Flow(velocity)
    for s in range(diff_ref.shape[0]):
        u = center(s)
        sides = ((below(s), above(s)), along(u, y_low(s), y_high(s), 0), along(u, u, u, 1))
        store(s, flow.step(u, sides, diff_ref[s]))


def planes_of(ref, x, rows, size):
    return lambda s: ref[pl.ds(pl.multiple_of(x * size + s * rows, rows), rows), :]


def advance(shape, diff_ref, vel_ref, u_ref, new_ref, low, high, y_low, y_high, after):
    planes, species, rows, _ = shape
    size = species * rows

    def group(x, first, last):
        for i in range(UNROLL):

            def store(s, new):
                new_ref[pl.ds(pl.multiple_of((x + i) * size + s * rows, rows), rows), :] = new

            advance_plane(
                diff_ref,
                [vel_ref[x + i, k] for k in range(3)],
                planes_of(u_ref, x + i, rows, size),
                low if first and i == 0 else planes_of(u_ref, x + i - 1, rows, size),
                high if last and i == UNROLL - 1 else planes_of(u_ref, x + i + 1, rows, size),
                y_low(x + i),
                y_high(x + i),
                store,
            )
        after(x // UNROLL)

    def body(g, carry):
        group(g * UNROLL, False, False)
        return carry

    group(0, True, False)
    lax.fori_loop(1, planes // UNROLL - 1, body, 0)
    group(planes - UNROLL, False, True)


def send_group(shape, from_ref, to_ref, sem, g):
    size = UNROLL * shape[1] * shape[2]
    part = pl.ds(pl.multiple_of(g * size, size), size)
    return pltpu.make_async_copy(from_ref.at[part], to_ref.at[part], sem.at[g])


def finish_groups(shape, from_ref, to_ref, sem):
    def finish(g, carry):
        send_group(shape, from_ref, to_ref, sem, g).wait()
        return carry

    lax.fori_loop(0, shape[0] // UNROLL, finish, 0)


def nothing(s):
    return 0.0


def first_step_kernel(shape, diff_ref, state_ref, vel_ref, out_ref, u0_ref, u1_ref, in_sem, out_sem):
    for g in range(shape[0] // UNROLL):
        send_group(shape, state_ref, u0_ref, in_sem, g).start()
    finish_groups(shape, state_ref, u0_ref, in_sem)
    advance(
        shape, diff_ref, vel_ref, u0_ref, u1_ref, nothing, nothing, lambda x: nothing, lambda x: nothing,
        lambda g: send_group(shape, u1_ref, out_ref, out_sem, g).start(),
    )
    finish_groups(shape, u1_ref, out_ref, out_sem)


def late_step_kernel(
    shape, late_ref, left_ref, fine_at_ref, coarse_at_ref, again_ref, diff_ref, second_ref, rest_ref, state_ref, vel_ref, _,
    out_ref, u0_ref, u1_ref, held_ref, plane_ref, sem, out_sem,
):
    planes, species, rows, lanes = shape
    half = rows // 2
    size = species * rows
    copy = pltpu.make_async_copy(state_ref, u0_ref.at[size : size + planes * size], sem)
    copy.start()
    u0_ref[0:size] = jnp.zeros((size, lanes), jnp.float32)
    u0_ref[size + planes * size : 2 * size + planes * size] = jnp.zeros((size, lanes), jnp.float32)
    copy.wait()

    def half_plane(x, h, ref, slot):
        for s in range(species):
            base = pl.multiple_of((x + 1) * size + s * rows + h * half, half)
            u0_ref[pl.ds(base, half), :] = ref[slot, s]

    def whole_plane(x):
        for s in range(species):
            u0_ref[pl.ds(pl.multiple_of((x + 1) * size + s * rows, rows), rows), :] = plane_ref[s]

    late_units(
        shape, late_ref, left_ref, fine_at_ref, coarse_at_ref, second_ref, rest_ref, held_ref, plane_ref,
        sem, half_plane, whole_plane,
    )

    def send(x):
        part = pl.ds(pl.multiple_of(x * size, size), size)
        return pltpu.make_async_copy(u1_ref.at[part], out_ref.at[part], out_sem.at[x])

    def take(x, carry):
        @pl.when(again_ref[x] > 0)
        def _():
            def store(s, new):
                u1_ref[pl.ds(pl.multiple_of(x * size + s * rows, rows), rows), :] = new

            around = [planes_of(u0_ref, x + 1 + i, rows, size) for i in (0, -1, 1)]
            advance_plane(diff_ref, [vel_ref[x, k] for k in range(3)], *around, nothing, nothing, store)
            send(x).start()

        return carry

    lax.fori_loop(0, planes, take, 0)

    def finish(x, carry):
        @pl.when(again_ref[x] > 0)
        def _():
            send(x).wait()

        return carry

    lax.fori_loop(0, planes, finish, 0)


def second_step_kernel(
    shape, inside_ref, diff_ref, first_ref, vel_ref, ylow_own_ref, yhigh_own_ref, xlow_own_ref, xhigh_own_ref, ylow_ref,
    yhigh_ref, xlow_ref, xhigh_ref, vylow_own_ref, vyhigh_own_ref, vylow_ref, vyhigh_ref, vxlow_ref, vxhigh_ref,
    out_ref, u1_ref, u2_ref, row_low_ref, row_high_ref, plane_low_ref, plane_high_ref, sem, out_sem,
):
    planes, species, rows, lanes = shape
    size = species * rows
    deep = ITERS * size
    copy = pltpu.make_async_copy(first_ref, u1_ref, sem)
    copy.start()

    for (near_ref, near, far, own_ref, own, v_ref, corner, target_ref, inside) in (
        (ylow_ref, 1, 0, ylow_own_ref, 0, vylow_ref, deep, row_low_ref, 0),
        (yhigh_ref, 0, 1, yhigh_own_ref, 1, vyhigh_ref, deep + 16, row_high_ref, 1),
    ):
        for x in range(0, planes, 16):
            flow = Flow([v_ref[k * planes + x : k * planes + x + 16] for k in range(3)])
            for s in range(species):

                def band(ref, r):
                    start = (r * species + s) * planes + x
                    return ref[start : start + 16]

                u = band(near_ref, near)
                start = (near * species + s) * planes
                if x == 0:
                    first = xlow_ref[corner + s : corner + s + 1]
                else:
                    first = near_ref[start + x - 1 : start + x]
                if x + 16 == planes:
                    last = xhigh_ref[corner + s : corner + s + 1]
                else:
                    last = near_ref[start + x + 16 : start + x + 17]
                outer, inner = band(near_ref, far), band(own_ref, own)
                across = (outer, inner) if inside == 0 else (inner, outer)
                new = flow.step(u, (along(u, first, last, 0), across, along(u, u, u, 1)), diff_ref[s])
                target_ref[s * planes + x : s * planes + x + 16] = new * inside_ref[inside]

    def at(ref, x):
        return planes_of(ref, x, rows, size)

    for (halo_ref, near, below, above, v_ref, target_ref, inside) in (
        (xlow_ref, 1, at(xlow_ref, 0), at(xlow_own_ref, 0), vxlow_ref, plane_low_ref, 2),
        (xhigh_ref, 0, at(xhigh_own_ref, ITERS - 1), at(xhigh_ref, 1), vxhigh_ref, plane_high_ref, 3),
    ):

        def store(s, new):
            target_ref[s * rows : (s + 1) * rows] = new * inside_ref[inside]

        def corner(offset):
            return lambda s: halo_ref[deep + offset + s : deep + offset + s + 1]

        velocity = [v_ref[k * rows : (k + 1) * rows] for k in range(3)]
        advance_plane(diff_ref, velocity, at(halo_ref, near), below, above, corner(0), corner(16), store)

    copy.wait()
    for x in range(0, planes, 8):
        up = jnp.maximum(vylow_own_ref[planes + x : planes + x + 8], 0.0)
        down = jnp.minimum(vyhigh_own_ref[planes + x : planes + x + 8], 0.0)
        for s in range(species):
            low = pl.ds((x * species + s) * rows, 8, stride=size)
            high = pl.ds((x * species + s) * rows + rows - 1, 8, stride=size)
            start = species * planes + s * planes + x
            u1_ref[low, :] = u1_ref[low, :] + (diff_ref[s] + up) * ylow_ref[start : start + 8]
            start = s * planes + x
            u1_ref[high, :] = u1_ref[high, :] + (diff_ref[s] - down) * yhigh_ref[start : start + 8]
    up = jnp.maximum(vel_ref[0, 0], 0.0)
    down = jnp.minimum(vel_ref[planes - 1, 0], 0.0)
    for s in range(species):
        low = slice(s * rows, (s + 1) * rows)
        high = slice((planes - 1) * size + s * rows, (planes - 1) * size + (s + 1) * rows)
        u1_ref[low] = u1_ref[low] + (diff_ref[s] + up) * at(xlow_ref, 1)(s)
        u1_ref[high] = u1_ref[high] + (diff_ref[s] - down) * at(xhigh_ref, 0)(s)

    def edge(ref):
        return lambda x: lambda s: ref[pl.ds(s * planes + x, 1), :]

    advance(
        shape, diff_ref, vel_ref, u1_ref, u2_ref, at(plane_low_ref, 0), at(plane_high_ref, 0), edge(row_low_ref),
        edge(row_high_ref), lambda g: send_group(shape, u2_ref, out_ref, out_sem, g).start(),
    )
    finish_groups(shape, u2_ref, out_ref, out_sem)


def empty_kernel(out_ref):
    pass


def cost(microseconds):
    return pl.CostEstimate(flops=0, bytes_accessed=int(microseconds * 3.6e6), transcendentals=0)


def neighbours(axis, low, high):
    size = lax.axis_size(axis)
    up = [(i, (i + 1) % size) for i in range(size - 1)]
    return lax.ppermute(high, axis, up), lax.ppermute(low, axis, [(b, a) for a, b in up])


def on_device(old_fine, old_ids, old_coarse, coarse_ids, velocity, diffusion):
    devices = lax.axis_size("dev")
    me = lax.axis_index("dev")
    me_ref = me.reshape(1).astype(jnp.int32)
    planes, species, rows, lanes = old_fine.shape
    half = rows // 2
    coarse_planes = old_coarse.shape[0]
    unit_count = DIRECT + EXTRA
    f32 = jnp.float32
    i32 = jnp.int32

    def units_shape(count):
        return jax.ShapeDtypeStruct((count, species, half, lanes), f32)

    own, own_coarse = old_ids[0], coarse_ids[0]
    labels = jnp.broadcast_to(jnp.concatenate([own, own_coarse])[None], (devices, planes + coarse_planes))
    labels = lax.all_to_all(labels, "dev", split_axis=0, concat_axis=0, tiled=True)
    all_ids, all_coarse = labels[:, :planes], labels[:, planes:]
    all_box = jnp.where(all_ids >= 0, all_ids // planes, -1)
    all_coarse_box = all_coarse // coarse_planes
    flat_parents = jnp.where(all_ids >= 0, all_ids // 2, -1).reshape(-1)

    def needed(coarse):
        kept = jnp.sum((flat_parents == coarse[..., None]).astype(i32), axis=-1)
        return kept < 2

    box = jnp.arange(lanes) % devices
    fine_units = jnp.sum((all_box[:, None, :] == box[None, :, None]).astype(i32), axis=-1)
    asked = needed(all_coarse)[:, None, :] & (all_coarse_box[:, None, :] == box[None, :, None])
    units = 2 * fine_units + jnp.max(asked.astype(i32), axis=-1)
    row, column = pl.pallas_call(
        plan_kernel,
        out_shape=[jax.ShapeDtypeStruct((8, lanes), i32), jax.ShapeDtypeStruct((devices, lanes), i32)],
        in_specs=[SMEM, VMEM],
        out_specs=[VMEM] * 2,
        name="plan",
    )(me_ref, units)
    left = jnp.max(row[EXTRA, :devices]).reshape(1)

    own_box = jnp.where(own >= 0, own // planes, -1)
    send_fine = jnp.where(own >= 0, own_box * FINE_CAP + ranks(own_box), -1)
    own_coarse_box = own_coarse // coarse_planes
    before = jnp.sum((own_box[None, :] == own_coarse_box[:, None]).astype(i32), axis=1)
    send_coarse = (own_coarse_box * unit_count + 2 * before) * 2 + ranks(own_coarse_box)
    send_coarse = jnp.where(needed(own_coarse), send_coarse, -1)

    order = jnp.arange(devices)[:, None]
    wanted = me * planes + jnp.arange(planes)
    fine_at = jnp.where(all_ids[None] == wanted[:, None, None], (order * FINE_CAP + ranks(all_box))[None], -1)
    fine_at = jnp.max(fine_at, axis=(1, 2))
    to_me = jnp.sum((all_box == me).astype(i32), axis=1, keepdims=True)
    coarse_wanted = me * coarse_planes + jnp.arange(coarse_planes)
    coarse_code = (order * unit_count + 2 * to_me) * 2 + ranks(all_coarse_box)
    coarse_at = jnp.where(all_coarse[None] == coarse_wanted[:, None, None], coarse_code[None], 0)
    coarse_at = jnp.max(coarse_at, axis=(1, 2))

    def exchange(value):
        return lax.all_to_all(value, "dev", split_axis=0, concat_axis=0, tiled=True)

    def pack(count, first, name):
        return pl.pallas_call(
            functools.partial(pack_kernel, devices, first),
            out_shape=units_shape(count),
            in_specs=[SMEM] * 4 + [ANY, VMEM],
            out_specs=VMEM,
            scratch_shapes=[pltpu.VMEM(old_fine.shape, f32), pltpu.SemaphoreType.DMA((4,))],
            compiler_params=PARAMS,
            name=name,
        )(me_ref, send_fine, send_coarse, row, old_fine, old_coarse)

    packed = pack(devices * DIRECT, True, "pack")

    def no_rest():
        return pl.pallas_call(empty_kernel, out_shape=units_shape(devices * EXTRA), out_specs=ANY, name="nothing")()

    def rest_direct():
        return exchange(pack(devices * EXTRA, False, "pack_rest"))

    rest = lax.cond(left[0] == 0, no_rest, rest_direct)
    packed, rest, flow = lax.optimization_barrier((packed, rest, velocity))
    first = exchange(packed)

    def edge_shapes(deep, count):
        along_y = jax.ShapeDtypeStruct((deep * count * planes, lanes), f32)
        along_x = jax.ShapeDtypeStruct((deep * count * rows, lanes), f32)
        return [along_y, along_y, along_x, along_x]

    directions = flow.shape[1]
    vylow, vyhigh, vxlow, vxhigh = pl.pallas_call(
        functools.partial(velocity_edges_kernel, shape=flow.shape),
        out_shape=edge_shapes(1, directions),
        in_specs=[VMEM],
        out_specs=[VMEM] * 4,
        compiler_params=PARAMS,
        name="velocity_edges",
    )(flow.reshape(planes * directions * rows, lanes))
    flow_edges = [*neighbours("grp", vylow, vyhigh), *neighbours("dev", vxlow, vxhigh)]
    first, *flow_edges = lax.optimization_barrier((first, *flow_edges))
    second = pl.pallas_call(
        forward_kernel,
        out_shape=units_shape(devices),
        in_specs=[SMEM] * 2 + [ANY],
        out_specs=VMEM,
        scratch_shapes=[pltpu.SemaphoreType.DMA((devices,))],
        compiler_params=PARAMS,
        cost_estimate=cost(3),
        name="forward",
    )(me_ref, column, first)
    second = exchange(second)

    size = species * rows
    state_shape = jax.ShapeDtypeStruct((planes * size, lanes), f32)
    state, *edges = pl.pallas_call(
        functools.partial(build_kernel, old_fine.shape),
        out_shape=[state_shape] + edge_shapes(ITERS, species),
        in_specs=[SMEM] * 2 + [VMEM],
        out_specs=[VMEM] * 5,
        compiler_params=PARAMS,
        cost_estimate=cost(10),
        name="build",
    )(fine_at, coarse_at, first)
    relay_of = (jnp.arange(devices)[:, None] + me + column[:, :EXTRA] // 8) % devices

    def through(source, unit, used):
        over = jnp.arange(EXTRA) == (unit - DIRECT)[:, None]
        hit = (source[:, None, None] == jnp.arange(devices)[None, :, None]) & over[:, None, :]
        relay = jnp.max(jnp.where(hit, relay_of[None], -1), axis=(1, 2))
        return jnp.where(used & (unit >= DIRECT), relay, -1)

    order = jnp.arange(devices)
    halves = jnp.arange(2 * planes)
    at = jnp.repeat(fine_at, 2)
    relay = through(at // FINE_CAP, 2 * (at % FINE_CAP) + halves % 2, at >= 0)
    late_fine = jnp.max(jnp.where(relay[:, None] == order[None], halves[:, None], -1), axis=0)
    parents = jnp.arange(coarse_planes)
    code = coarse_at // 2
    fresh = jnp.min(fine_at.reshape(coarse_planes, 2), axis=1) < 0
    relay = through(code // unit_count, code % unit_count, fresh)
    late_parents = [
        jnp.max(jnp.where((relay[:, None] == order[None]) & (coarse_at % 2 == j)[:, None], parents[:, None], -1), axis=0)
        for j in range(COARSE_CAP)
    ]
    late = jnp.concatenate([late_fine, *late_parents])
    late_child = jnp.repeat(fresh & (code % unit_count >= DIRECT), 2) & (fine_at < 0)
    late_plane = late_child | ((fine_at >= 0) & (2 * (fine_at % FINE_CAP) + 1 >= DIRECT))
    beside = jnp.pad(late_plane, 1)
    again = (beside[:-2] | beside[1:-1] | beside[2:]).astype(i32)
    late_scratch = [
        pltpu.VMEM((1, species, half, lanes), f32),
        pltpu.VMEM((species, rows, lanes), f32),
        pltpu.SemaphoreType.DMA,
    ]
    state_scratch = pltpu.VMEM(state_shape.shape, f32)
    group_sems = pltpu.SemaphoreType.DMA((planes // UNROLL,))
    stepped = pl.pallas_call(
        functools.partial(first_step_kernel, old_fine.shape),
        out_shape=state_shape,
        in_specs=[SMEM, ANY, VMEM],
        out_specs=ANY,
        scratch_shapes=[state_scratch] * 2 + [group_sems] * 2,
        compiler_params=PARAMS,
        cost_estimate=cost(10),
        name="first_step",
    )(diffusion, state, velocity)
    second, stepped = lax.optimization_barrier((second, stepped))
    ylow_own, yhigh_own, xlow_own, xhigh_own = pl.pallas_call(
        functools.partial(edges_kernel, old_fine.shape),
        out_shape=edge_shapes(ITERS, species),
        in_specs=[SMEM] * 4 + [VMEM, ANY] + [VMEM] * 4,
        out_specs=[VMEM] * 4,
        scratch_shapes=late_scratch,
        compiler_params=PARAMS,
        cost_estimate=cost(4),
        name="edges",
    )(late, left, fine_at, coarse_at, second, rest, *edges)
    ylow, yhigh = neighbours("grp", ylow_own, yhigh_own)
    stepped = pl.pallas_call(
        functools.partial(late_step_kernel, old_fine.shape),
        out_shape=state_shape,
        in_specs=[SMEM] * 6 + [VMEM, ANY, ANY, VMEM, ANY],
        out_specs=ANY,
        scratch_shapes=[pltpu.VMEM(((planes + 2) * size, lanes), f32), state_scratch]
        + late_scratch
        + [pltpu.SemaphoreType.DMA((planes,))],
        input_output_aliases={10: 0},
        compiler_params=PARAMS,
        cost_estimate=cost(7),
        name="late_step",
    )(late, left, fine_at, coarse_at, again, diffusion, second, rest, state, velocity, stepped)
    ylow, yhigh, stepped = lax.optimization_barrier((ylow, yhigh, stepped))
    message = jax.ShapeDtypeStruct((ITERS * size + 32, lanes), f32)
    down, up = pl.pallas_call(
        functools.partial(corners_kernel, planes, species),
        out_shape=[message] * 2,
        in_specs=[VMEM] * 4,
        out_specs=[VMEM] * 2,
        compiler_params=PARAMS,
        name="corners",
    )(ylow, yhigh, xlow_own, xhigh_own)
    xlow, xhigh = neighbours("dev", down, up)
    grp, dev = lax.axis_index("grp"), lax.axis_index("dev")
    inside = jnp.stack([grp > 0, grp < lax.axis_size("grp") - 1, dev > 0, dev < devices - 1]).astype(f32)
    row_edge = pltpu.VMEM((species * planes, lanes), f32)
    plane_edge = pltpu.VMEM((size, lanes), f32)
    done = pl.pallas_call(
        functools.partial(second_step_kernel, old_fine.shape),
        out_shape=state_shape,
        in_specs=[SMEM] * 2 + [ANY] + [VMEM] * 15,
        out_specs=ANY,
        scratch_shapes=[state_scratch] * 2
        + [row_edge] * 2
        + [plane_edge] * 2
        + [pltpu.SemaphoreType.DMA, group_sems],
        compiler_params=PARAMS,
        cost_estimate=cost(10),
        name="second_step",
    )(
        inside, diffusion, stepped, velocity, ylow_own, yhigh_own, xlow_own, xhigh_own, ylow, yhigh, xlow, xhigh,
        vylow, vyhigh, *flow_edges,
    )
    return done.reshape(old_fine.shape)


def solution(mesh):
    in_specs = (
        P("dev", None, "grp", None),
        P("grp", "dev"),
        P("dev", None, "grp", None),
        P("grp", "dev"),
        P("dev", None, "grp", None),
        P(),
    )
    out_specs = P("dev", None, "grp", None)
    return jax.shard_map(
        on_device, mesh=mesh, in_specs=in_specs, out_specs=out_specs, check_vma=False
    )
```

```python
import functools

import jax
import jax.numpy as jnp
from jax import lax
from jax.experimental import pallas as pl
from jax.experimental.pallas import tpu as pltpu
from jax.sharding import PartitionSpec as P

ITERS = 2
FINE_CAP = 4
COARSE_CAP = 2
DIRECT = 5
EXTRA = 2 * FINE_CAP + 1 - DIRECT
VMEM = pl.BlockSpec(memory_space=pltpu.VMEM)
SMEM = pl.BlockSpec(memory_space=pltpu.SMEM)
ANY = pl.BlockSpec(memory_space=pl.ANY)
PARAMS = pltpu.CompilerParams(vmem_limit_bytes=56 * 1024 * 1024)
UNROLL = 4


def ranks(boxes):
    count = boxes.shape[-1]
    earlier = jnp.arange(count)[None, :] < jnp.arange(count)[:, None]
    same = boxes[..., None, :] == boxes[..., :, None]
    return jnp.sum((same & earlier).astype(jnp.int32), axis=-1)


def plan_kernel(me_ref, units_ref, row_ref, column_ref, left_ref):
    devices, lanes = units_ref.shape
    me = me_ref[0]
    units = units_ref[...]
    source = lax.broadcasted_iota(jnp.int32, units.shape, 0)
    lane = lax.broadcasted_iota(jnp.int32, units.shape, 1)
    none = jnp.full(units.shape, -1, jnp.int32)

    def one_round(r, carry):
        left, codes, free, second, through = carry
        ok = (left > 0) & (free > 0) & (second > 0)
        position = DIRECT - free
        code = jnp.left_shift(r * 8 + position, 8 * jnp.maximum(left - 1, 0))
        codes = jnp.where(ok, codes | code, codes)
        through = jnp.where(ok, source * 8 + position, through)
        used = ok.astype(jnp.int32)
        left, free, second = left - used, free - used, second - used
        return (
            pltpu.roll(left, 1, 1),
            pltpu.roll(codes, 1, 1),
            free,
            pltpu.roll(second, devices - 1, 0),
            pltpu.roll(through, devices - 1, 0),
        )

    surplus = pltpu.roll(jnp.maximum(units - DIRECT, 0), 0, 1, stride=1, stride_axis=0)
    free = jnp.maximum(DIRECT - units, 0)
    init = (surplus, jnp.zeros_like(units), free, jnp.ones_like(units), none)
    left, codes, _, _, through = lax.fori_loop(0, devices, one_round, init)
    column = none
    for i in range(EXTRA):
        chosen = jnp.where(left <= i, lax.shift_right_logical(codes, jnp.full_like(codes, 8 * i)) & 255, -1)
        row_ref[i : i + 1] = jnp.max(jnp.where(source == me, chosen, -1), axis=0, keepdims=True)
        mine = (lane < devices) & (lane == (source + me) % devices)
        found = jnp.max(jnp.where(mine, chosen, -1), axis=1, keepdims=True)
        column = jnp.where(lane == i, found, column)
    found = jnp.max(jnp.where(lane == me, through, -1), axis=1, keepdims=True)
    column_ref[...] = jnp.where(lane == EXTRA, found, column)
    left_ref[0] = jnp.max(left.astype(jnp.float32)).astype(jnp.int32)


def pack_kernel(
    devices, first, me_ref, fine_at_ref, coarse_at_ref, row_ref, fine_in_ref, coarse_ref, out_ref, fine_ref, sem
):
    planes = fine_ref.shape[0]
    coarse_planes, _, half, depth = coarse_ref.shape
    part = planes // sem.shape[0]

    def bring(i):
        planes_of = pl.ds(i * part, part)
        return pltpu.make_async_copy(fine_in_ref.at[planes_of], fine_ref.at[planes_of], sem.at[i])

    def slot_of(box, unit):
        if first:
            return first_slot(devices, me_ref[0], row_ref, box, unit)
        return jnp.where(unit < DIRECT, -1, box * EXTRA + unit - DIRECT)

    for i in range(sem.shape[0]):
        bring(i).start()

    def coarse_plane(k, carry):
        code = coarse_at_ref[k]

        @pl.when(code >= 0)
        def _():
            at = code // 2
            slot = slot_of(at // (DIRECT + EXTRA), at % (DIRECT + EXTRA))
            for j in range(2):

                @pl.when((slot >= 0) & (code % 2 == j))
                def _():
                    out_ref[slot, :, :, j * depth : (j + 1) * depth] = coarse_ref[k]

        return carry

    lax.fori_loop(0, coarse_planes, coarse_plane, 0)

    def fine_plane(k, carry):
        code = fine_at_ref[k]
        box, rank = code // FINE_CAP, code % FINE_CAP
        whole = DIRECT // 2

        if first:

            @pl.when((code >= 0) & (rank < whole))
            def _():
                for h in range(2):
                    out_ref[box * DIRECT + 2 * rank + h] = fine_ref[k, :, h * half : (h + 1) * half, :]

        @pl.when((code >= 0) & (rank >= whole))
        def _():
            for h in range(2):
                slot = slot_of(box, 2 * rank + h)

                @pl.when(slot >= 0)
                def _():
                    out_ref[slot] = fine_ref[k, :, h * half : (h + 1) * half, :]

        return carry

    for i in range(sem.shape[0]):
        bring(i).wait()
        lax.fori_loop(i * part, (i + 1) * part, fine_plane, 0)


def first_slot(devices, me, row_ref, box, unit):
    t = (me + box) % devices
    code = row_ref[jnp.maximum(unit - DIRECT, 0), t]
    relay = jnp.where(code >= 0, ((t + code // 8) % devices) * DIRECT + code % 8, -1)
    return jnp.where(unit < DIRECT, box * DIRECT + unit, relay)


def forward_kernel(me_ref, column_ref, in_ref, out_ref, sem):
    devices = out_ref.shape[0]

    def each(act):
        def body(a, carry):
            code = column_ref[a, EXTRA]

            @pl.when(code >= 0)
            def _():
                box = (me_ref[0] - a + devices) % devices
                act(pltpu.make_async_copy(in_ref.at[(code // 8) * DIRECT + code % 8], out_ref.at[box], sem.at[a]))

            return carry

        lax.fori_loop(0, devices, body, 0)

    each(lambda copy: copy.start())
    each(lambda copy: copy.wait())


def rows_to_edges(flat_ref, edge_ref, offset, row, planes, species, rows):
    for s in range(species):
        for x in range(0, planes, 8):
            at = offset + s * planes + x
            edge_ref[at : at + 8] = flat_ref[pl.ds((x * species + s) * rows + row, 8, stride=species * rows), :]


def interpolate(ref, slot, part, store):
    _, species, half, lanes = ref.shape
    lane = lax.broadcasted_iota(jnp.int32, (half, lanes), 1)
    row = lax.broadcasted_iota(jnp.int32, (half, lanes), 0)
    sign = jnp.where(lane % 2 == 0, -0.25, 0.25)
    lane_first = lane % (lanes // 2) == 0
    lane_last = lane % (lanes // 2) == lanes // 2 - 1
    index = part * (lanes // 2) + lane // 2
    for s in range(species):
        p = ref[slot, s]
        below = jnp.where(row == 0, p, pltpu.roll(p, 1, 0))
        above = jnp.where(row == half - 1, p, pltpu.roll(p, half - 1, 0))
        left = jnp.where(lane_first, p, pltpu.roll(p, 1, 1))
        right = jnp.where(lane_last, p, pltpu.roll(p, lanes - 1, 1))
        slope_y = 0.125 * (above - below)
        slope_z = 0.5 * (right - left)
        gz = jnp.take_along_axis(slope_z, index, axis=1) * sign
        even = jnp.take_along_axis(p - slope_y, index, axis=1) + gz
        odd = jnp.take_along_axis(p + slope_y, index, axis=1) + gz
        store(s, even, odd)


def build_kernel(shape, fine_at_ref, coarse_at_ref, first_ref, out_ref, ylow_ref, yhigh_ref, xlow_ref, xhigh_ref):
    planes, species, rows, lanes = shape
    half = rows // 2

    def body(c, carry):
        at = [fine_at_ref[2 * c], fine_at_ref[2 * c + 1]]
        code = coarse_at_ref[c]
        unit = code // 2 % (DIRECT + EXTRA)

        @pl.when(((at[0] < 0) | (at[1] < 0)) & (unit < DIRECT))
        def _():
            def store(s, even, odd):
                for child in range(2):
                    base = pl.multiple_of(((2 * c + child) * species + s) * rows, rows)
                    out_ref[pl.ds(base, half, stride=2), :] = even
                    out_ref[pl.ds(base + 1, half, stride=2), :] = odd

            interpolate(first_ref, code // 2 // (DIRECT + EXTRA) * DIRECT + unit, code % 2, store)

        for child in range(2):
            for h in range(2):
                late = 2 * (at[child] % FINE_CAP) + h

                @pl.when((at[child] >= 0) & (late < DIRECT))
                def _():
                    slot = at[child] // FINE_CAP * DIRECT + late
                    for s in range(species):
                        base = pl.multiple_of(((2 * c + child) * species + s) * rows + h * half, half)
                        out_ref[pl.ds(base, half), :] = first_ref[slot, s]

        return carry

    lax.fori_loop(0, planes // 2, body, 0)
    for r in range(ITERS):
        rows_to_edges(out_ref, ylow_ref, r * species * planes, r, planes, species, rows)
        rows_to_edges(out_ref, yhigh_ref, r * species * planes, rows - ITERS + r, planes, species, rows)
    deep = ITERS * species * rows
    xlow_ref[...] = out_ref[0:deep]
    xhigh_ref[...] = out_ref[planes * species * rows - deep : planes * species * rows]


def late_units(shape, late_ref, left_ref, fine_at_ref, coarse_at_ref, second_ref, rest_ref, held_ref,
               plane_ref, sem, half_plane, whole_plane):
    planes, _, rows, _ = shape
    half = rows // 2
    planned = left_ref[0] == 0

    def children(c, ref, slot):
        def store(s, even, odd):
            plane_ref[s, pl.ds(0, half, stride=2), :] = even
            plane_ref[s, pl.ds(1, half, stride=2), :] = odd

        interpolate(ref, slot, coarse_at_ref[c] % 2, store)
        for child in range(2):

            @pl.when(fine_at_ref[2 * c + child] < 0)
            def _():
                whole_plane(2 * c + child)

    def from_relay(m, carry):
        what = late_ref[m]

        @pl.when((what >= 0) & (what < 2 * planes))
        def _():
            for h in range(2):

                @pl.when(what % 2 == h)
                def _():
                    half_plane(what // 2, h, second_ref, m)

        for more in range(2):
            parent = late_ref[(1 + more) * late_ref.shape[0] // 3 + m]

            @pl.when(parent >= 0)
            def _():
                children(parent, second_ref, m)

        return carry

    @pl.when(planned)
    def _():
        lax.fori_loop(0, second_ref.shape[0], from_relay, 0)

    def bring(source, unit):
        copy = pltpu.make_async_copy(
            rest_ref.at[pl.ds(source * EXTRA + jnp.maximum(unit - DIRECT, 0), 1)], held_ref, sem
        )
        copy.start()
        copy.wait()

    def direct(c, carry):
        code = coarse_at_ref[c]
        unit = code // 2 % (DIRECT + EXTRA)

        @pl.when(((fine_at_ref[2 * c] < 0) | (fine_at_ref[2 * c + 1] < 0)) & (unit >= DIRECT))
        def _():
            bring(code // 2 // (DIRECT + EXTRA), unit)
            children(c, held_ref, 0)

        for x in (2 * c, 2 * c + 1):
            at = fine_at_ref[x]
            for h in range(2):
                late = 2 * (at % FINE_CAP) + h

                @pl.when((at >= 0) & (late >= DIRECT))
                def _():
                    bring(at // FINE_CAP, late)
                    half_plane(x, h, held_ref, 0)

        return carry

    @pl.when(jnp.logical_not(planned))
    def _():
        lax.fori_loop(0, planes // 2, direct, 0)


def edges_kernel(
    shape, late_ref, left_ref, fine_at_ref, coarse_at_ref, second_ref, rest_ref,
    ylow_in_ref, yhigh_in_ref, xlow_in_ref, xhigh_in_ref,
    ylow_ref, yhigh_ref, xlow_ref, xhigh_ref, held_ref, plane_ref, sem,
):
    planes, species, rows, _ = shape
    half = rows // 2
    size = species * rows
    ylow_ref[...] = ylow_in_ref[...]
    yhigh_ref[...] = yhigh_in_ref[...]
    xlow_ref[...] = xlow_in_ref[...]
    xhigh_ref[...] = xhigh_in_ref[...]

    def half_edges(x, h, value):
        edge_ref, first = ((ylow_ref, 0), (yhigh_ref, half - ITERS))[h]
        for s in range(species):
            for r in range(ITERS):
                edge_ref[pl.ds((r * species + s) * planes + x, 1), :] = value(s, slice(first + r, first + r + 1))
        for near, xedge_ref, at in ((x < ITERS, xlow_ref, x), (x >= planes - ITERS, xhigh_ref, x - planes + ITERS)):

            @pl.when(near)
            def _():
                for s in range(species):
                    base = pl.multiple_of(at * size + s * rows + h * half, half)
                    xedge_ref[pl.ds(base, half), :] = value(s, slice(0, half))

    def half_plane(x, h, ref, slot):
        half_edges(x, h, lambda s, part: ref[slot, s, part])

    def whole_plane(x):
        for h in range(2):
            half_edges(x, h, lambda s, part: plane_ref[s, h * half + part.start : h * half + part.stop])

    late_units(
        shape, late_ref, left_ref, fine_at_ref, coarse_at_ref, second_ref, rest_ref, held_ref, plane_ref,
        sem, half_plane, whole_plane,
    )


def corners_kernel(planes, species, ylow_ref, yhigh_ref, xlow_ref, xhigh_ref, down_ref, up_ref):
    deep = xlow_ref.shape[0]
    down_ref[0:deep] = xlow_ref[...]
    up_ref[0:deep] = xhigh_ref[...]
    for message_ref, x in ((down_ref, 0), (up_ref, planes - 1)):
        for s in range(species):
            low = ((ITERS - 1) * species + s) * planes + x
            high = s * planes + x
            message_ref[deep + s : deep + s + 1] = ylow_ref[low : low + 1]
            message_ref[deep + 16 + s : deep + 16 + s + 1] = yhigh_ref[high : high + 1]
        for at in (deep + species, deep + 16 + species):
            message_ref[at : at + 16 - species] = jnp.zeros((16 - species, message_ref.shape[1]), jnp.float32)


def velocity_edges_kernel(vel_ref, ylow_ref, yhigh_ref, xlow_ref, xhigh_ref, *, shape):
    planes, directions, rows, _ = shape
    size = directions * rows
    rows_to_edges(vel_ref, ylow_ref, 0, 0, planes, directions, rows)
    rows_to_edges(vel_ref, yhigh_ref, 0, rows - 1, planes, directions, rows)
    xlow_ref[...] = vel_ref[0:size]
    xhigh_ref[...] = vel_ref[(planes - 1) * size : planes * size]


class Flow:
    def __init__(self, velocity):
        self.positive = [jnp.maximum(v, 0.0) for v in velocity]
        self.negative = [jnp.minimum(v, 0.0) for v in velocity]
        self.keep = 1.0
        for low, high in zip(self.positive, self.negative):
            self.keep = self.keep - (low - high)

    def step(self, u, neighbours, d):
        new = u * (self.keep - 6.0 * d)
        for k, (low, high) in enumerate(neighbours):
            new = new + low * (d + self.positive[k]) + high * (d - self.negative[k])
        return new


def along(u, first, last, dim):
    count = u.shape[dim]
    at = lax.broadcasted_iota(jnp.int32, u.shape, dim)
    low = jnp.where(at == 0, first, pltpu.roll(u, 1, dim))
    high = jnp.where(at == count - 1, last, pltpu.roll(u, count - 1, dim))
    return low, high


def advance_plane(diff_ref, velocity, center, below, above, y_low, y_high, store):
    flow = Flow(velocity)
    for s in range(diff_ref.shape[0]):
        u = center(s)
        sides = ((below(s), above(s)), along(u, y_low(s), y_high(s), 0), along(u, u, u, 1))
        store(s, flow.step(u, sides, diff_ref[s]))


def planes_of(ref, x, rows, size):
    return lambda s: ref[pl.ds(pl.multiple_of(x * size + s * rows, rows), rows), :]


def advance(shape, diff_ref, vel_ref, u_ref, new_ref, low, high, y_low, y_high, after):
    planes, species, rows, _ = shape
    size = species * rows

    def group(x, first, last):
        for i in range(UNROLL):

            def store(s, new):
                new_ref[pl.ds(pl.multiple_of((x + i) * size + s * rows, rows), rows), :] = new

            advance_plane(
                diff_ref,
                [vel_ref[x + i, k] for k in range(3)],
                planes_of(u_ref, x + i, rows, size),
                low if first and i == 0 else planes_of(u_ref, x + i - 1, rows, size),
                high if last and i == UNROLL - 1 else planes_of(u_ref, x + i + 1, rows, size),
                y_low(x + i),
                y_high(x + i),
                store,
            )
        after(x // UNROLL)

    def body(g, carry):
        group(g * UNROLL, False, False)
        return carry

    group(0, True, False)
    lax.fori_loop(1, planes // UNROLL - 1, body, 0)
    group(planes - UNROLL, False, True)


def send_group(shape, from_ref, to_ref, sem, g):
    size = UNROLL * shape[1] * shape[2]
    part = pl.ds(pl.multiple_of(g * size, size), size)
    return pltpu.make_async_copy(from_ref.at[part], to_ref.at[part], sem.at[g])


def finish_groups(shape, from_ref, to_ref, sem):
    def finish(g, carry):
        send_group(shape, from_ref, to_ref, sem, g).wait()
        return carry

    lax.fori_loop(0, shape[0] // UNROLL, finish, 0)


def nothing(s):
    return 0.0


def first_step_kernel(shape, diff_ref, state_ref, vel_ref, out_ref, u0_ref, u1_ref, in_sem, out_sem):
    for g in range(shape[0] // UNROLL):
        send_group(shape, state_ref, u0_ref, in_sem, g).start()
    finish_groups(shape, state_ref, u0_ref, in_sem)
    advance(
        shape, diff_ref, vel_ref, u0_ref, u1_ref, nothing, nothing, lambda x: nothing, lambda x: nothing,
        lambda g: send_group(shape, u1_ref, out_ref, out_sem, g).start(),
    )
    finish_groups(shape, u1_ref, out_ref, out_sem)


def late_step_kernel(
    shape, late_ref, left_ref, fine_at_ref, coarse_at_ref, again_ref, diff_ref, second_ref, rest_ref, state_ref, vel_ref, _,
    out_ref, u0_ref, u1_ref, held_ref, plane_ref, sem, out_sem,
):
    planes, species, rows, lanes = shape
    half = rows // 2
    size = species * rows
    copy = pltpu.make_async_copy(state_ref, u0_ref.at[size : size + planes * size], sem)
    copy.start()
    u0_ref[0:size] = jnp.zeros((size, lanes), jnp.float32)
    u0_ref[size + planes * size : 2 * size + planes * size] = jnp.zeros((size, lanes), jnp.float32)
    copy.wait()

    def half_plane(x, h, ref, slot):
        for s in range(species):
            base = pl.multiple_of((x + 1) * size + s * rows + h * half, half)
            u0_ref[pl.ds(base, half), :] = ref[slot, s]

    def whole_plane(x):
        for s in range(species):
            u0_ref[pl.ds(pl.multiple_of((x + 1) * size + s * rows, rows), rows), :] = plane_ref[s]

    late_units(
        shape, late_ref, left_ref, fine_at_ref, coarse_at_ref, second_ref, rest_ref, held_ref, plane_ref,
        sem, half_plane, whole_plane,
    )

    def send(x):
        part = pl.ds(pl.multiple_of(x * size, size), size)
        return pltpu.make_async_copy(u1_ref.at[part], out_ref.at[part], out_sem.at[x])

    def take(i, carry):
        for x in (again_ref[2 * i], again_ref[2 * i + 1]):
            read, write = jnp.maximum(x, 0), jnp.where(x < 0, planes, x)

            def store(s, new):
                u1_ref[pl.ds(pl.multiple_of(write * size + s * rows, rows), rows), :] = new

            around = [planes_of(u0_ref, read + 1 + j, rows, size) for j in (0, -1, 1)]
            advance_plane(diff_ref, [vel_ref[read, k] for k in range(3)], *around, nothing, nothing, store)
        return carry

    def each(act):
        def body(i, carry):
            act(send(again_ref[i]))
            return carry

        lax.fori_loop(0, count, body, 0)

    count = again_ref[planes]
    lax.fori_loop(0, (count + 1) // 2, take, 0)
    each(lambda copy: copy.start())
    each(lambda copy: copy.wait())


def second_step_kernel(
    shape, inside_ref, diff_ref, first_ref, vel_ref, ylow_own_ref, yhigh_own_ref, xlow_own_ref, xhigh_own_ref, ylow_ref,
    yhigh_ref, xlow_ref, xhigh_ref, vylow_own_ref, vyhigh_own_ref, vylow_ref, vyhigh_ref, vxlow_ref, vxhigh_ref,
    out_ref, u1_ref, u2_ref, row_low_ref, row_high_ref, plane_low_ref, plane_high_ref, sem, out_sem,
):
    planes, species, rows, lanes = shape
    size = species * rows
    deep = ITERS * size
    copy = pltpu.make_async_copy(first_ref, u1_ref, sem)
    copy.start()

    for (near_ref, near, far, own_ref, own, v_ref, corner, target_ref, inside) in (
        (ylow_ref, 1, 0, ylow_own_ref, 0, vylow_ref, deep, row_low_ref, 0),
        (yhigh_ref, 0, 1, yhigh_own_ref, 1, vyhigh_ref, deep + 16, row_high_ref, 1),
    ):
        for x in range(0, planes, 16):
            flow = Flow([v_ref[k * planes + x : k * planes + x + 16] for k in range(3)])
            for s in range(species):

                def band(ref, r):
                    start = (r * species + s) * planes + x
                    return ref[start : start + 16]

                u = band(near_ref, near)
                start = (near * species + s) * planes
                if x == 0:
                    first = xlow_ref[corner + s : corner + s + 1]
                else:
                    first = near_ref[start + x - 1 : start + x]
                if x + 16 == planes:
                    last = xhigh_ref[corner + s : corner + s + 1]
                else:
                    last = near_ref[start + x + 16 : start + x + 17]
                outer, inner = band(near_ref, far), band(own_ref, own)
                across = (outer, inner) if inside == 0 else (inner, outer)
                new = flow.step(u, (along(u, first, last, 0), across, along(u, u, u, 1)), diff_ref[s])
                target_ref[s * planes + x : s * planes + x + 16] = new * inside_ref[inside]

    def at(ref, x):
        return planes_of(ref, x, rows, size)

    for (halo_ref, near, below, above, v_ref, target_ref, inside) in (
        (xlow_ref, 1, at(xlow_ref, 0), at(xlow_own_ref, 0), vxlow_ref, plane_low_ref, 2),
        (xhigh_ref, 0, at(xhigh_own_ref, ITERS - 1), at(xhigh_ref, 1), vxhigh_ref, plane_high_ref, 3),
    ):

        def store(s, new):
            target_ref[s * rows : (s + 1) * rows] = new * inside_ref[inside]

        def corner(offset):
            return lambda s: halo_ref[deep + offset + s : deep + offset + s + 1]

        velocity = [v_ref[k * rows : (k + 1) * rows] for k in range(3)]
        advance_plane(diff_ref, velocity, at(halo_ref, near), below, above, corner(0), corner(16), store)

    copy.wait()
    for x in range(0, planes, 8):
        up = jnp.maximum(vylow_own_ref[planes + x : planes + x + 8], 0.0)
        down = jnp.minimum(vyhigh_own_ref[planes + x : planes + x + 8], 0.0)
        for s in range(species):
            low = pl.ds((x * species + s) * rows, 8, stride=size)
            high = pl.ds((x * species + s) * rows + rows - 1, 8, stride=size)
            start = species * planes + s * planes + x
            u1_ref[low, :] = u1_ref[low, :] + (diff_ref[s] + up) * ylow_ref[start : start + 8]
            start = s * planes + x
            u1_ref[high, :] = u1_ref[high, :] + (diff_ref[s] - down) * yhigh_ref[start : start + 8]
    up = jnp.maximum(vel_ref[0, 0], 0.0)
    down = jnp.minimum(vel_ref[planes - 1, 0], 0.0)
    for s in range(species):
        low = slice(s * rows, (s + 1) * rows)
        high = slice((planes - 1) * size + s * rows, (planes - 1) * size + (s + 1) * rows)
        u1_ref[low] = u1_ref[low] + (diff_ref[s] + up) * at(xlow_ref, 1)(s)
        u1_ref[high] = u1_ref[high] + (diff_ref[s] - down) * at(xhigh_ref, 0)(s)

    def edge(ref):
        return lambda x: lambda s: ref[pl.ds(s * planes + x, 1), :]

    advance(
        shape, diff_ref, vel_ref, u1_ref, u2_ref, at(plane_low_ref, 0), at(plane_high_ref, 0), edge(row_low_ref),
        edge(row_high_ref), lambda g: send_group(shape, u2_ref, out_ref, out_sem, g).start(),
    )
    finish_groups(shape, u2_ref, out_ref, out_sem)


def empty_kernel(out_ref):
    pass


def cost(microseconds):
    return pl.CostEstimate(flops=0, bytes_accessed=int(microseconds * 3.6e6), transcendentals=0)


def neighbours(axis, low, high):
    size = lax.axis_size(axis)
    up = [(i, (i + 1) % size) for i in range(size - 1)]
    return lax.ppermute(high, axis, up), lax.ppermute(low, axis, [(b, a) for a, b in up])


def on_device(old_fine, old_ids, old_coarse, coarse_ids, velocity, diffusion):
    devices = lax.axis_size("dev")
    me = lax.axis_index("dev")
    me_ref = me.reshape(1).astype(jnp.int32)
    planes, species, rows, lanes = old_fine.shape
    half = rows // 2
    coarse_planes = old_coarse.shape[0]
    unit_count = DIRECT + EXTRA
    f32 = jnp.float32
    i32 = jnp.int32

    def units_shape(count):
        return jax.ShapeDtypeStruct((count, species, half, lanes), f32)

    own, own_coarse = old_ids[0], coarse_ids[0]
    labels = jnp.broadcast_to(jnp.concatenate([own, own_coarse])[None], (devices, planes + coarse_planes))
    labels = lax.all_to_all(labels, "dev", split_axis=0, concat_axis=0, tiled=True)
    all_ids, all_coarse = labels[:, :planes], labels[:, planes:]
    all_box = jnp.where(all_ids >= 0, all_ids // planes, -1)
    all_coarse_box = all_coarse // coarse_planes
    flat_parents = jnp.where(all_ids >= 0, all_ids // 2, -1).reshape(-1)

    def needed(coarse):
        kept = jnp.sum((flat_parents == coarse[..., None]).astype(i32), axis=-1)
        return kept < 2

    box = jnp.arange(lanes) % devices
    fine_units = jnp.sum((all_box[:, None, :] == box[None, :, None]).astype(i32), axis=-1)
    asked = needed(all_coarse)[:, None, :] & (all_coarse_box[:, None, :] == box[None, :, None])
    units = 2 * fine_units + jnp.max(asked.astype(i32), axis=-1)
    row, column, left = pl.pallas_call(
        plan_kernel,
        out_shape=[
            jax.ShapeDtypeStruct((EXTRA, lanes), i32),
            jax.ShapeDtypeStruct((devices, lanes), i32),
            jax.ShapeDtypeStruct((1,), i32),
        ],
        in_specs=[SMEM, VMEM],
        out_specs=[VMEM, VMEM, SMEM],
        name="plan",
    )(me_ref, units)
    own_box = jnp.where(own >= 0, own // planes, -1)
    send_fine = jnp.where(own >= 0, own_box * FINE_CAP + ranks(own_box), -1)
    own_coarse_box = own_coarse // coarse_planes
    before = jnp.sum((own_box[None, :] == own_coarse_box[:, None]).astype(i32), axis=1)
    send_coarse = (own_coarse_box * unit_count + 2 * before) * 2 + ranks(own_coarse_box)
    send_coarse = jnp.where(needed(own_coarse), send_coarse, -1)

    order = jnp.arange(devices)[:, None]
    wanted = me * planes + jnp.arange(planes)
    fine_at = jnp.where(all_ids[None] == wanted[:, None, None], (order * FINE_CAP + ranks(all_box))[None], -1)
    fine_at = jnp.max(fine_at, axis=(1, 2))
    to_me = jnp.sum((all_box == me).astype(i32), axis=1, keepdims=True)
    coarse_wanted = me * coarse_planes + jnp.arange(coarse_planes)
    coarse_code = (order * unit_count + 2 * to_me) * 2 + ranks(all_coarse_box)
    coarse_at = jnp.where(all_coarse[None] == coarse_wanted[:, None, None], coarse_code[None], 0)
    coarse_at = jnp.max(coarse_at, axis=(1, 2))

    def exchange(value):
        return lax.all_to_all(value, "dev", split_axis=0, concat_axis=0, tiled=True)

    def pack(count, first, name):
        return pl.pallas_call(
            functools.partial(pack_kernel, devices, first),
            out_shape=units_shape(count),
            in_specs=[SMEM] * 4 + [ANY, VMEM],
            out_specs=VMEM,
            scratch_shapes=[pltpu.VMEM(old_fine.shape, f32), pltpu.SemaphoreType.DMA((4,))],
            compiler_params=PARAMS,
            name=name,
        )(me_ref, send_fine, send_coarse, row, old_fine, old_coarse)

    packed = pack(devices * DIRECT, True, "pack")

    def no_rest():
        return pl.pallas_call(empty_kernel, out_shape=units_shape(devices * EXTRA), out_specs=ANY, name="nothing")()

    def rest_direct():
        return exchange(pack(devices * EXTRA, False, "pack_rest"))

    rest = lax.cond(left[0] == 0, no_rest, rest_direct)
    packed, rest, flow = lax.optimization_barrier((packed, rest, velocity))
    first = exchange(packed)

    def edge_shapes(deep, count):
        along_y = jax.ShapeDtypeStruct((deep * count * planes, lanes), f32)
        along_x = jax.ShapeDtypeStruct((deep * count * rows, lanes), f32)
        return [along_y, along_y, along_x, along_x]

    directions = flow.shape[1]
    vylow, vyhigh, vxlow, vxhigh = pl.pallas_call(
        functools.partial(velocity_edges_kernel, shape=flow.shape),
        out_shape=edge_shapes(1, directions),
        in_specs=[VMEM],
        out_specs=[VMEM] * 4,
        compiler_params=PARAMS,
        name="velocity_edges",
    )(flow.reshape(planes * directions * rows, lanes))
    flow_edges = [*neighbours("grp", vylow, vyhigh), *neighbours("dev", vxlow, vxhigh)]
    first, *flow_edges = lax.optimization_barrier((first, *flow_edges))
    second = pl.pallas_call(
        forward_kernel,
        out_shape=units_shape(devices),
        in_specs=[SMEM] * 2 + [ANY],
        out_specs=VMEM,
        scratch_shapes=[pltpu.SemaphoreType.DMA((devices,))],
        compiler_params=PARAMS,
        cost_estimate=cost(3),
        name="forward",
    )(me_ref, column, first)
    second = exchange(second)

    size = species * rows
    state_shape = jax.ShapeDtypeStruct((planes * size, lanes), f32)
    state, *edges = pl.pallas_call(
        functools.partial(build_kernel, old_fine.shape),
        out_shape=[state_shape] + edge_shapes(ITERS, species),
        in_specs=[SMEM] * 2 + [VMEM],
        out_specs=[VMEM] * 5,
        compiler_params=PARAMS,
        cost_estimate=cost(10),
        name="build",
    )(fine_at, coarse_at, first)
    relay_of = (jnp.arange(devices)[:, None] + me + column[:, :EXTRA] // 8) % devices

    def through(source, unit, used):
        over = jnp.arange(EXTRA) == (unit - DIRECT)[:, None]
        hit = (source[:, None, None] == jnp.arange(devices)[None, :, None]) & over[:, None, :]
        relay = jnp.max(jnp.where(hit, relay_of[None], -1), axis=(1, 2))
        return jnp.where(used & (unit >= DIRECT), relay, -1)

    order = jnp.arange(devices)
    halves = jnp.arange(2 * planes)
    at = jnp.repeat(fine_at, 2)
    relay = through(at // FINE_CAP, 2 * (at % FINE_CAP) + halves % 2, at >= 0)
    late_fine = jnp.max(jnp.where(relay[:, None] == order[None], halves[:, None], -1), axis=0)
    parents = jnp.arange(coarse_planes)
    code = coarse_at // 2
    fresh = jnp.min(fine_at.reshape(coarse_planes, 2), axis=1) < 0
    relay = through(code // unit_count, code % unit_count, fresh)
    late_parents = [
        jnp.max(jnp.where((relay[:, None] == order[None]) & (coarse_at % 2 == j)[:, None], parents[:, None], -1), axis=0)
        for j in range(COARSE_CAP)
    ]
    late = jnp.concatenate([late_fine, *late_parents])
    late_child = jnp.repeat(fresh & (code % unit_count >= DIRECT), 2) & (fine_at < 0)
    late_plane = late_child | ((fine_at >= 0) & (2 * (fine_at % FINE_CAP) + 1 >= DIRECT))
    beside = jnp.pad(late_plane, 1)
    new_plane = jnp.arange(planes)
    again = beside[:-2] | beside[1:-1] | beside[2:]
    place = jnp.sum((again[None, :] & (new_plane[None, :] < new_plane[:, None])).astype(i32), axis=1)
    listed = again[None, :] & (place[None, :] == new_plane[:, None])
    again = jnp.concatenate(
        [jnp.max(jnp.where(listed, new_plane[None, :], -1), axis=1), jnp.sum(again.astype(i32)).reshape(1)]
    )
    late_scratch = [
        pltpu.VMEM((1, species, half, lanes), f32),
        pltpu.VMEM((species, rows, lanes), f32),
        pltpu.SemaphoreType.DMA,
    ]
    state_scratch = pltpu.VMEM(state_shape.shape, f32)
    group_sems = pltpu.SemaphoreType.DMA((planes // UNROLL,))
    stepped = pl.pallas_call(
        functools.partial(first_step_kernel, old_fine.shape),
        out_shape=state_shape,
        in_specs=[SMEM, ANY, VMEM],
        out_specs=ANY,
        scratch_shapes=[state_scratch] * 2 + [group_sems] * 2,
        compiler_params=PARAMS,
        cost_estimate=cost(10),
        name="first_step",
    )(diffusion, state, velocity)
    second, stepped = lax.optimization_barrier((second, stepped))
    ylow_own, yhigh_own, xlow_own, xhigh_own = pl.pallas_call(
        functools.partial(edges_kernel, old_fine.shape),
        out_shape=edge_shapes(ITERS, species),
        in_specs=[SMEM] * 4 + [VMEM, ANY] + [VMEM] * 4,
        out_specs=[VMEM] * 4,
        scratch_shapes=late_scratch,
        compiler_params=PARAMS,
        cost_estimate=cost(4),
        name="edges",
    )(late, left, fine_at, coarse_at, second, rest, *edges)
    ylow, yhigh = neighbours("grp", ylow_own, yhigh_own)
    stepped = pl.pallas_call(
        functools.partial(late_step_kernel, old_fine.shape),
        out_shape=state_shape,
        in_specs=[SMEM] * 6 + [VMEM, ANY, ANY, VMEM, ANY],
        out_specs=ANY,
        scratch_shapes=[pltpu.VMEM(((planes + 2) * size, lanes), f32), pltpu.VMEM(((planes + 1) * size, lanes), f32)]
        + late_scratch
        + [pltpu.SemaphoreType.DMA((planes,))],
        input_output_aliases={10: 0},
        compiler_params=PARAMS,
        cost_estimate=cost(7),
        name="late_step",
    )(late, left, fine_at, coarse_at, again, diffusion, second, rest, state, velocity, stepped)
    ylow, yhigh, stepped = lax.optimization_barrier((ylow, yhigh, stepped))
    message = jax.ShapeDtypeStruct((ITERS * size + 32, lanes), f32)
    down, up = pl.pallas_call(
        functools.partial(corners_kernel, planes, species),
        out_shape=[message] * 2,
        in_specs=[VMEM] * 4,
        out_specs=[VMEM] * 2,
        compiler_params=PARAMS,
        name="corners",
    )(ylow, yhigh, xlow_own, xhigh_own)
    xlow, xhigh = neighbours("dev", down, up)
    grp, dev = lax.axis_index("grp"), lax.axis_index("dev")
    inside = jnp.stack([grp > 0, grp < lax.axis_size("grp") - 1, dev > 0, dev < devices - 1]).astype(f32)
    row_edge = pltpu.VMEM((species * planes, lanes), f32)
    plane_edge = pltpu.VMEM((size, lanes), f32)
    done = pl.pallas_call(
        functools.partial(second_step_kernel, old_fine.shape),
        out_shape=state_shape,
        in_specs=[SMEM] * 2 + [ANY] + [VMEM] * 15,
        out_specs=ANY,
        scratch_shapes=[state_scratch] * 2
        + [row_edge] * 2
        + [plane_edge] * 2
        + [pltpu.SemaphoreType.DMA, group_sems],
        compiler_params=PARAMS,
        cost_estimate=cost(10),
        name="second_step",
    )(
        inside, diffusion, stepped, velocity, ylow_own, yhigh_own, xlow_own, xhigh_own, ylow, yhigh, xlow, xhigh,
        vylow, vyhigh, *flow_edges,
    )
    return done.reshape(old_fine.shape)


def solution(mesh):
    in_specs = (
        P("dev", None, "grp", None),
        P("grp", "dev"),
        P("dev", None, "grp", None),
        P("grp", "dev"),
        P("dev", None, "grp", None),
        P(),
    )
    out_specs = P("dev", None, "grp", None)
    return jax.shard_map(
        on_device, mesh=mesh, in_specs=in_specs, out_specs=out_specs, check_vma=False
    )
```

```python
import functools

import jax
import jax.numpy as jnp
from jax import lax
from jax.experimental import pallas as pl
from jax.experimental.pallas import tpu as pltpu
from jax.sharding import PartitionSpec as P

ITERS = 2
FINE_CAP = 4
COARSE_CAP = 2
DIRECT = 5
EXTRA = 2 * FINE_CAP + 1 - DIRECT
VMEM = pl.BlockSpec(memory_space=pltpu.VMEM)
SMEM = pl.BlockSpec(memory_space=pltpu.SMEM)
ANY = pl.BlockSpec(memory_space=pl.ANY)
PARAMS = pltpu.CompilerParams(vmem_limit_bytes=56 * 1024 * 1024)
UNROLL = 4


def room(mib):
    return pltpu.CompilerParams(vmem_limit_bytes=mib * 1024 * 1024)


def ranks(boxes):
    count = boxes.shape[-1]
    earlier = jnp.arange(count)[None, :] < jnp.arange(count)[:, None]
    same = boxes[..., None, :] == boxes[..., :, None]
    return jnp.sum((same & earlier).astype(jnp.int32), axis=-1)


def plan_kernel(me_ref, units_ref, row_ref, column_ref, left_ref):
    devices, lanes = units_ref.shape
    me = me_ref[0]
    units = units_ref[...]
    source = lax.broadcasted_iota(jnp.int32, units.shape, 0)
    lane = lax.broadcasted_iota(jnp.int32, units.shape, 1)
    none = jnp.full(units.shape, -1, jnp.int32)

    def one_round(r, carry):
        left, codes, free, second, through = carry
        ok = (left > 0) & (free > 0) & (second > 0)
        position = DIRECT - free
        code = jnp.left_shift(r * 8 + position, 8 * jnp.maximum(left - 1, 0))
        codes = jnp.where(ok, codes | code, codes)
        through = jnp.where(ok, source * 8 + position, through)
        used = ok.astype(jnp.int32)
        left, free, second = left - used, free - used, second - used
        return (
            pltpu.roll(left, 1, 1),
            pltpu.roll(codes, 1, 1),
            free,
            pltpu.roll(second, devices - 1, 0),
            pltpu.roll(through, devices - 1, 0),
        )

    surplus = pltpu.roll(jnp.maximum(units - DIRECT, 0), 0, 1, stride=1, stride_axis=0)
    free = jnp.maximum(DIRECT - units, 0)
    init = (surplus, jnp.zeros_like(units), free, jnp.ones_like(units), none)
    left, codes, _, _, through = lax.fori_loop(0, devices, one_round, init)
    column = none
    for i in range(EXTRA):
        chosen = jnp.where(left <= i, lax.shift_right_logical(codes, jnp.full_like(codes, 8 * i)) & 255, -1)
        row_ref[i : i + 1] = jnp.max(jnp.where(source == me, chosen, -1), axis=0, keepdims=True)
        mine = (lane < devices) & (lane == (source + me) % devices)
        found = jnp.max(jnp.where(mine, chosen, -1), axis=1, keepdims=True)
        column = jnp.where(lane == i, found, column)
    found = jnp.max(jnp.where(lane == me, through, -1), axis=1, keepdims=True)
    column_ref[...] = jnp.where(lane == EXTRA, found, column)
    left_ref[0] = jnp.max(left.astype(jnp.float32)).astype(jnp.int32)


def pack_kernel(
    devices, first, me_ref, fine_at_ref, coarse_at_ref, row_ref, fine_in_ref, coarse_ref, out_ref, fine_ref, sem
):
    planes = fine_ref.shape[0]
    coarse_planes, _, half, depth = coarse_ref.shape
    part = planes // sem.shape[0]

    def bring(i):
        planes_of = pl.ds(i * part, part)
        return pltpu.make_async_copy(fine_in_ref.at[planes_of], fine_ref.at[planes_of], sem.at[i])

    def slot_of(box, unit):
        if first:
            return first_slot(devices, me_ref[0], row_ref, box, unit)
        return jnp.where(unit < DIRECT, -1, box * EXTRA + unit - DIRECT)

    for i in range(sem.shape[0]):
        bring(i).start()

    def coarse_plane(k, carry):
        code = coarse_at_ref[k]

        @pl.when(code >= 0)
        def _():
            at = code // 2
            slot = slot_of(at // (DIRECT + EXTRA), at % (DIRECT + EXTRA))
            for j in range(2):

                @pl.when((slot >= 0) & (code % 2 == j))
                def _():
                    out_ref[slot, :, :, j * depth : (j + 1) * depth] = coarse_ref[k]

        return carry

    lax.fori_loop(0, coarse_planes, coarse_plane, 0)

    def fine_plane(k, carry):
        code = fine_at_ref[k]
        box, rank = code // FINE_CAP, code % FINE_CAP
        whole = DIRECT // 2

        if first:

            @pl.when((code >= 0) & (rank < whole))
            def _():
                for h in range(2):
                    out_ref[box * DIRECT + 2 * rank + h] = fine_ref[k, :, h * half : (h + 1) * half, :]

        @pl.when((code >= 0) & (rank >= whole))
        def _():
            for h in range(2):
                slot = slot_of(box, 2 * rank + h)

                @pl.when(slot >= 0)
                def _():
                    out_ref[slot] = fine_ref[k, :, h * half : (h + 1) * half, :]

        return carry

    for i in range(sem.shape[0]):
        bring(i).wait()
        lax.fori_loop(i * part, (i + 1) * part, fine_plane, 0)


def first_slot(devices, me, row_ref, box, unit):
    t = (me + box) % devices
    code = row_ref[jnp.maximum(unit - DIRECT, 0), t]
    relay = jnp.where(code >= 0, ((t + code // 8) % devices) * DIRECT + code % 8, -1)
    return jnp.where(unit < DIRECT, box * DIRECT + unit, relay)


def forward_kernel(me_ref, column_ref, in_ref, out_ref, sem):
    devices = out_ref.shape[0]

    def each(act):
        def body(a, carry):
            code = column_ref[a, EXTRA]

            @pl.when(code >= 0)
            def _():
                box = (me_ref[0] - a + devices) % devices
                act(pltpu.make_async_copy(in_ref.at[(code // 8) * DIRECT + code % 8], out_ref.at[box], sem.at[a]))

            return carry

        lax.fori_loop(0, devices, body, 0)

    each(lambda copy: copy.start())
    each(lambda copy: copy.wait())


def rows_to_edges(flat_ref, edge_ref, offset, row, planes, species, rows):
    for s in range(species):
        for x in range(0, planes, 8):
            at = offset + s * planes + x
            edge_ref[at : at + 8] = flat_ref[pl.ds((x * species + s) * rows + row, 8, stride=species * rows), :]


def interpolate(ref, slot, part, store):
    _, species, half, lanes = ref.shape
    lane = lax.broadcasted_iota(jnp.int32, (half, lanes), 1)
    row = lax.broadcasted_iota(jnp.int32, (half, lanes), 0)
    sign = jnp.where(lane % 2 == 0, -0.25, 0.25)
    lane_first = lane % (lanes // 2) == 0
    lane_last = lane % (lanes // 2) == lanes // 2 - 1
    index = part * (lanes // 2) + lane // 2
    for s in range(species):
        p = ref[slot, s]
        below = jnp.where(row == 0, p, pltpu.roll(p, 1, 0))
        above = jnp.where(row == half - 1, p, pltpu.roll(p, half - 1, 0))
        left = jnp.where(lane_first, p, pltpu.roll(p, 1, 1))
        right = jnp.where(lane_last, p, pltpu.roll(p, lanes - 1, 1))
        slope_y = 0.125 * (above - below)
        slope_z = 0.5 * (right - left)
        gz = jnp.take_along_axis(slope_z, index, axis=1) * sign
        even = jnp.take_along_axis(p - slope_y, index, axis=1) + gz
        odd = jnp.take_along_axis(p + slope_y, index, axis=1) + gz
        store(s, even, odd)


def build_kernel(shape, fine_at_ref, coarse_at_ref, first_ref, out_ref, ylow_ref, yhigh_ref, xlow_ref, xhigh_ref):
    planes, species, rows, lanes = shape
    half = rows // 2

    def body(c, carry):
        at = [fine_at_ref[2 * c], fine_at_ref[2 * c + 1]]
        code = coarse_at_ref[c]
        unit = code // 2 % (DIRECT + EXTRA)

        @pl.when(((at[0] < 0) | (at[1] < 0)) & (unit < DIRECT))
        def _():
            def store(s, even, odd):
                for child in range(2):
                    base = pl.multiple_of(((2 * c + child) * species + s) * rows, rows)
                    out_ref[pl.ds(base, half, stride=2), :] = even
                    out_ref[pl.ds(base + 1, half, stride=2), :] = odd

            interpolate(first_ref, code // 2 // (DIRECT + EXTRA) * DIRECT + unit, code % 2, store)

        for child in range(2):
            for h in range(2):
                late = 2 * (at[child] % FINE_CAP) + h

                @pl.when((at[child] >= 0) & (late < DIRECT))
                def _():
                    slot = at[child] // FINE_CAP * DIRECT + late
                    for s in range(species):
                        base = pl.multiple_of(((2 * c + child) * species + s) * rows + h * half, half)
                        out_ref[pl.ds(base, half), :] = first_ref[slot, s]

        return carry

    lax.fori_loop(0, planes // 2, body, 0)
    for r in range(ITERS):
        rows_to_edges(out_ref, ylow_ref, r * species * planes, r, planes, species, rows)
        rows_to_edges(out_ref, yhigh_ref, r * species * planes, rows - ITERS + r, planes, species, rows)
    deep = ITERS * species * rows
    xlow_ref[...] = out_ref[0:deep]
    xhigh_ref[...] = out_ref[planes * species * rows - deep : planes * species * rows]


def late_units(shape, late_ref, left_ref, fine_at_ref, coarse_at_ref, second_ref, rest_ref, held_ref,
               plane_ref, sem, half_plane, whole_plane):
    planes, _, rows, _ = shape
    half = rows // 2
    planned = left_ref[0] == 0

    def children(c, ref, slot):
        def store(s, even, odd):
            plane_ref[s, pl.ds(0, half, stride=2), :] = even
            plane_ref[s, pl.ds(1, half, stride=2), :] = odd

        interpolate(ref, slot, coarse_at_ref[c] % 2, store)
        for child in range(2):

            @pl.when(fine_at_ref[2 * c + child] < 0)
            def _():
                whole_plane(2 * c + child)

    def from_relay(m, carry):
        what = late_ref[m]

        @pl.when((what >= 0) & (what < 2 * planes))
        def _():
            for h in range(2):

                @pl.when(what % 2 == h)
                def _():
                    half_plane(what // 2, h, second_ref, m)

        for more in range(2):
            parent = late_ref[(1 + more) * late_ref.shape[0] // 3 + m]

            @pl.when(parent >= 0)
            def _():
                children(parent, second_ref, m)

        return carry

    @pl.when(planned)
    def _():
        lax.fori_loop(0, second_ref.shape[0], from_relay, 0)

    def bring(source, unit):
        copy = pltpu.make_async_copy(
            rest_ref.at[pl.ds(source * EXTRA + jnp.maximum(unit - DIRECT, 0), 1)], held_ref, sem
        )
        copy.start()
        copy.wait()

    def direct(c, carry):
        code = coarse_at_ref[c]
        unit = code // 2 % (DIRECT + EXTRA)

        @pl.when(((fine_at_ref[2 * c] < 0) | (fine_at_ref[2 * c + 1] < 0)) & (unit >= DIRECT))
        def _():
            bring(code // 2 // (DIRECT + EXTRA), unit)
            children(c, held_ref, 0)

        for x in (2 * c, 2 * c + 1):
            at = fine_at_ref[x]
            for h in range(2):
                late = 2 * (at % FINE_CAP) + h

                @pl.when((at >= 0) & (late >= DIRECT))
                def _():
                    bring(at // FINE_CAP, late)
                    half_plane(x, h, held_ref, 0)

        return carry

    @pl.when(jnp.logical_not(planned))
    def _():
        lax.fori_loop(0, planes // 2, direct, 0)


def load_all(pairs, sem):
    copies = [pltpu.make_async_copy(source, target, sem.at[i]) for i, (source, target) in enumerate(pairs)]
    for copy in copies:
        copy.start()
    return copies


def edges_kernel(
    shape, late_ref, left_ref, fine_at_ref, coarse_at_ref, second_in_ref, rest_ref,
    ylow_in_ref, yhigh_in_ref, xlow_in_ref, xhigh_in_ref,
    ylow_ref, yhigh_ref, xlow_ref, xhigh_ref, held_ref, plane_ref, sem, second_ref, load_sem,
):
    planes, species, rows, _ = shape
    half = rows // 2
    size = species * rows
    loads = load_all(
        [
            (second_in_ref, second_ref),
            (ylow_in_ref, ylow_ref),
            (yhigh_in_ref, yhigh_ref),
            (xlow_in_ref, xlow_ref),
            (xhigh_in_ref, xhigh_ref),
        ],
        load_sem,
    )
    for load in loads:
        load.wait()

    def half_edges(x, h, value):
        edge_ref, first = ((ylow_ref, 0), (yhigh_ref, half - ITERS))[h]
        for s in range(species):
            for r in range(ITERS):
                edge_ref[pl.ds((r * species + s) * planes + x, 1), :] = value(s, slice(first + r, first + r + 1))
        for near, xedge_ref, at in ((x < ITERS, xlow_ref, x), (x >= planes - ITERS, xhigh_ref, x - planes + ITERS)):

            @pl.when(near)
            def _():
                for s in range(species):
                    base = pl.multiple_of(at * size + s * rows + h * half, half)
                    xedge_ref[pl.ds(base, half), :] = value(s, slice(0, half))

    def half_plane(x, h, ref, slot):
        half_edges(x, h, lambda s, part: ref[slot, s, part])

    def whole_plane(x):
        for h in range(2):
            half_edges(x, h, lambda s, part: plane_ref[s, h * half + part.start : h * half + part.stop])

    late_units(
        shape, late_ref, left_ref, fine_at_ref, coarse_at_ref, second_ref, rest_ref, held_ref, plane_ref,
        sem, half_plane, whole_plane,
    )


def corners_kernel(planes, species, ylow_ref, yhigh_ref, xlow_ref, xhigh_ref, down_ref, up_ref):
    deep = xlow_ref.shape[0]
    down_ref[0:deep] = xlow_ref[...]
    up_ref[0:deep] = xhigh_ref[...]
    for message_ref, x in ((down_ref, 0), (up_ref, planes - 1)):
        for s in range(species):
            low = ((ITERS - 1) * species + s) * planes + x
            high = s * planes + x
            message_ref[deep + s : deep + s + 1] = ylow_ref[low : low + 1]
            message_ref[deep + 16 + s : deep + 16 + s + 1] = yhigh_ref[high : high + 1]
        for at in (deep + species, deep + 16 + species):
            message_ref[at : at + 16 - species] = jnp.zeros((16 - species, message_ref.shape[1]), jnp.float32)


def velocity_edges_kernel(vel_ref, ylow_ref, yhigh_ref, xlow_ref, xhigh_ref, *, shape):
    planes, directions, rows, _ = shape
    size = directions * rows
    rows_to_edges(vel_ref, ylow_ref, 0, 0, planes, directions, rows)
    rows_to_edges(vel_ref, yhigh_ref, 0, rows - 1, planes, directions, rows)
    xlow_ref[...] = vel_ref[0:size]
    xhigh_ref[...] = vel_ref[(planes - 1) * size : planes * size]


class Flow:
    def __init__(self, velocity):
        self.positive = [jnp.maximum(v, 0.0) for v in velocity]
        self.negative = [jnp.minimum(v, 0.0) for v in velocity]
        self.keep = 1.0
        for low, high in zip(self.positive, self.negative):
            self.keep = self.keep - (low - high)

    def step(self, u, neighbours, d):
        new = u * (self.keep - 6.0 * d)
        for k, (low, high) in enumerate(neighbours):
            new = new + low * (d + self.positive[k]) + high * (d - self.negative[k])
        return new


def along(u, first, last, dim):
    count = u.shape[dim]
    at = lax.broadcasted_iota(jnp.int32, u.shape, dim)
    low = jnp.where(at == 0, first, pltpu.roll(u, 1, dim))
    high = jnp.where(at == count - 1, last, pltpu.roll(u, count - 1, dim))
    return low, high


def advance_plane(diff_ref, velocity, center, below, above, y_low, y_high, store):
    flow = Flow(velocity)
    for s in range(diff_ref.shape[0]):
        u = center(s)
        sides = ((below(s), above(s)), along(u, y_low(s), y_high(s), 0), along(u, u, u, 1))
        store(s, flow.step(u, sides, diff_ref[s]))


def planes_of(ref, x, rows, size):
    return lambda s: ref[pl.ds(pl.multiple_of(x * size + s * rows, rows), rows), :]


def advance(shape, diff_ref, vel_ref, u_ref, new_ref, low, high, y_low, y_high, after):
    planes, species, rows, _ = shape
    size = species * rows

    def group(x, first, last):
        for i in range(UNROLL):

            def store(s, new):
                new_ref[pl.ds(pl.multiple_of((x + i) * size + s * rows, rows), rows), :] = new

            advance_plane(
                diff_ref,
                [vel_ref[x + i, k] for k in range(3)],
                planes_of(u_ref, x + i, rows, size),
                low if first and i == 0 else planes_of(u_ref, x + i - 1, rows, size),
                high if last and i == UNROLL - 1 else planes_of(u_ref, x + i + 1, rows, size),
                y_low(x + i),
                y_high(x + i),
                store,
            )
        after(x // UNROLL)

    def body(g, carry):
        group(g * UNROLL, False, False)
        return carry

    group(0, True, False)
    lax.fori_loop(1, planes // UNROLL - 1, body, 0)
    group(planes - UNROLL, False, True)


def send_group(shape, from_ref, to_ref, sem, g):
    size = UNROLL * shape[1] * shape[2]
    part = pl.ds(pl.multiple_of(g * size, size), size)
    return pltpu.make_async_copy(from_ref.at[part], to_ref.at[part], sem.at[g])


def finish_groups(shape, from_ref, to_ref, sem):
    def finish(g, carry):
        send_group(shape, from_ref, to_ref, sem, g).wait()
        return carry

    lax.fori_loop(0, shape[0] // UNROLL, finish, 0)


def nothing(s):
    return 0.0


def first_step_kernel(shape, diff_ref, state_ref, vel_ref, out_ref, u0_ref, u1_ref, in_sem, out_sem):
    for g in range(shape[0] // UNROLL):
        send_group(shape, state_ref, u0_ref, in_sem, g).start()
    finish_groups(shape, state_ref, u0_ref, in_sem)
    advance(
        shape, diff_ref, vel_ref, u0_ref, u1_ref, nothing, nothing, lambda x: nothing, lambda x: nothing,
        lambda g: send_group(shape, u1_ref, out_ref, out_sem, g).start(),
    )
    finish_groups(shape, u1_ref, out_ref, out_sem)


def late_step_kernel(
    shape, late_ref, left_ref, fine_at_ref, coarse_at_ref, again_ref, diff_ref, second_in_ref, rest_ref, state_ref,
    vel_in_ref, _, out_ref, u0_ref, u1_ref, held_ref, plane_ref, sem, second_ref, vel_ref, load_sem, out_sem,
):
    planes, species, rows, lanes = shape
    half = rows // 2
    size = species * rows
    loads = load_all(
        [(second_in_ref, second_ref), (state_ref, u0_ref.at[size : size + planes * size]), (vel_in_ref, vel_ref)], load_sem
    )
    u0_ref[0:size] = jnp.zeros((size, lanes), jnp.float32)
    u0_ref[size + planes * size : 2 * size + planes * size] = jnp.zeros((size, lanes), jnp.float32)
    for load in loads[:2]:
        load.wait()

    def half_plane(x, h, ref, slot):
        for s in range(species):
            base = pl.multiple_of((x + 1) * size + s * rows + h * half, half)
            u0_ref[pl.ds(base, half), :] = ref[slot, s]

    def whole_plane(x):
        for s in range(species):
            u0_ref[pl.ds(pl.multiple_of((x + 1) * size + s * rows, rows), rows), :] = plane_ref[s]

    late_units(
        shape, late_ref, left_ref, fine_at_ref, coarse_at_ref, second_ref, rest_ref, held_ref, plane_ref,
        sem, half_plane, whole_plane,
    )

    def send(x):
        part = pl.ds(pl.multiple_of(x * size, size), size)
        return pltpu.make_async_copy(u1_ref.at[part], out_ref.at[part], out_sem.at[x])

    def take(i, carry):
        for x in (again_ref[2 * i], again_ref[2 * i + 1]):
            read, write = jnp.maximum(x, 0), jnp.where(x < 0, planes, x)

            def store(s, new):
                u1_ref[pl.ds(pl.multiple_of(write * size + s * rows, rows), rows), :] = new

            around = [planes_of(u0_ref, read + 1 + j, rows, size) for j in (0, -1, 1)]
            advance_plane(diff_ref, [vel_ref[read, k] for k in range(3)], *around, nothing, nothing, store)
        return carry

    def each(act):
        def body(i, carry):
            act(send(again_ref[i]))
            return carry

        lax.fori_loop(0, count, body, 0)

    loads[2].wait()
    count = again_ref[planes]
    lax.fori_loop(0, (count + 1) // 2, take, 0)
    each(lambda copy: copy.start())
    each(lambda copy: copy.wait())


def second_step_kernel(
    shape, inside_ref, diff_ref, first_ref, vel_in_ref, ylow_own_ref, yhigh_own_ref, xlow_own_ref, xhigh_own_ref, ylow_ref,
    yhigh_ref, xlow_ref, xhigh_ref, vylow_own_ref, vyhigh_own_ref, vylow_ref, vyhigh_ref, vxlow_ref, vxhigh_ref,
    out_ref, u1_ref, u2_ref, row_low_ref, row_high_ref, plane_low_ref, plane_high_ref, vel_ref, load_sem, out_sem,
):
    planes, species, rows, lanes = shape
    size = species * rows
    deep = ITERS * size
    loads = load_all([(first_ref, u1_ref), (vel_in_ref, vel_ref)], load_sem)

    for (near_ref, near, far, own_ref, own, v_ref, corner, target_ref, inside) in (
        (ylow_ref, 1, 0, ylow_own_ref, 0, vylow_ref, deep, row_low_ref, 0),
        (yhigh_ref, 0, 1, yhigh_own_ref, 1, vyhigh_ref, deep + 16, row_high_ref, 1),
    ):
        for x in range(0, planes, 16):
            flow = Flow([v_ref[k * planes + x : k * planes + x + 16] for k in range(3)])
            for s in range(species):

                def band(ref, r):
                    start = (r * species + s) * planes + x
                    return ref[start : start + 16]

                u = band(near_ref, near)
                start = (near * species + s) * planes
                if x == 0:
                    first = xlow_ref[corner + s : corner + s + 1]
                else:
                    first = near_ref[start + x - 1 : start + x]
                if x + 16 == planes:
                    last = xhigh_ref[corner + s : corner + s + 1]
                else:
                    last = near_ref[start + x + 16 : start + x + 17]
                outer, inner = band(near_ref, far), band(own_ref, own)
                across = (outer, inner) if inside == 0 else (inner, outer)
                new = flow.step(u, (along(u, first, last, 0), across, along(u, u, u, 1)), diff_ref[s])
                target_ref[s * planes + x : s * planes + x + 16] = new * inside_ref[inside]

    def at(ref, x):
        return planes_of(ref, x, rows, size)

    for (halo_ref, near, below, above, v_ref, target_ref, inside) in (
        (xlow_ref, 1, at(xlow_ref, 0), at(xlow_own_ref, 0), vxlow_ref, plane_low_ref, 2),
        (xhigh_ref, 0, at(xhigh_own_ref, ITERS - 1), at(xhigh_ref, 1), vxhigh_ref, plane_high_ref, 3),
    ):

        def store(s, new):
            target_ref[s * rows : (s + 1) * rows] = new * inside_ref[inside]

        def corner(offset):
            return lambda s: halo_ref[deep + offset + s : deep + offset + s + 1]

        velocity = [v_ref[k * rows : (k + 1) * rows] for k in range(3)]
        advance_plane(diff_ref, velocity, at(halo_ref, near), below, above, corner(0), corner(16), store)

    for load in loads:
        load.wait()
    for x in range(0, planes, 8):
        up = jnp.maximum(vylow_own_ref[planes + x : planes + x + 8], 0.0)
        down = jnp.minimum(vyhigh_own_ref[planes + x : planes + x + 8], 0.0)
        for s in range(species):
            low = pl.ds((x * species + s) * rows, 8, stride=size)
            high = pl.ds((x * species + s) * rows + rows - 1, 8, stride=size)
            start = species * planes + s * planes + x
            u1_ref[low, :] = u1_ref[low, :] + (diff_ref[s] + up) * ylow_ref[start : start + 8]
            start = s * planes + x
            u1_ref[high, :] = u1_ref[high, :] + (diff_ref[s] - down) * yhigh_ref[start : start + 8]
    up = jnp.maximum(vel_ref[0, 0], 0.0)
    down = jnp.minimum(vel_ref[planes - 1, 0], 0.0)
    for s in range(species):
        low = slice(s * rows, (s + 1) * rows)
        high = slice((planes - 1) * size + s * rows, (planes - 1) * size + (s + 1) * rows)
        u1_ref[low] = u1_ref[low] + (diff_ref[s] + up) * at(xlow_ref, 1)(s)
        u1_ref[high] = u1_ref[high] + (diff_ref[s] - down) * at(xhigh_ref, 0)(s)

    def edge(ref):
        return lambda x: lambda s: ref[pl.ds(s * planes + x, 1), :]

    advance(
        shape, diff_ref, vel_ref, u1_ref, u2_ref, at(plane_low_ref, 0), at(plane_high_ref, 0), edge(row_low_ref),
        edge(row_high_ref), lambda g: send_group(shape, u2_ref, out_ref, out_sem, g).start(),
    )
    finish_groups(shape, u2_ref, out_ref, out_sem)


def empty_kernel(out_ref):
    pass


def cost(microseconds):
    return pl.CostEstimate(flops=0, bytes_accessed=int(microseconds * 3.6e6), transcendentals=0)


def neighbours(axis, low, high):
    size = lax.axis_size(axis)
    up = [(i, (i + 1) % size) for i in range(size - 1)]
    return lax.ppermute(high, axis, up), lax.ppermute(low, axis, [(b, a) for a, b in up])


def on_device(old_fine, old_ids, old_coarse, coarse_ids, velocity, diffusion):
    devices = lax.axis_size("dev")
    me = lax.axis_index("dev")
    me_ref = me.reshape(1).astype(jnp.int32)
    planes, species, rows, lanes = old_fine.shape
    half = rows // 2
    coarse_planes = old_coarse.shape[0]
    unit_count = DIRECT + EXTRA
    f32 = jnp.float32
    i32 = jnp.int32

    def units_shape(count):
        return jax.ShapeDtypeStruct((count, species, half, lanes), f32)

    own, own_coarse = old_ids[0], coarse_ids[0]
    labels = jnp.broadcast_to(jnp.concatenate([own, own_coarse])[None], (devices, planes + coarse_planes))
    labels = lax.all_to_all(labels, "dev", split_axis=0, concat_axis=0, tiled=True)
    all_ids, all_coarse = labels[:, :planes], labels[:, planes:]
    all_box = jnp.where(all_ids >= 0, all_ids // planes, -1)
    all_coarse_box = all_coarse // coarse_planes
    flat_parents = jnp.where(all_ids >= 0, all_ids // 2, -1).reshape(-1)

    def needed(coarse):
        kept = jnp.sum((flat_parents == coarse[..., None]).astype(i32), axis=-1)
        return kept < 2

    box = jnp.arange(lanes) % devices
    fine_units = jnp.sum((all_box[:, None, :] == box[None, :, None]).astype(i32), axis=-1)
    asked = needed(all_coarse)[:, None, :] & (all_coarse_box[:, None, :] == box[None, :, None])
    units = 2 * fine_units + jnp.max(asked.astype(i32), axis=-1)
    row, column, left = pl.pallas_call(
        plan_kernel,
        out_shape=[
            jax.ShapeDtypeStruct((EXTRA, lanes), i32),
            jax.ShapeDtypeStruct((devices, lanes), i32),
            jax.ShapeDtypeStruct((1,), i32),
        ],
        in_specs=[SMEM, VMEM],
        out_specs=[VMEM, VMEM, SMEM],
        name="plan",
    )(me_ref, units)
    own_box = jnp.where(own >= 0, own // planes, -1)
    send_fine = jnp.where(own >= 0, own_box * FINE_CAP + ranks(own_box), -1)
    own_coarse_box = own_coarse // coarse_planes
    before = jnp.sum((own_box[None, :] == own_coarse_box[:, None]).astype(i32), axis=1)
    send_coarse = (own_coarse_box * unit_count + 2 * before) * 2 + ranks(own_coarse_box)
    send_coarse = jnp.where(needed(own_coarse), send_coarse, -1)

    order = jnp.arange(devices)[:, None]
    wanted = me * planes + jnp.arange(planes)
    fine_at = jnp.where(all_ids[None] == wanted[:, None, None], (order * FINE_CAP + ranks(all_box))[None], -1)
    fine_at = jnp.max(fine_at, axis=(1, 2))
    to_me = jnp.sum((all_box == me).astype(i32), axis=1, keepdims=True)
    coarse_wanted = me * coarse_planes + jnp.arange(coarse_planes)
    coarse_code = (order * unit_count + 2 * to_me) * 2 + ranks(all_coarse_box)
    coarse_at = jnp.where(all_coarse[None] == coarse_wanted[:, None, None], coarse_code[None], 0)
    coarse_at = jnp.max(coarse_at, axis=(1, 2))

    def exchange(value):
        return lax.all_to_all(value, "dev", split_axis=0, concat_axis=0, tiled=True)

    def pack(count, first, name):
        return pl.pallas_call(
            functools.partial(pack_kernel, devices, first),
            out_shape=units_shape(count),
            in_specs=[SMEM] * 4 + [ANY, VMEM],
            out_specs=VMEM,
            scratch_shapes=[pltpu.VMEM(old_fine.shape, f32), pltpu.SemaphoreType.DMA((4,))],
            compiler_params=PARAMS,
            name=name,
        )(me_ref, send_fine, send_coarse, row, old_fine, old_coarse)

    packed = pack(devices * DIRECT, True, "pack")

    def no_rest():
        return pl.pallas_call(empty_kernel, out_shape=units_shape(devices * EXTRA), out_specs=ANY, name="nothing")()

    def rest_direct():
        return exchange(pack(devices * EXTRA, False, "pack_rest"))

    rest = lax.cond(left[0] == 0, no_rest, rest_direct)
    packed, rest, flow = lax.optimization_barrier((packed, rest, velocity))
    first = exchange(packed)

    def edge_shapes(deep, count):
        along_y = jax.ShapeDtypeStruct((deep * count * planes, lanes), f32)
        along_x = jax.ShapeDtypeStruct((deep * count * rows, lanes), f32)
        return [along_y, along_y, along_x, along_x]

    directions = flow.shape[1]
    vylow, vyhigh, vxlow, vxhigh = pl.pallas_call(
        functools.partial(velocity_edges_kernel, shape=flow.shape),
        out_shape=edge_shapes(1, directions),
        in_specs=[VMEM],
        out_specs=[VMEM] * 4,
        compiler_params=PARAMS,
        name="velocity_edges",
    )(flow.reshape(planes * directions * rows, lanes))
    flow_edges = [*neighbours("grp", vylow, vyhigh), *neighbours("dev", vxlow, vxhigh)]
    first, *flow_edges = lax.optimization_barrier((first, *flow_edges))
    second = pl.pallas_call(
        forward_kernel,
        out_shape=units_shape(devices),
        in_specs=[SMEM] * 2 + [ANY],
        out_specs=VMEM,
        scratch_shapes=[pltpu.SemaphoreType.DMA((devices,))],
        compiler_params=PARAMS,
        cost_estimate=cost(3),
        name="forward",
    )(me_ref, column, first)
    second = exchange(second)

    size = species * rows
    state_shape = jax.ShapeDtypeStruct((planes * size, lanes), f32)
    state, *edges = pl.pallas_call(
        functools.partial(build_kernel, old_fine.shape),
        out_shape=[state_shape] + edge_shapes(ITERS, species),
        in_specs=[SMEM] * 2 + [VMEM],
        out_specs=[VMEM] * 5,
        compiler_params=PARAMS,
        cost_estimate=cost(10),
        name="build",
    )(fine_at, coarse_at, first)
    relay_of = (jnp.arange(devices)[:, None] + me + column[:, :EXTRA] // 8) % devices

    def through(source, unit, used):
        over = jnp.arange(EXTRA) == (unit - DIRECT)[:, None]
        hit = (source[:, None, None] == jnp.arange(devices)[None, :, None]) & over[:, None, :]
        relay = jnp.max(jnp.where(hit, relay_of[None], -1), axis=(1, 2))
        return jnp.where(used & (unit >= DIRECT), relay, -1)

    order = jnp.arange(devices)
    halves = jnp.arange(2 * planes)
    at = jnp.repeat(fine_at, 2)
    relay = through(at // FINE_CAP, 2 * (at % FINE_CAP) + halves % 2, at >= 0)
    late_fine = jnp.max(jnp.where(relay[:, None] == order[None], halves[:, None], -1), axis=0)
    parents = jnp.arange(coarse_planes)
    code = coarse_at // 2
    fresh = jnp.min(fine_at.reshape(coarse_planes, 2), axis=1) < 0
    relay = through(code // unit_count, code % unit_count, fresh)
    late_parents = [
        jnp.max(jnp.where((relay[:, None] == order[None]) & (coarse_at % 2 == j)[:, None], parents[:, None], -1), axis=0)
        for j in range(COARSE_CAP)
    ]
    late = jnp.concatenate([late_fine, *late_parents])
    late_child = jnp.repeat(fresh & (code % unit_count >= DIRECT), 2) & (fine_at < 0)
    late_plane = late_child | ((fine_at >= 0) & (2 * (fine_at % FINE_CAP) + 1 >= DIRECT))
    beside = jnp.pad(late_plane, 1)
    new_plane = jnp.arange(planes)
    again = beside[:-2] | beside[1:-1] | beside[2:]
    place = jnp.sum((again[None, :] & (new_plane[None, :] < new_plane[:, None])).astype(i32), axis=1)
    listed = again[None, :] & (place[None, :] == new_plane[:, None])
    again = jnp.concatenate(
        [jnp.max(jnp.where(listed, new_plane[None, :], -1), axis=1), jnp.sum(again.astype(i32)).reshape(1)]
    )
    late_scratch = [
        pltpu.VMEM((1, species, half, lanes), f32),
        pltpu.VMEM((species, rows, lanes), f32),
        pltpu.SemaphoreType.DMA,
    ]
    state_scratch = pltpu.VMEM(state_shape.shape, f32)
    group_sems = pltpu.SemaphoreType.DMA((planes // UNROLL,))
    stepped = pl.pallas_call(
        functools.partial(first_step_kernel, old_fine.shape),
        out_shape=state_shape,
        in_specs=[SMEM, ANY, VMEM],
        out_specs=ANY,
        scratch_shapes=[state_scratch] * 2 + [group_sems] * 2,
        compiler_params=PARAMS,
        cost_estimate=cost(10),
        name="first_step",
    )(diffusion, state, velocity)
    second, stepped = lax.optimization_barrier((second, stepped))
    ylow_own, yhigh_own, xlow_own, xhigh_own = pl.pallas_call(
        functools.partial(edges_kernel, old_fine.shape),
        out_shape=edge_shapes(ITERS, species),
        in_specs=[SMEM] * 4 + [ANY] * 6,
        out_specs=[VMEM] * 4,
        scratch_shapes=late_scratch + [pltpu.VMEM(second.shape, f32), pltpu.SemaphoreType.DMA((5,))],
        compiler_params=room(12),
        cost_estimate=cost(4),
        name="edges",
    )(late, left, fine_at, coarse_at, second, rest, *edges)
    ylow, yhigh = neighbours("grp", ylow_own, yhigh_own)
    stepped = pl.pallas_call(
        functools.partial(late_step_kernel, old_fine.shape),
        out_shape=state_shape,
        in_specs=[SMEM] * 6 + [ANY] * 5,
        out_specs=ANY,
        scratch_shapes=[pltpu.VMEM(((planes + 2) * size, lanes), f32), pltpu.VMEM(((planes + 1) * size, lanes), f32)]
        + late_scratch
        + [pltpu.VMEM(second.shape, f32), pltpu.VMEM(velocity.shape, f32), pltpu.SemaphoreType.DMA((3,))]
        + [pltpu.SemaphoreType.DMA((planes,))],
        input_output_aliases={10: 0},
        compiler_params=room(24),
        cost_estimate=cost(7),
        name="late_step",
    )(late, left, fine_at, coarse_at, again, diffusion, second, rest, state, velocity, stepped)
    ylow, yhigh, stepped = lax.optimization_barrier((ylow, yhigh, stepped))
    message = jax.ShapeDtypeStruct((ITERS * size + 32, lanes), f32)
    down, up = pl.pallas_call(
        functools.partial(corners_kernel, planes, species),
        out_shape=[message] * 2,
        in_specs=[VMEM] * 4,
        out_specs=[VMEM] * 2,
        compiler_params=room(8),
        name="corners",
    )(ylow, yhigh, xlow_own, xhigh_own)
    xlow, xhigh = neighbours("dev", down, up)
    grp, dev = lax.axis_index("grp"), lax.axis_index("dev")
    inside = jnp.stack([grp > 0, grp < lax.axis_size("grp") - 1, dev > 0, dev < devices - 1]).astype(f32)
    row_edge = pltpu.VMEM((species * planes, lanes), f32)
    plane_edge = pltpu.VMEM((size, lanes), f32)
    done = pl.pallas_call(
        functools.partial(second_step_kernel, old_fine.shape),
        out_shape=state_shape,
        in_specs=[SMEM] * 2 + [ANY] * 2 + [VMEM] * 14,
        out_specs=ANY,
        scratch_shapes=[state_scratch] * 2
        + [row_edge] * 2
        + [plane_edge] * 2
        + [pltpu.VMEM(velocity.shape, f32), pltpu.SemaphoreType.DMA((2,)), group_sems],
        compiler_params=room(28),
        cost_estimate=cost(10),
        name="second_step",
    )(
        inside, diffusion, stepped, velocity, ylow_own, yhigh_own, xlow_own, xhigh_own, ylow, yhigh, xlow, xhigh,
        vylow, vyhigh, *flow_edges,
    )
    return done.reshape(old_fine.shape)


def solution(mesh):
    in_specs = (
        P("dev", None, "grp", None),
        P("grp", "dev"),
        P("dev", None, "grp", None),
        P("grp", "dev"),
        P("dev", None, "grp", None),
        P(),
    )
    out_specs = P("dev", None, "grp", None)
    return jax.shard_map(
        on_device, mesh=mesh, in_specs=in_specs, out_specs=out_specs, check_vma=False
    )
```

```python
import functools

import jax
import jax.numpy as jnp
from jax import lax
from jax.experimental import pallas as pl
from jax.experimental.pallas import tpu as pltpu
from jax.sharding import PartitionSpec as P

ITERS = 2
FINE_CAP = 4
COARSE_CAP = 2
DIRECT = 5
EXTRA = 2 * FINE_CAP + 1 - DIRECT
VMEM = pl.BlockSpec(memory_space=pltpu.VMEM)
SMEM = pl.BlockSpec(memory_space=pltpu.SMEM)
ANY = pl.BlockSpec(memory_space=pl.ANY)
PARAMS = pltpu.CompilerParams(vmem_limit_bytes=58 * 1024 * 1024)
UNROLL = 4


def ranks(boxes):
    count = boxes.shape[-1]
    earlier = jnp.arange(count)[None, :] < jnp.arange(count)[:, None]
    same = boxes[..., None, :] == boxes[..., :, None]
    return jnp.sum((same & earlier).astype(jnp.int32), axis=-1)


def plan_kernel(me_ref, units_ref, row_ref, column_ref, left_ref):
    devices, lanes = units_ref.shape
    me = me_ref[0]
    units = units_ref[...]
    source = lax.broadcasted_iota(jnp.int32, units.shape, 0)
    lane = lax.broadcasted_iota(jnp.int32, units.shape, 1)
    none = jnp.full(units.shape, -1, jnp.int32)

    def one_round(r, carry):
        left, codes, free, second, through = carry
        ok = (left > 0) & (free > 0) & (second > 0)
        position = DIRECT - free
        code = jnp.left_shift(r * 8 + position, 8 * jnp.maximum(left - 1, 0))
        codes = jnp.where(ok, codes | code, codes)
        through = jnp.where(ok, source * 8 + position, through)
        used = ok.astype(jnp.int32)
        left, free, second = left - used, free - used, second - used
        return (
            pltpu.roll(left, 1, 1),
            pltpu.roll(codes, 1, 1),
            free,
            pltpu.roll(second, devices - 1, 0),
            pltpu.roll(through, devices - 1, 0),
        )

    surplus = pltpu.roll(jnp.maximum(units - DIRECT, 0), 0, 1, stride=1, stride_axis=0)
    free = jnp.maximum(DIRECT - units, 0)
    init = (surplus, jnp.zeros_like(units), free, jnp.ones_like(units), none)
    left, codes, _, _, through = lax.fori_loop(0, devices, one_round, init)
    column = none
    for i in range(EXTRA):
        chosen = jnp.where(left <= i, lax.shift_right_logical(codes, jnp.full_like(codes, 8 * i)) & 255, -1)
        row_ref[i : i + 1] = jnp.max(jnp.where(source == me, chosen, -1), axis=0, keepdims=True)
        mine = (lane < devices) & (lane == (source + me) % devices)
        found = jnp.max(jnp.where(mine, chosen, -1), axis=1, keepdims=True)
        column = jnp.where(lane == i, found, column)
    found = jnp.max(jnp.where(lane == me, through, -1), axis=1, keepdims=True)
    column_ref[...] = jnp.where(lane == EXTRA, found, column)
    left_ref[0] = jnp.max(left.astype(jnp.float32)).astype(jnp.int32)


def pack_kernel(
    devices, first, me_ref, fine_at_ref, coarse_at_ref, row_ref, fine_in_ref, coarse_ref, out_ref, fine_ref, sem
):
    planes = fine_ref.shape[0]
    coarse_planes, _, half, depth = coarse_ref.shape
    part = planes // sem.shape[0]

    def bring(i):
        planes_of = pl.ds(i * part, part)
        return pltpu.make_async_copy(fine_in_ref.at[planes_of], fine_ref.at[planes_of], sem.at[i])

    def slot_of(box, unit):
        if first:
            return first_slot(devices, me_ref[0], row_ref, box, unit)
        return jnp.where(unit < DIRECT, -1, box * EXTRA + unit - DIRECT)

    for i in range(sem.shape[0]):
        bring(i).start()

    def coarse_plane(k, carry):
        code = coarse_at_ref[k]

        @pl.when(code >= 0)
        def _():
            at = code // 2
            slot = slot_of(at // (DIRECT + EXTRA), at % (DIRECT + EXTRA))
            for j in range(2):

                @pl.when((slot >= 0) & (code % 2 == j))
                def _():
                    out_ref[slot, :, :, j * depth : (j + 1) * depth] = coarse_ref[k]

        return carry

    lax.fori_loop(0, coarse_planes, coarse_plane, 0)

    def fine_plane(k, carry):
        code = fine_at_ref[k]
        box, rank = code // FINE_CAP, code % FINE_CAP
        whole = DIRECT // 2

        if first:

            @pl.when((code >= 0) & (rank < whole))
            def _():
                for h in range(2):
                    out_ref[box * DIRECT + 2 * rank + h] = fine_ref[k, :, h * half : (h + 1) * half, :]

        @pl.when((code >= 0) & (rank >= whole))
        def _():
            for h in range(2):
                slot = slot_of(box, 2 * rank + h)

                @pl.when(slot >= 0)
                def _():
                    out_ref[slot] = fine_ref[k, :, h * half : (h + 1) * half, :]

        return carry

    for i in range(sem.shape[0]):
        bring(i).wait()
        lax.fori_loop(i * part, (i + 1) * part, fine_plane, 0)


def first_slot(devices, me, row_ref, box, unit):
    t = (me + box) % devices
    code = row_ref[jnp.maximum(unit - DIRECT, 0), t]
    relay = jnp.where(code >= 0, ((t + code // 8) % devices) * DIRECT + code % 8, -1)
    return jnp.where(unit < DIRECT, box * DIRECT + unit, relay)


def forward_kernel(me_ref, column_ref, in_ref, out_ref, sem):
    devices = out_ref.shape[0]

    def each(act):
        def body(a, carry):
            code = column_ref[a, EXTRA]

            @pl.when(code >= 0)
            def _():
                box = (me_ref[0] - a + devices) % devices
                act(pltpu.make_async_copy(in_ref.at[(code // 8) * DIRECT + code % 8], out_ref.at[box], sem.at[a]))

            return carry

        lax.fori_loop(0, devices, body, 0)

    each(lambda copy: copy.start())
    each(lambda copy: copy.wait())


def rows_to_edges(flat_ref, edge_ref, offset, row, planes, species, rows):
    for s in range(species):
        for x in range(0, planes, 8):
            at = offset + s * planes + x
            edge_ref[at : at + 8] = flat_ref[pl.ds((x * species + s) * rows + row, 8, stride=species * rows), :]


def interpolate(ref, slot, part, store):
    _, species, half, lanes = ref.shape
    lane = lax.broadcasted_iota(jnp.int32, (half, lanes), 1)
    row = lax.broadcasted_iota(jnp.int32, (half, lanes), 0)
    sign = jnp.where(lane % 2 == 0, -0.25, 0.25)
    lane_first = lane % (lanes // 2) == 0
    lane_last = lane % (lanes // 2) == lanes // 2 - 1
    index = part * (lanes // 2) + lane // 2
    for s in range(species):
        p = ref[slot, s]
        below = jnp.where(row == 0, p, pltpu.roll(p, 1, 0))
        above = jnp.where(row == half - 1, p, pltpu.roll(p, half - 1, 0))
        left = jnp.where(lane_first, p, pltpu.roll(p, 1, 1))
        right = jnp.where(lane_last, p, pltpu.roll(p, lanes - 1, 1))
        slope_y = 0.125 * (above - below)
        slope_z = 0.5 * (right - left)
        gz = jnp.take_along_axis(slope_z, index, axis=1) * sign
        even = jnp.take_along_axis(p - slope_y, index, axis=1) + gz
        odd = jnp.take_along_axis(p + slope_y, index, axis=1) + gz
        store(s, even, odd)


def build_kernel(shape, fine_at_ref, coarse_at_ref, first_ref, out_ref, ylow_ref, yhigh_ref, xlow_ref, xhigh_ref):
    planes, species, rows, lanes = shape
    half = rows // 2

    def body(c, carry):
        at = [fine_at_ref[2 * c], fine_at_ref[2 * c + 1]]
        code = coarse_at_ref[c]
        unit = code // 2 % (DIRECT + EXTRA)

        @pl.when(((at[0] < 0) | (at[1] < 0)) & (unit < DIRECT))
        def _():
            def store(s, even, odd):
                for child in range(2):
                    base = pl.multiple_of(((2 * c + child) * species + s) * rows, rows)
                    out_ref[pl.ds(base, half, stride=2), :] = even
                    out_ref[pl.ds(base + 1, half, stride=2), :] = odd

            interpolate(first_ref, code // 2 // (DIRECT + EXTRA) * DIRECT + unit, code % 2, store)

        for child in range(2):
            for h in range(2):
                late = 2 * (at[child] % FINE_CAP) + h

                @pl.when((at[child] >= 0) & (late < DIRECT))
                def _():
                    slot = at[child] // FINE_CAP * DIRECT + late
                    for s in range(species):
                        base = pl.multiple_of(((2 * c + child) * species + s) * rows + h * half, half)
                        out_ref[pl.ds(base, half), :] = first_ref[slot, s]

        return carry

    lax.fori_loop(0, planes // 2, body, 0)
    for r in range(ITERS):
        rows_to_edges(out_ref, ylow_ref, r * species * planes, r, planes, species, rows)
        rows_to_edges(out_ref, yhigh_ref, r * species * planes, rows - ITERS + r, planes, species, rows)
    deep = ITERS * species * rows
    xlow_ref[...] = out_ref[0:deep]
    xhigh_ref[...] = out_ref[planes * species * rows - deep : planes * species * rows]


def late_units(shape, late_ref, left_ref, fine_at_ref, coarse_at_ref, second_ref, rest_ref, held_ref,
               plane_ref, sem, half_plane, whole_plane):
    planes, _, rows, _ = shape
    half = rows // 2
    planned = left_ref[0] == 0

    def children(c, ref, slot):
        def store(s, even, odd):
            plane_ref[s, pl.ds(0, half, stride=2), :] = even
            plane_ref[s, pl.ds(1, half, stride=2), :] = odd

        interpolate(ref, slot, coarse_at_ref[c] % 2, store)
        for child in range(2):

            @pl.when(fine_at_ref[2 * c + child] < 0)
            def _():
                whole_plane(2 * c + child)

    def from_relay(m, carry):
        what = late_ref[m]

        @pl.when((what >= 0) & (what < 2 * planes))
        def _():
            for h in range(2):

                @pl.when(what % 2 == h)
                def _():
                    half_plane(what // 2, h, second_ref, m)

        for more in range(2):
            parent = late_ref[(1 + more) * late_ref.shape[0] // 3 + m]

            @pl.when(parent >= 0)
            def _():
                children(parent, second_ref, m)

        return carry

    @pl.when(planned)
    def _():
        lax.fori_loop(0, second_ref.shape[0], from_relay, 0)

    def bring(source, unit):
        copy = pltpu.make_async_copy(
            rest_ref.at[pl.ds(source * EXTRA + jnp.maximum(unit - DIRECT, 0), 1)], held_ref, sem
        )
        copy.start()
        copy.wait()

    def direct(c, carry):
        code = coarse_at_ref[c]
        unit = code // 2 % (DIRECT + EXTRA)

        @pl.when(((fine_at_ref[2 * c] < 0) | (fine_at_ref[2 * c + 1] < 0)) & (unit >= DIRECT))
        def _():
            bring(code // 2 // (DIRECT + EXTRA), unit)
            children(c, held_ref, 0)

        for x in (2 * c, 2 * c + 1):
            at = fine_at_ref[x]
            for h in range(2):
                late = 2 * (at % FINE_CAP) + h

                @pl.when((at >= 0) & (late >= DIRECT))
                def _():
                    bring(at // FINE_CAP, late)
                    half_plane(x, h, held_ref, 0)

        return carry

    @pl.when(jnp.logical_not(planned))
    def _():
        lax.fori_loop(0, planes // 2, direct, 0)


def load_all(pairs, sem):
    copies = [pltpu.make_async_copy(source, target, sem.at[i]) for i, (source, target) in enumerate(pairs)]
    for copy in copies:
        copy.start()
    return copies


def edges_kernel(
    shape, late_ref, left_ref, fine_at_ref, coarse_at_ref, second_in_ref, rest_ref,
    ylow_in_ref, yhigh_in_ref, xlow_in_ref, xhigh_in_ref,
    ylow_ref, yhigh_ref, xlow_ref, xhigh_ref, held_ref, plane_ref, sem, second_ref, load_sem,
):
    planes, species, rows, _ = shape
    half = rows // 2
    size = species * rows
    loads = load_all(
        [
            (second_in_ref, second_ref),
            (ylow_in_ref, ylow_ref),
            (yhigh_in_ref, yhigh_ref),
            (xlow_in_ref, xlow_ref),
            (xhigh_in_ref, xhigh_ref),
        ],
        load_sem,
    )
    for load in loads:
        load.wait()

    def half_edges(x, h, value):
        edge_ref, first = ((ylow_ref, 0), (yhigh_ref, half - ITERS))[h]
        for s in range(species):
            for r in range(ITERS):
                edge_ref[pl.ds((r * species + s) * planes + x, 1), :] = value(s, slice(first + r, first + r + 1))
        for near, xedge_ref, at in ((x < ITERS, xlow_ref, x), (x >= planes - ITERS, xhigh_ref, x - planes + ITERS)):

            @pl.when(near)
            def _():
                for s in range(species):
                    base = pl.multiple_of(at * size + s * rows + h * half, half)
                    xedge_ref[pl.ds(base, half), :] = value(s, slice(0, half))

    def half_plane(x, h, ref, slot):
        half_edges(x, h, lambda s, part: ref[slot, s, part])

    def whole_plane(x):
        for h in range(2):
            half_edges(x, h, lambda s, part: plane_ref[s, h * half + part.start : h * half + part.stop])

    late_units(
        shape, late_ref, left_ref, fine_at_ref, coarse_at_ref, second_ref, rest_ref, held_ref, plane_ref,
        sem, half_plane, whole_plane,
    )


def corners_kernel(planes, species, ylow_ref, yhigh_ref, xlow_ref, xhigh_ref, down_ref, up_ref):
    deep = xlow_ref.shape[0]
    down_ref[0:deep] = xlow_ref[...]
    up_ref[0:deep] = xhigh_ref[...]
    for message_ref, x in ((down_ref, 0), (up_ref, planes - 1)):
        for s in range(species):
            low = ((ITERS - 1) * species + s) * planes + x
            high = s * planes + x
            message_ref[deep + s : deep + s + 1] = ylow_ref[low : low + 1]
            message_ref[deep + 16 + s : deep + 16 + s + 1] = yhigh_ref[high : high + 1]
        for at in (deep + species, deep + 16 + species):
            message_ref[at : at + 16 - species] = jnp.zeros((16 - species, message_ref.shape[1]), jnp.float32)


def velocity_edges_kernel(vel_ref, ylow_ref, yhigh_ref, xlow_ref, xhigh_ref, *, shape):
    planes, directions, rows, _ = shape
    size = directions * rows
    rows_to_edges(vel_ref, ylow_ref, 0, 0, planes, directions, rows)
    rows_to_edges(vel_ref, yhigh_ref, 0, rows - 1, planes, directions, rows)
    xlow_ref[...] = vel_ref[0:size]
    xhigh_ref[...] = vel_ref[(planes - 1) * size : planes * size]


class Flow:
    def __init__(self, velocity):
        self.positive = [jnp.maximum(v, 0.0) for v in velocity]
        self.negative = [jnp.minimum(v, 0.0) for v in velocity]
        self.keep = 1.0
        for low, high in zip(self.positive, self.negative):
            self.keep = self.keep - (low - high)

    def step(self, u, neighbours, d):
        new = u * (self.keep - 6.0 * d)
        for k, (low, high) in enumerate(neighbours):
            new = new + low * (d + self.positive[k]) + high * (d - self.negative[k])
        return new


def along(u, first, last, dim):
    count = u.shape[dim]
    at = lax.broadcasted_iota(jnp.int32, u.shape, dim)
    low = jnp.where(at == 0, first, pltpu.roll(u, 1, dim))
    high = jnp.where(at == count - 1, last, pltpu.roll(u, count - 1, dim))
    return low, high


def advance_plane(diff_ref, velocity, center, below, above, y_low, y_high, store):
    flow = Flow(velocity)
    for s in range(diff_ref.shape[0]):
        u = center(s)
        sides = ((below(s), above(s)), along(u, y_low(s), y_high(s), 0), along(u, u, u, 1))
        store(s, flow.step(u, sides, diff_ref[s]))


def planes_of(ref, x, rows, size):
    return lambda s: ref[pl.ds(pl.multiple_of(x * size + s * rows, rows), rows), :]


def advance(shape, diff_ref, vel_ref, u_ref, new_ref, low, high, y_low, y_high, after):
    planes, species, rows, _ = shape
    size = species * rows

    def group(x, first, last):
        for i in range(UNROLL):

            def store(s, new):
                new_ref[pl.ds(pl.multiple_of((x + i) * size + s * rows, rows), rows), :] = new

            advance_plane(
                diff_ref,
                [vel_ref[x + i, k] for k in range(3)],
                planes_of(u_ref, x + i, rows, size),
                low if first and i == 0 else planes_of(u_ref, x + i - 1, rows, size),
                high if last and i == UNROLL - 1 else planes_of(u_ref, x + i + 1, rows, size),
                y_low(x + i),
                y_high(x + i),
                store,
            )
        after(x // UNROLL)

    def body(g, carry):
        group(g * UNROLL, False, False)
        return carry

    group(0, True, False)
    lax.fori_loop(1, planes // UNROLL - 1, body, 0)
    group(planes - UNROLL, False, True)


def send_group(shape, from_ref, to_ref, sem, g):
    size = UNROLL * shape[1] * shape[2]
    part = pl.ds(pl.multiple_of(g * size, size), size)
    return pltpu.make_async_copy(from_ref.at[part], to_ref.at[part], sem.at[g])


def finish_groups(shape, from_ref, to_ref, sem):
    def finish(g, carry):
        send_group(shape, from_ref, to_ref, sem, g).wait()
        return carry

    lax.fori_loop(0, shape[0] // UNROLL, finish, 0)


def nothing(s):
    return 0.0


def first_step_kernel(shape, diff_ref, state_ref, vel_ref, out_ref, u0_ref, u1_ref, in_sem, out_sem):
    for g in range(shape[0] // UNROLL):
        send_group(shape, state_ref, u0_ref, in_sem, g).start()
    finish_groups(shape, state_ref, u0_ref, in_sem)
    advance(
        shape, diff_ref, vel_ref, u0_ref, u1_ref, nothing, nothing, lambda x: nothing, lambda x: nothing,
        lambda g: send_group(shape, u1_ref, out_ref, out_sem, g).start(),
    )
    finish_groups(shape, u1_ref, out_ref, out_sem)


def late_step_kernel(
    shape, late_ref, left_ref, fine_at_ref, coarse_at_ref, again_ref, diff_ref, second_in_ref, rest_ref, state_ref,
    vel_in_ref, _, out_ref, u0_ref, u1_ref, held_ref, plane_ref, sem, second_ref, vel_ref, load_sem, out_sem,
):
    planes, species, rows, lanes = shape
    half = rows // 2
    size = species * rows
    loads = load_all(
        [(second_in_ref, second_ref), (state_ref, u0_ref.at[size : size + planes * size]), (vel_in_ref, vel_ref)], load_sem
    )
    u0_ref[0:size] = jnp.zeros((size, lanes), jnp.float32)
    u0_ref[size + planes * size : 2 * size + planes * size] = jnp.zeros((size, lanes), jnp.float32)
    for load in loads[:2]:
        load.wait()

    def half_plane(x, h, ref, slot):
        for s in range(species):
            base = pl.multiple_of((x + 1) * size + s * rows + h * half, half)
            u0_ref[pl.ds(base, half), :] = ref[slot, s]

    def whole_plane(x):
        for s in range(species):
            u0_ref[pl.ds(pl.multiple_of((x + 1) * size + s * rows, rows), rows), :] = plane_ref[s]

    late_units(
        shape, late_ref, left_ref, fine_at_ref, coarse_at_ref, second_ref, rest_ref, held_ref, plane_ref,
        sem, half_plane, whole_plane,
    )

    def send(x):
        part = pl.ds(pl.multiple_of(x * size, size), size)
        return pltpu.make_async_copy(u1_ref.at[part], out_ref.at[part], out_sem.at[x])

    def take(i, carry):
        for x in (again_ref[2 * i], again_ref[2 * i + 1]):
            read, write = jnp.maximum(x, 0), jnp.where(x < 0, planes, x)

            def store(s, new):
                u1_ref[pl.ds(pl.multiple_of(write * size + s * rows, rows), rows), :] = new

            around = [planes_of(u0_ref, read + 1 + j, rows, size) for j in (0, -1, 1)]
            advance_plane(diff_ref, [vel_ref[read, k] for k in range(3)], *around, nothing, nothing, store)
        return carry

    def each(act):
        def body(i, carry):
            act(send(again_ref[i]))
            return carry

        lax.fori_loop(0, count, body, 0)

    loads[2].wait()
    count = again_ref[planes]
    lax.fori_loop(0, (count + 1) // 2, take, 0)
    each(lambda copy: copy.start())
    each(lambda copy: copy.wait())


def second_step_kernel(
    shape, inside_ref, diff_ref, first_ref, vel_in_ref, ylow_own_ref, yhigh_own_ref, xlow_own_ref, xhigh_own_ref, ylow_ref,
    yhigh_ref, xlow_ref, xhigh_ref, vylow_own_ref, vyhigh_own_ref, vylow_ref, vyhigh_ref, vxlow_ref, vxhigh_ref,
    out_ref, u1_ref, u2_ref, row_low_ref, row_high_ref, plane_low_ref, plane_high_ref, vel_ref, load_sem, out_sem,
):
    planes, species, rows, lanes = shape
    size = species * rows
    deep = ITERS * size
    loads = load_all([(first_ref, u1_ref), (vel_in_ref, vel_ref)], load_sem)

    for (near_ref, near, far, own_ref, own, v_ref, corner, target_ref, inside) in (
        (ylow_ref, 1, 0, ylow_own_ref, 0, vylow_ref, deep, row_low_ref, 0),
        (yhigh_ref, 0, 1, yhigh_own_ref, 1, vyhigh_ref, deep + 16, row_high_ref, 1),
    ):
        for x in range(0, planes, 16):
            flow = Flow([v_ref[k * planes + x : k * planes + x + 16] for k in range(3)])
            for s in range(species):

                def band(ref, r):
                    start = (r * species + s) * planes + x
                    return ref[start : start + 16]

                u = band(near_ref, near)
                start = (near * species + s) * planes
                if x == 0:
                    first = xlow_ref[corner + s : corner + s + 1]
                else:
                    first = near_ref[start + x - 1 : start + x]
                if x + 16 == planes:
                    last = xhigh_ref[corner + s : corner + s + 1]
                else:
                    last = near_ref[start + x + 16 : start + x + 17]
                outer, inner = band(near_ref, far), band(own_ref, own)
                across = (outer, inner) if inside == 0 else (inner, outer)
                new = flow.step(u, (along(u, first, last, 0), across, along(u, u, u, 1)), diff_ref[s])
                target_ref[s * planes + x : s * planes + x + 16] = new * inside_ref[inside]

    def at(ref, x):
        return planes_of(ref, x, rows, size)

    for (halo_ref, near, below, above, v_ref, target_ref, inside) in (
        (xlow_ref, 1, at(xlow_ref, 0), at(xlow_own_ref, 0), vxlow_ref, plane_low_ref, 2),
        (xhigh_ref, 0, at(xhigh_own_ref, ITERS - 1), at(xhigh_ref, 1), vxhigh_ref, plane_high_ref, 3),
    ):

        def store(s, new):
            target_ref[s * rows : (s + 1) * rows] = new * inside_ref[inside]

        def corner(offset):
            return lambda s: halo_ref[deep + offset + s : deep + offset + s + 1]

        velocity = [v_ref[k * rows : (k + 1) * rows] for k in range(3)]
        advance_plane(diff_ref, velocity, at(halo_ref, near), below, above, corner(0), corner(16), store)

    for load in loads:
        load.wait()
    for x in range(0, planes, 8):
        up = jnp.maximum(vylow_own_ref[planes + x : planes + x + 8], 0.0)
        down = jnp.minimum(vyhigh_own_ref[planes + x : planes + x + 8], 0.0)
        for s in range(species):
            low = pl.ds((x * species + s) * rows, 8, stride=size)
            high = pl.ds((x * species + s) * rows + rows - 1, 8, stride=size)
            start = species * planes + s * planes + x
            u1_ref[low, :] = u1_ref[low, :] + (diff_ref[s] + up) * ylow_ref[start : start + 8]
            start = s * planes + x
            u1_ref[high, :] = u1_ref[high, :] + (diff_ref[s] - down) * yhigh_ref[start : start + 8]
    up = jnp.maximum(vel_ref[0, 0], 0.0)
    down = jnp.minimum(vel_ref[planes - 1, 0], 0.0)
    for s in range(species):
        low = slice(s * rows, (s + 1) * rows)
        high = slice((planes - 1) * size + s * rows, (planes - 1) * size + (s + 1) * rows)
        u1_ref[low] = u1_ref[low] + (diff_ref[s] + up) * at(xlow_ref, 1)(s)
        u1_ref[high] = u1_ref[high] + (diff_ref[s] - down) * at(xhigh_ref, 0)(s)

    def edge(ref):
        return lambda x: lambda s: ref[pl.ds(s * planes + x, 1), :]

    advance(
        shape, diff_ref, vel_ref, u1_ref, u2_ref, at(plane_low_ref, 0), at(plane_high_ref, 0), edge(row_low_ref),
        edge(row_high_ref), lambda g: send_group(shape, u2_ref, out_ref, out_sem, g).start(),
    )
    finish_groups(shape, u2_ref, out_ref, out_sem)


def empty_kernel(out_ref):
    pass


def cost(microseconds):
    return pl.CostEstimate(flops=0, bytes_accessed=int(microseconds * 3.6e6), transcendentals=0)


def neighbours(axis, low, high):
    size = lax.axis_size(axis)
    up = [(i, (i + 1) % size) for i in range(size - 1)]
    return lax.ppermute(high, axis, up), lax.ppermute(low, axis, [(b, a) for a, b in up])


def on_device(old_fine, old_ids, old_coarse, coarse_ids, velocity, diffusion):
    devices = lax.axis_size("dev")
    me = lax.axis_index("dev")
    me_ref = me.reshape(1).astype(jnp.int32)
    planes, species, rows, lanes = old_fine.shape
    half = rows // 2
    coarse_planes = old_coarse.shape[0]
    unit_count = DIRECT + EXTRA
    f32 = jnp.float32
    i32 = jnp.int32

    def units_shape(count):
        return jax.ShapeDtypeStruct((count, species, half, lanes), f32)

    own, own_coarse = old_ids[0], coarse_ids[0]
    labels = jnp.broadcast_to(jnp.concatenate([own, own_coarse])[None], (devices, planes + coarse_planes))
    labels = lax.all_to_all(labels, "dev", split_axis=0, concat_axis=0, tiled=True)
    all_ids, all_coarse = labels[:, :planes], labels[:, planes:]
    all_box = jnp.where(all_ids >= 0, all_ids // planes, -1)
    all_coarse_box = all_coarse // coarse_planes
    flat_parents = jnp.where(all_ids >= 0, all_ids // 2, -1).reshape(-1)

    def needed(coarse):
        kept = jnp.sum((flat_parents == coarse[..., None]).astype(i32), axis=-1)
        return kept < 2

    box = jnp.arange(lanes) % devices
    fine_units = jnp.sum((all_box[:, None, :] == box[None, :, None]).astype(i32), axis=-1)
    asked = needed(all_coarse)[:, None, :] & (all_coarse_box[:, None, :] == box[None, :, None])
    units = 2 * fine_units + jnp.max(asked.astype(i32), axis=-1)
    row, column, left = pl.pallas_call(
        plan_kernel,
        out_shape=[
            jax.ShapeDtypeStruct((EXTRA, lanes), i32),
            jax.ShapeDtypeStruct((devices, lanes), i32),
            jax.ShapeDtypeStruct((1,), i32),
        ],
        in_specs=[SMEM, VMEM],
        out_specs=[VMEM, VMEM, SMEM],
        name="plan",
    )(me_ref, units)
    own_box = jnp.where(own >= 0, own // planes, -1)
    send_fine = jnp.where(own >= 0, own_box * FINE_CAP + ranks(own_box), -1)
    own_coarse_box = own_coarse // coarse_planes
    before = jnp.sum((own_box[None, :] == own_coarse_box[:, None]).astype(i32), axis=1)
    send_coarse = (own_coarse_box * unit_count + 2 * before) * 2 + ranks(own_coarse_box)
    send_coarse = jnp.where(needed(own_coarse), send_coarse, -1)

    order = jnp.arange(devices)[:, None]
    wanted = me * planes + jnp.arange(planes)
    fine_at = jnp.where(all_ids[None] == wanted[:, None, None], (order * FINE_CAP + ranks(all_box))[None], -1)
    fine_at = jnp.max(fine_at, axis=(1, 2))
    to_me = jnp.sum((all_box == me).astype(i32), axis=1, keepdims=True)
    coarse_wanted = me * coarse_planes + jnp.arange(coarse_planes)
    coarse_code = (order * unit_count + 2 * to_me) * 2 + ranks(all_coarse_box)
    coarse_at = jnp.where(all_coarse[None] == coarse_wanted[:, None, None], coarse_code[None], 0)
    coarse_at = jnp.max(coarse_at, axis=(1, 2))

    def exchange(value):
        return lax.all_to_all(value, "dev", split_axis=0, concat_axis=0, tiled=True)

    def pack(count, first, name):
        return pl.pallas_call(
            functools.partial(pack_kernel, devices, first),
            out_shape=units_shape(count),
            in_specs=[SMEM] * 4 + [ANY, VMEM],
            out_specs=VMEM,
            scratch_shapes=[pltpu.VMEM(old_fine.shape, f32), pltpu.SemaphoreType.DMA((4,))],
            compiler_params=PARAMS,
            name=name,
        )(me_ref, send_fine, send_coarse, row, old_fine, old_coarse)

    packed = pack(devices * DIRECT, True, "pack")

    def no_rest():
        return pl.pallas_call(empty_kernel, out_shape=units_shape(devices * EXTRA), out_specs=ANY, name="nothing")()

    def rest_direct():
        return exchange(pack(devices * EXTRA, False, "pack_rest"))

    rest = lax.cond(left[0] == 0, no_rest, rest_direct)
    packed, rest, flow = lax.optimization_barrier((packed, rest, velocity))
    first = exchange(packed)

    def edge_shapes(deep, count):
        along_y = jax.ShapeDtypeStruct((deep * count * planes, lanes), f32)
        along_x = jax.ShapeDtypeStruct((deep * count * rows, lanes), f32)
        return [along_y, along_y, along_x, along_x]

    directions = flow.shape[1]
    vylow, vyhigh, vxlow, vxhigh = pl.pallas_call(
        functools.partial(velocity_edges_kernel, shape=flow.shape),
        out_shape=edge_shapes(1, directions),
        in_specs=[VMEM],
        out_specs=[VMEM] * 4,
        compiler_params=PARAMS,
        name="velocity_edges",
    )(flow.reshape(planes * directions * rows, lanes))
    flow_edges = [*neighbours("grp", vylow, vyhigh), *neighbours("dev", vxlow, vxhigh)]
    first, *flow_edges = lax.optimization_barrier((first, *flow_edges))
    second = pl.pallas_call(
        forward_kernel,
        out_shape=units_shape(devices),
        in_specs=[SMEM] * 2 + [ANY],
        out_specs=VMEM,
        scratch_shapes=[pltpu.SemaphoreType.DMA((devices,))],
        compiler_params=PARAMS,
        cost_estimate=cost(3),
        name="forward",
    )(me_ref, column, first)
    second = exchange(second)

    size = species * rows
    state_shape = jax.ShapeDtypeStruct((planes * size, lanes), f32)
    state, *edges = pl.pallas_call(
        functools.partial(build_kernel, old_fine.shape),
        out_shape=[state_shape] + edge_shapes(ITERS, species),
        in_specs=[SMEM] * 2 + [VMEM],
        out_specs=[VMEM] * 5,
        compiler_params=PARAMS,
        cost_estimate=cost(10),
        name="build",
    )(fine_at, coarse_at, first)
    relay_of = (jnp.arange(devices)[:, None] + me + column[:, :EXTRA] // 8) % devices

    def through(source, unit, used):
        over = jnp.arange(EXTRA) == (unit - DIRECT)[:, None]
        hit = (source[:, None, None] == jnp.arange(devices)[None, :, None]) & over[:, None, :]
        relay = jnp.max(jnp.where(hit, relay_of[None], -1), axis=(1, 2))
        return jnp.where(used & (unit >= DIRECT), relay, -1)

    order = jnp.arange(devices)
    halves = jnp.arange(2 * planes)
    at = jnp.repeat(fine_at, 2)
    relay = through(at // FINE_CAP, 2 * (at % FINE_CAP) + halves % 2, at >= 0)
    late_fine = jnp.max(jnp.where(relay[:, None] == order[None], halves[:, None], -1), axis=0)
    parents = jnp.arange(coarse_planes)
    code = coarse_at // 2
    fresh = jnp.min(fine_at.reshape(coarse_planes, 2), axis=1) < 0
    relay = through(code // unit_count, code % unit_count, fresh)
    late_parents = [
        jnp.max(jnp.where((relay[:, None] == order[None]) & (coarse_at % 2 == j)[:, None], parents[:, None], -1), axis=0)
        for j in range(COARSE_CAP)
    ]
    late = jnp.concatenate([late_fine, *late_parents])
    late_child = jnp.repeat(fresh & (code % unit_count >= DIRECT), 2) & (fine_at < 0)
    late_plane = late_child | ((fine_at >= 0) & (2 * (fine_at % FINE_CAP) + 1 >= DIRECT))
    beside = jnp.pad(late_plane, 1)
    new_plane = jnp.arange(planes)
    again = beside[:-2] | beside[1:-1] | beside[2:]
    place = jnp.sum((again[None, :] & (new_plane[None, :] < new_plane[:, None])).astype(i32), axis=1)
    listed = again[None, :] & (place[None, :] == new_plane[:, None])
    again = jnp.concatenate(
        [jnp.max(jnp.where(listed, new_plane[None, :], -1), axis=1), jnp.sum(again.astype(i32)).reshape(1)]
    )
    late_scratch = [
        pltpu.VMEM((1, species, half, lanes), f32),
        pltpu.VMEM((species, rows, lanes), f32),
        pltpu.SemaphoreType.DMA,
    ]
    state_scratch = pltpu.VMEM(state_shape.shape, f32)
    group_sems = pltpu.SemaphoreType.DMA((planes // UNROLL,))
    stepped = pl.pallas_call(
        functools.partial(first_step_kernel, old_fine.shape),
        out_shape=state_shape,
        in_specs=[SMEM, ANY, VMEM],
        out_specs=ANY,
        scratch_shapes=[state_scratch] * 2 + [group_sems] * 2,
        compiler_params=PARAMS,
        cost_estimate=cost(10),
        name="first_step",
    )(diffusion, state, velocity)
    second, stepped = lax.optimization_barrier((second, stepped))
    ylow_own, yhigh_own, xlow_own, xhigh_own = pl.pallas_call(
        functools.partial(edges_kernel, old_fine.shape),
        out_shape=edge_shapes(ITERS, species),
        in_specs=[SMEM] * 4 + [ANY] * 6,
        out_specs=[VMEM] * 4,
        scratch_shapes=late_scratch + [pltpu.VMEM(second.shape, f32), pltpu.SemaphoreType.DMA((5,))],
        compiler_params=PARAMS,
        cost_estimate=cost(4),
        name="edges",
    )(late, left, fine_at, coarse_at, second, rest, *edges)
    ylow, yhigh = neighbours("grp", ylow_own, yhigh_own)
    stepped = pl.pallas_call(
        functools.partial(late_step_kernel, old_fine.shape),
        out_shape=state_shape,
        in_specs=[SMEM] * 6 + [ANY] * 5,
        out_specs=ANY,
        scratch_shapes=[pltpu.VMEM(((planes + 2) * size, lanes), f32), pltpu.VMEM(((planes + 1) * size, lanes), f32)]
        + late_scratch
        + [pltpu.VMEM(second.shape, f32), pltpu.VMEM(velocity.shape, f32), pltpu.SemaphoreType.DMA((3,))]
        + [pltpu.SemaphoreType.DMA((planes,))],
        input_output_aliases={10: 0},
        compiler_params=PARAMS,
        cost_estimate=cost(7),
        name="late_step",
    )(late, left, fine_at, coarse_at, again, diffusion, second, rest, state, velocity, stepped)
    ylow, yhigh, stepped = lax.optimization_barrier((ylow, yhigh, stepped))
    message = jax.ShapeDtypeStruct((ITERS * size + 32, lanes), f32)
    down, up = pl.pallas_call(
        functools.partial(corners_kernel, planes, species),
        out_shape=[message] * 2,
        in_specs=[VMEM] * 4,
        out_specs=[VMEM] * 2,
        compiler_params=PARAMS,
        name="corners",
    )(ylow, yhigh, xlow_own, xhigh_own)
    xlow, xhigh = neighbours("dev", down, up)
    grp, dev = lax.axis_index("grp"), lax.axis_index("dev")
    inside = jnp.stack([grp > 0, grp < lax.axis_size("grp") - 1, dev > 0, dev < devices - 1]).astype(f32)
    row_edge = pltpu.VMEM((species * planes, lanes), f32)
    plane_edge = pltpu.VMEM((size, lanes), f32)
    done = pl.pallas_call(
        functools.partial(second_step_kernel, old_fine.shape),
        out_shape=state_shape,
        in_specs=[SMEM] * 2 + [ANY] * 2 + [VMEM] * 14,
        out_specs=ANY,
        scratch_shapes=[state_scratch] * 2
        + [row_edge] * 2
        + [plane_edge] * 2
        + [pltpu.VMEM(velocity.shape, f32), pltpu.SemaphoreType.DMA((2,)), group_sems],
        compiler_params=PARAMS,
        cost_estimate=cost(10),
        name="second_step",
    )(
        inside, diffusion, stepped, velocity, ylow_own, yhigh_own, xlow_own, xhigh_own, ylow, yhigh, xlow, xhigh,
        vylow, vyhigh, *flow_edges,
    )
    return done.reshape(old_fine.shape)


def solution(mesh):
    in_specs = (
        P("dev", None, "grp", None),
        P("grp", "dev"),
        P("dev", None, "grp", None),
        P("grp", "dev"),
        P("dev", None, "grp", None),
        P(),
    )
    out_specs = P("dev", None, "grp", None)
    return jax.shard_map(
        on_device, mesh=mesh, in_specs=in_specs, out_specs=out_specs, check_vma=False
    )
```
